32 devices in a mesh: row: 4 (over x, core), col: 8 (over z, y).
Axes of the slice: x: 2, y: 2, z: 4, core: 2. Of those that a mesh axis runs over, the one named last changes fastest.
Arguments:
- features: bfloat16 [8192, 256], P(('row', 'col')), may hold values from -6 to 6
- node_order: int32 [8192], P(('row', 'col')), may hold values from 0 to 8191, as said below
- tile_vals: bfloat16 [4, 8, 192, 128, 128], P('row', 'col'), may hold values from -0.109375 to 0.109375
- tile_coord: int32 [4, 8, 192], P('row', 'col'), may hold values from 0 to 127
- tile_count: int32 [4, 8], P('row', 'col'), may hold values from 12 to 192, as said below
- weight: bfloat16 [256, 256], replicated, may hold values from -0.375 to 0.375
- cotangent: bfloat16 [8192, 256], P(('row', 'col')), may hold values from -6 to 6
Outputs:
- activations: bfloat16 [8192, 256], P(('row', 'col'))
- weight_grad: float32 [256, 256], replicated
- feature_grad: bfloat16 [8192, 256], P(('row', 'col'))
The draws below stay inside these ranges and needn't reach their ends.
Inputs may be any that keep to these rules, and one draw needn't show every extreme that they name: `node_order`: each aligned block of 256 entries is a permutation of that block's own indices. `tile_count`: some device holds exactly 192 used slots.
All inputs are finite; a program needn't handle non-finite values.
Results may differ from the reference program's by a relative error of at most 0.015.
Values may be sent and summed in bfloat16 or wider, within the bound.
No kernel may reach another device: no remote copies, remote signals or barrier semaphores. Data moves between devices by JAX's collectives and lax.ppermute only.
A program may use at most 128 MiB of HBM per device.

```python
import jax
import jax.numpy as jnp
from jax import lax

WIDTH = 256
TILE = 128
NODE_DEV = 256
TILE_CAP = 192
NODES = 8192
BLOCK_ROWS = 16
BLOCK_COLS = 8
PIECE_BLOCKS = 2
N_ROW = 4
N_COL = 8


def draw_node_order(key, part):
    key = jax.random.fold_in(key, 11)
    piece_total = NODES // NODE_DEV
    subkeys = jax.random.split(key, piece_total)
    shuffled = jax.vmap(lambda subkey: jax.random.permutation(subkey, NODE_DEV))(subkeys)
    offsets = jnp.arange(piece_total, dtype=jnp.int32)[:, None] * NODE_DEV
    return (shuffled.astype(jnp.int32) + offsets).reshape(NODES)


def draw_tile_count(key, part):
    key = jax.random.fold_in(key, 23)
    key_one, key_two, key_three = jax.random.split(key, 3)
    first_draw = jax.random.randint(key_one, (N_ROW, N_COL), 1, TILE_CAP + 1)
    second_draw = jax.random.randint(key_two, (N_ROW, N_COL), 1, TILE_CAP + 1)
    counts = jnp.maximum(first_draw * second_draw // TILE_CAP, TILE_CAP // 16)
    busiest = jax.random.randint(key_three, (), 0, N_ROW * N_COL)
    flat_counts = counts.reshape(N_ROW * N_COL)
    flat_counts = jnp.where(jnp.arange(N_ROW * N_COL) == busiest, TILE_CAP, flat_counts)
    return flat_counts.reshape(N_ROW, N_COL).astype(jnp.int32)


def set_ends(result, rng, least, largest):
    spot = [jax.random.randint(jax.random.fold_in(rng, axis), (), 0, length) for axis, length in enumerate(result.shape)]
    main_axis = result.shape.index(max(result.shape))
    next_to = spot[:main_axis] + [(spot[main_axis] + 1) % result.shape[main_axis]] + spot[main_axis + 1:]
    return result.at[tuple(spot)].set(least).at[tuple(next_to)].set(largest)


def block_levels(stream_key, shape, shards, low, top_value):
    level = 1.0
    for axis_at, shards_of in shards:
        heights = jax.random.uniform(jax.random.fold_in(jax.random.fold_in(stream_key, 6), axis_at), (shards_of,), jnp.float32, low / len(shards), top_value / len(shards))
        level = level * jnp.repeat(jnp.exp(heights), shape[axis_at] // shards_of).reshape((-1,) + (1,) * (len(shape) - 1 - axis_at))
    return level


def normal_values(stream_key, extent, scale, limit, cuts=(), held_as=jnp.bfloat16):
    array = scale * jax.random.normal(stream_key, extent, jnp.float32)
    if cuts:
        array = array * block_levels(stream_key, extent, cuts, -0.22, 0.18)
    return jnp.clip(array, -limit, limit).astype(held_as)


def setup_inputs(seed: int = 0) -> dict:
    arg_keys = jax.random.split(jax.random.key(seed), 8)
    features = normal_values(arg_keys[0], (NODES, WIDTH), 1.0, 6.0, ((0, 32),))
    node_order = draw_node_order(jax.random.fold_in(arg_keys[7], 71), 0)
    tile_vals = normal_values(arg_keys[2], (N_ROW, N_COL, TILE_CAP, TILE, TILE), (max(1, TILE * TILE * TILE_CAP // (4 * NODE_DEV))) ** -0.5, 0.109375, ((0, 4), (1, 8)))
    tile_coord = set_ends(jax.random.randint(arg_keys[3], (N_ROW, N_COL, TILE_CAP), 0, BLOCK_ROWS * BLOCK_COLS), jax.random.fold_in(arg_keys[3], 1), 0, (BLOCK_ROWS * BLOCK_COLS) - 1).astype(jnp.int32)
    tile_count = draw_tile_count(jax.random.fold_in(arg_keys[7], 71), 0)
    weight = normal_values(arg_keys[5], (WIDTH, WIDTH), WIDTH ** -0.5, 0.375)
    cotangent = normal_values(arg_keys[6], (NODES, WIDTH), 1.0, 6.0, ((0, 32),))
    return {"features": features, "node_order": node_order, "tile_vals": tile_vals, "tile_coord": tile_coord, "tile_count": tile_count, "weight": weight, "cotangent": cotangent}


def elu_value(pre_act):
    return jnp.where(pre_act > 0, pre_act, jnp.expm1(jnp.minimum(pre_act, 0.0)))


def elu_slope(pre_act):
    return jnp.where(pre_act > 0, 1.0, jnp.exp(jnp.minimum(pre_act, 0.0)))


def spread(blocks_in, tile_vals, tile_coord, tile_count, forward):
    device_total = N_ROW * N_COL
    tiles_all = tile_vals.reshape(device_total, TILE_CAP, TILE, TILE)
    coord_all = tile_coord.reshape(device_total, TILE_CAP)
    count_all = tile_count.reshape(device_total)
    slots = jnp.arange(TILE_CAP, dtype=jnp.int32)
    row_range = jnp.arange(BLOCK_ROWS, dtype=jnp.int32)
    col_range = jnp.arange(BLOCK_COLS, dtype=jnp.int32)

    def global_col(local_col, col_id):
        return (((local_col // PIECE_BLOCKS) * N_COL + col_id) * PIECE_BLOCKS + local_col % PIECE_BLOCKS).astype(jnp.int32)

    def one_device(running, device):
        row_id = (device // N_COL).astype(jnp.int32)
        col_id = (device % N_COL).astype(jnp.int32)
        local_row = (coord_all[device] // BLOCK_COLS).astype(jnp.int32)
        local_col = (coord_all[device] % BLOCK_COLS).astype(jnp.int32)
        live_mask = (slots < count_all[device]).astype(jnp.float32)
        tiles_here = tiles_all[device].astype(jnp.float32) * live_mask[:, None, None]
        if forward:
            block_col = global_col(local_col, col_id)
            picked = blocks_in[block_col].astype(jnp.float32)
            products = jnp.einsum("tij,tjf->tif", tiles_here, picked)
            local = jnp.zeros((BLOCK_ROWS, TILE, WIDTH), jnp.float32).at[local_row].add(products)
            rounded = lax.optimization_barrier(local.astype(jnp.bfloat16)).astype(jnp.float32)
            target = (row_id * BLOCK_ROWS + row_range).astype(jnp.int32)
        else:
            block_row = (row_id * BLOCK_ROWS + local_row).astype(jnp.int32)
            picked = blocks_in[block_row].astype(jnp.float32)
            products = jnp.einsum("tji,tjf->tif", tiles_here, picked)
            local = jnp.zeros((BLOCK_COLS, TILE, WIDTH), jnp.float32).at[local_col].add(products)
            rounded = lax.optimization_barrier(local.astype(jnp.bfloat16)).astype(jnp.float32)
            target = global_col(col_range, col_id)
        running = running.at[target].add(rounded)
        return running, None

    block_total = NODES // TILE
    start = jnp.zeros((block_total, TILE, WIDTH), jnp.float32)
    summed, unused = lax.scan(one_device, start, jnp.arange(device_total, dtype=jnp.int32))
    return summed


def reference(features, node_order, tile_vals, tile_coord, tile_count, weight, cotangent):
    block_total = NODES // TILE
    placed = features[node_order]
    grads_in = cotangent[node_order]
    summed = spread(placed.reshape(block_total, TILE, WIDTH), tile_vals, tile_coord, tile_count, True)
    aggregate = summed.reshape(NODES, WIDTH).astype(jnp.bfloat16)
    pre_act = jnp.dot(aggregate, weight, preferred_element_type=jnp.float32)
    act_placed = elu_value(pre_act).astype(jnp.bfloat16)
    grad_pre = (grads_in.astype(jnp.float32) * elu_slope(pre_act)).astype(jnp.bfloat16)
    weight_grad = jnp.dot(aggregate.T, grad_pre, preferred_element_type=jnp.float32) * (NODES ** -0.5)
    grad_agg = jnp.dot(grad_pre, weight.T, preferred_element_type=jnp.float32).astype(jnp.bfloat16)
    summed_back = spread(grad_agg.reshape(block_total, TILE, WIDTH), tile_vals, tile_coord, tile_count, False)
    placed_grad = summed_back.reshape(NODES, WIDTH).astype(jnp.bfloat16)
    activations = jnp.zeros((NODES, WIDTH), jnp.bfloat16).at[node_order].set(act_placed)
    feature_grad = jnp.zeros((NODES, WIDTH), jnp.bfloat16).at[node_order].set(placed_grad)
    return activations, weight_grad, feature_grad
```

```python
import functools

import jax
import jax.numpy as jnp
from jax import lax
from jax.experimental import pallas as pl
from jax.experimental.pallas import tpu as pltpu
from jax.sharding import PartitionSpec as P

CORES = 2
GROUP = 4
PACK = 256
F32 = jnp.float32
BF16 = jnp.bfloat16


def elu_value(pre_act):
    return jnp.where(pre_act > 0, pre_act, jnp.expm1(jnp.minimum(pre_act, 0.0)))


def elu_slope(pre_act):
    return jnp.where(pre_act > 0, 1.0, jnp.exp(jnp.minimum(pre_act, 0.0)))


def permuter(node_order, nodes_here):
    local_pos = node_order % nodes_here
    return (local_pos[:, None] == jnp.arange(nodes_here, dtype=jnp.int32)[None, :]).astype(BF16)


def reorder(onehot, values):
    return jnp.dot(onehot, values, preferred_element_type=F32).astype(BF16)


def restore(onehot, values):
    moved = lax.dot_general(onehot, values, (((0,), (0,)), ((), ())), preferred_element_type=F32)
    return moved.astype(BF16)


def tile_lists(src_index, dst_index, tile_total, dst_blocks):
    slot_total = src_index.shape[0]
    slots = jnp.arange(slot_total, dtype=jnp.int32)
    dst = jnp.where(slots < tile_total, dst_index, dst_blocks)
    key = dst * slot_total + slots
    rank = jnp.sum((key[None, :] < key[:, None]).astype(jnp.int32), axis=1)
    packed = slots * PACK + src_index
    places = jnp.sum(jnp.where(rank[None, :] == slots[:, None], packed[None, :], 0), axis=1)
    marks = jnp.arange(dst_blocks + 1, dtype=jnp.int32)
    starts = jnp.sum((dst[None, :] < marks[:, None]).astype(jnp.int32), axis=1)
    return places, starts


def tile_kernel(transposed, place_ref, start_ref, where_ref, tiles_ref, *refs):
    *source_refs, out_ref, source = refs
    slot_total, tile_size, _ = tiles_ref.shape
    dst_blocks = start_ref.shape[0] - 1
    at = 0
    for ref in source_refs:
        source[at : at + ref.shape[0], :] = ref[...]
        at += ref.shape[0]
    source[at : at + tile_size, :] = jnp.zeros((tile_size, source.shape[1]), source.dtype)
    empty = at // tile_size

    def one_dst(dst, carry):
        first = start_ref[dst]
        last = start_ref[dst + 1]

        def one_group(group, total):
            left, right = [], []
            for member in range(GROUP):
                place = first + group * GROUP + member
                packed = place_ref[jnp.minimum(place, slot_total - 1)]
                slot = packed >> 8
                src = jnp.where(place < last, where_ref[packed & (PACK - 1)], empty)
                left.append(tiles_ref[slot])
                row = pl.multiple_of(src * tile_size, tile_size)
                right.append(source[pl.ds(row, tile_size), :])
            contract = 0 if transposed else 1
            return total + lax.dot_general(
                jnp.concatenate(left, axis=contract),
                jnp.concatenate(right, axis=0),
                (((contract,), (0,)), ((), ())),
                preferred_element_type=F32,
            )

        groups = (last - first + GROUP - 1) // GROUP
        total = lax.fori_loop(0, groups, one_group, jnp.zeros((tile_size, source.shape[1]), F32))
        place_out = where_ref[PACK + dst]
        row = pl.multiple_of(place_out * tile_size, tile_size)
        out_ref[pl.ds(row, tile_size), :] = total.astype(out_ref.dtype)
        return carry

    lax.fori_loop(0, dst_blocks, one_dst, 0)


def tile_sum(transposed, places, starts, src_where, dst_where, tiles, sources):
    slot_total, tile_size, _ = tiles.shape
    dst_blocks = starts.shape[0] - 1
    width = sources[0].shape[1]
    src_rows = sum(source.shape[0] for source in sources)
    where = jnp.concatenate(
        [src_where, jnp.zeros((PACK - src_where.shape[0],), jnp.int32), dst_where]
    )
    smem = pl.BlockSpec(memory_space=pltpu.SMEM)
    vmem = pl.BlockSpec(memory_space=pltpu.VMEM)
    return pl.pallas_call(
        functools.partial(tile_kernel, transposed),
        out_shape=jax.ShapeDtypeStruct((dst_blocks * tile_size, width), BF16),
        in_specs=[smem, smem, smem, vmem] + [vmem] * len(sources),
        out_specs=vmem,
        scratch_shapes=[pltpu.VMEM((src_rows + tile_size, width), BF16)],
        compiler_params=pltpu.CompilerParams(vmem_limit_bytes=40 * 1024 * 1024),
        cost_estimate=pl.CostEstimate(
            flops=2 * slot_total * tile_size * tile_size * width,
            bytes_accessed=2 * slot_total * tile_size * tile_size,
            transcendentals=0,
        ),
    )(places, starts, where, tiles, *sources)


def grid_cycle(size):
    ny = 1
    while (2 * ny) ** 2 <= size:
        ny *= 2
    nz = size // ny
    walk = [0]
    for z in range(nz):
        ys = range(1, ny) if z % 2 == 0 else range(ny - 1, 0, -1)
        walk += [z * ny + y for y in ys]
    walk += [z * ny for z in range(nz - 1, 0, -1)]
    return walk


def ring_perm(walks, step):
    return [
        (walk[k], walk[(k + step) % len(walk)]) for walk in walks for k in range(len(walk))
    ]


def ring_gather(own, axis, walks):
    size = len(walks[0])
    found = {0: own}
    ahead = behind = own
    for step in range(1, size // 2 + 1):
        behind = lax.ppermute(behind, axis, ring_perm(walks, 1))
        found[size - step] = behind
        if step <= (size - 1) // 2:
            ahead = lax.ppermute(ahead, axis, ring_perm(walks, -1))
            found[step] = ahead
    return [found[k] for k in range(size)]


def ring_scatter(chunks, axis, walks):
    size = len(walks[0])

    def travel(hops, sign):
        running = None
        for hop in range(hops, 0, -1):
            term = chunks[(sign * hop) % size]
            if running is not None:
                term = (running.astype(F32) + term.astype(F32)).astype(BF16)
            running = lax.ppermute(term, axis, ring_perm(walks, sign))
        return running

    total = chunks[0].astype(F32)
    for hops, sign in ((size // 2, 1), ((size - 1) // 2, -1)):
        if hops:
            total = total + travel(hops, sign).astype(F32)
    return total


def butterfly(size, bit):
    return [(k, k ^ bit) for k in range(size)]


def summed_everywhere(part, row_devices, col_devices):
    row = lax.axis_index("row")
    col = lax.axis_index("col")
    row_bits = [1 << k for k in range(row_devices.bit_length() - 1)]
    col_bits = [1 << k for k in range(col_devices.bit_length() - 1)]
    held = part.astype(BF16)
    for bit in row_bits:
        half = held.shape[0] // 2
        mine = (row // bit) % 2
        keep = lax.dynamic_slice_in_dim(held, mine * half, half, 0)
        give = lax.dynamic_slice_in_dim(held, (1 - mine) * half, half, 0)
        got = lax.ppermute(give, "row", butterfly(row_devices, bit))
        held = (keep.astype(F32) + got.astype(F32)).astype(BF16)
    for bit in col_bits:
        got = lax.ppermute(held, "col", butterfly(col_devices, bit))
        held = (held.astype(F32) + got.astype(F32)).astype(BF16)
    for bit in reversed(row_bits):
        got = lax.ppermute(held, "row", butterfly(row_devices, bit))
        mine = (row // bit) % 2
        held = jnp.where(
            mine == 0, jnp.concatenate([held, got]), jnp.concatenate([got, held])
        )
    return held.astype(F32)


def per_device(features, node_order, tile_vals, tile_coord, tile_count, weight, cotangent):
    nodes_here, feat_width = features.shape
    tile_size = tile_vals.shape[3]
    row_devices = lax.axis_size("row")
    col_devices = lax.axis_size("col")
    piece = nodes_here // tile_size
    block_cols = row_devices * piece
    block_rows = col_devices * piece
    grad_scale = float(nodes_here * row_devices * col_devices) ** (-0.5)
    row = lax.axis_index("row")
    col = lax.axis_index("col")
    chips = row_devices // CORES

    x_rings = [[x * CORES + core for x in range(chips)] for core in range(CORES)]
    core_rings = [[x * CORES + core for core in range(CORES)] for x in range(chips)]
    walk = grid_cycle(col_devices)
    place_of = [walk.index(c) for c in range(col_devices)]
    my_place = sum(jnp.where(col == c, place_of[c], 0) for c in range(col_devices))
    x, core = row // CORES, row % CORES

    row_where = jnp.stack(
        [
            ((((r % CORES) - core) % CORES) * chips + ((r // CORES) - x) % chips) * piece + part
            for r in range(row_devices)
            for part in range(piece)
        ]
    )
    col_where = jnp.stack(
        [
            ((place_of[c] - my_place) % col_devices) * piece + part
            for c in range(col_devices)
            for part in range(piece)
        ]
    )

    onehot = permuter(node_order, nodes_here)
    placed = reorder(onehot, features)
    grads_in = reorder(onehot, cotangent)
    tiles_here = tile_vals[0, 0]
    coord_here = tile_coord[0, 0]
    tile_total = tile_count[0, 0]
    row_of = coord_here // block_cols
    col_of = coord_here % block_cols
    places_out, starts_out = tile_lists(col_of, row_of, tile_total, block_rows)
    places_back, starts_back = tile_lists(row_of, col_of, tile_total, block_cols)

    along_x = ring_gather(placed, "row", x_rings)
    other_core = [lax.ppermute(block, "row", ring_perm(core_rings, 1)) for block in along_x]
    partial_low = tile_sum(
        False, places_out, starts_out, row_where, col_where, tiles_here, along_x + other_core
    )
    chunks = [
        partial_low[k * nodes_here : (k + 1) * nodes_here] for k in range(col_devices)
    ]
    own_rows = ring_scatter(chunks, "col", [walk]).astype(BF16)

    pre_act = jnp.dot(own_rows, weight, preferred_element_type=F32)
    own_act = elu_value(pre_act).astype(BF16)
    own_grad = (grads_in.astype(F32) * elu_slope(pre_act)).astype(BF16)
    own_agg_grad = lax.dot_general(
        own_grad, weight, (((1,), (1,)), ((), ())), preferred_element_type=F32
    ).astype(BF16)
    grad_blocks = ring_gather(own_agg_grad, "col", [walk])
    weight_part = (
        lax.dot_general(own_rows, own_grad, (((0,), (0,)), ((), ())), preferred_element_type=F32)
        * grad_scale
    )
    weight_grad = summed_everywhere(weight_part, row_devices, col_devices)

    column_low = tile_sum(
        True, places_back, starts_back, col_where, row_where, tiles_here, grad_blocks
    )
    half = chips * nodes_here
    from_core = lax.ppermute(column_low[half:], "row", ring_perm(core_rings, 1))
    both = (column_low[:half].astype(F32) + from_core.astype(F32)).astype(BF16)
    placed_grad = ring_scatter(
        [both[k * nodes_here : (k + 1) * nodes_here] for k in range(chips)], "row", x_rings
    ).astype(BF16)
    activations = restore(onehot, own_act)
    feature_grad = restore(onehot, placed_grad)
    return (activations, weight_grad, feature_grad)


def solution(mesh):
    in_specs = (
        P(("row", "col"), None),
        P(("row", "col")),
        P("row", "col", None, None, None),
        P("row", "col", None),
        P("row", "col"),
        P(),
        P(("row", "col"), None),
    )
    out_specs = (P(("row", "col"), None), P(), P(("row", "col"), None))
    return jax.shard_map(
        per_device, mesh=mesh, in_specs=in_specs, out_specs=out_specs, check_vma=False
    )
```

```python
import functools

import jax
import jax.numpy as jnp
from jax import lax
from jax.experimental import pallas as pl
from jax.experimental.pallas import tpu as pltpu
from jax.sharding import PartitionSpec as P

CORES = 2
GROUP = 4
PACK = 256
F32 = jnp.float32
BF16 = jnp.bfloat16


def elu_value(pre_act):
    return jnp.where(pre_act > 0, pre_act, jnp.expm1(jnp.minimum(pre_act, 0.0)))


def elu_slope(pre_act):
    return jnp.where(pre_act > 0, 1.0, jnp.exp(jnp.minimum(pre_act, 0.0)))


def permuter(node_order, nodes_here):
    local_pos = node_order % nodes_here
    return (local_pos[:, None] == jnp.arange(nodes_here, dtype=jnp.int32)[None, :]).astype(BF16)


def reorder(onehot, values):
    return jnp.dot(onehot, values, preferred_element_type=F32).astype(BF16)


def restore(onehot, values):
    moved = lax.dot_general(onehot, values, (((0,), (0,)), ((), ())), preferred_element_type=F32)
    return moved.astype(BF16)


def tile_lists(src_index, dst_index, tile_total, dst_blocks):
    slot_total = src_index.shape[0]
    slots = jnp.arange(slot_total, dtype=jnp.int32)
    dst = jnp.where(slots < tile_total, dst_index, dst_blocks)
    key = dst * slot_total + slots
    rank = jnp.sum((key[None, :] < key[:, None]).astype(jnp.int32), axis=1)
    packed = slots * PACK + src_index
    places = jnp.sum(jnp.where(rank[None, :] == slots[:, None], packed[None, :], 0), axis=1)
    marks = jnp.arange(dst_blocks + 1, dtype=jnp.int32)
    starts = jnp.sum((dst[None, :] < marks[:, None]).astype(jnp.int32), axis=1)
    return places, starts


def tile_kernel(transposed, place_ref, start_ref, where_ref, tiles_ref, *refs):
    *source_refs, out_ref, source = refs
    slot_total, tile_size, _ = tiles_ref.shape
    dst_blocks = start_ref.shape[0] - 1
    at = 0
    for ref in source_refs:
        source[at : at + ref.shape[0], :] = ref[...]
        at += ref.shape[0]
    source[at : at + tile_size, :] = jnp.zeros((tile_size, source.shape[1]), source.dtype)
    empty = at // tile_size

    def one_dst(dst, carry):
        first = start_ref[dst]
        last = start_ref[dst + 1]

        def one_group(group, total):
            left, right = [], []
            for member in range(GROUP):
                place = first + group * GROUP + member
                packed = place_ref[jnp.minimum(place, slot_total - 1)]
                slot = packed >> 8
                src = jnp.where(place < last, where_ref[packed & (PACK - 1)], empty)
                left.append(tiles_ref[slot])
                row = pl.multiple_of(src * tile_size, tile_size)
                right.append(source[pl.ds(row, tile_size), :])
            contract = 0 if transposed else 1
            return total + lax.dot_general(
                jnp.concatenate(left, axis=contract),
                jnp.concatenate(right, axis=0),
                (((contract,), (0,)), ((), ())),
                preferred_element_type=F32,
            )

        groups = (last - first + GROUP - 1) // GROUP
        total = lax.fori_loop(0, groups, one_group, jnp.zeros((tile_size, source.shape[1]), F32))
        place_out = where_ref[PACK + dst]
        row = pl.multiple_of(place_out * tile_size, tile_size)
        out_ref[pl.ds(row, tile_size), :] = total.astype(out_ref.dtype)
        return carry

    lax.fori_loop(0, dst_blocks, one_dst, 0)


def tile_sum(transposed, places, starts, src_where, dst_where, tiles, sources):
    slot_total, tile_size, _ = tiles.shape
    dst_blocks = starts.shape[0] - 1
    width = sources[0].shape[1]
    src_rows = sum(source.shape[0] for source in sources)
    where = jnp.concatenate(
        [src_where, jnp.zeros((PACK - src_where.shape[0],), jnp.int32), dst_where]
    )
    smem = pl.BlockSpec(memory_space=pltpu.SMEM)
    vmem = pl.BlockSpec(memory_space=pltpu.VMEM)
    return pl.pallas_call(
        functools.partial(tile_kernel, transposed),
        out_shape=jax.ShapeDtypeStruct((dst_blocks * tile_size, width), BF16),
        in_specs=[smem, smem, smem, vmem] + [vmem] * len(sources),
        out_specs=vmem,
        scratch_shapes=[pltpu.VMEM((src_rows + tile_size, width), BF16)],
        compiler_params=pltpu.CompilerParams(vmem_limit_bytes=40 * 1024 * 1024),
        cost_estimate=pl.CostEstimate(
            flops=2 * slot_total * tile_size * tile_size * width,
            bytes_accessed=2 * slot_total * tile_size * tile_size,
            transcendentals=0,
        ),
    )(places, starts, where, tiles, *sources)


def grid_cycle(size):
    ny = 1
    while (2 * ny) ** 2 <= size:
        ny *= 2
    nz = size // ny
    walk = [0]
    for z in range(nz):
        ys = range(1, ny) if z % 2 == 0 else range(ny - 1, 0, -1)
        walk += [z * ny + y for y in ys]
    walk += [z * ny for z in range(nz - 1, 0, -1)]
    return walk


def ring_perm(walks, step):
    return [
        (walk[k], walk[(k + step) % len(walk)]) for walk in walks for k in range(len(walk))
    ]


def ring_gather(own, axis, walks):
    size = len(walks[0])
    found = {0: own}
    ahead = behind = own
    for step in range(1, size // 2 + 1):
        behind = lax.ppermute(behind, axis, ring_perm(walks, 1))
        found[size - step] = behind
        if step <= (size - 1) // 2:
            ahead = lax.ppermute(ahead, axis, ring_perm(walks, -1))
            found[step] = ahead
    return [found[k] for k in range(size)]


def ring_scatter(chunks, axis, walks):
    size = len(walks[0])

    def travel(hops, sign):
        running = None
        for hop in range(hops, 0, -1):
            term = chunks[(sign * hop) % size]
            if running is not None:
                term = (running.astype(F32) + term.astype(F32)).astype(BF16)
            running = lax.ppermute(term, axis, ring_perm(walks, sign))
        return running

    total = chunks[0].astype(F32)
    for hops, sign in ((size // 2, 1), ((size - 1) // 2, -1)):
        if hops:
            total = total + travel(hops, sign).astype(F32)
    return total


def summed_everywhere(part):
    own = lax.psum_scatter(part.astype(BF16), "col", scatter_dimension=0, tiled=True)
    own = lax.psum(own, "row")
    return lax.all_gather(own, "col", axis=0, tiled=True).astype(F32)


def per_device(features, node_order, tile_vals, tile_coord, tile_count, weight, cotangent):
    nodes_here, feat_width = features.shape
    tile_size = tile_vals.shape[3]
    row_devices = lax.axis_size("row")
    col_devices = lax.axis_size("col")
    piece = nodes_here // tile_size
    block_cols = row_devices * piece
    block_rows = col_devices * piece
    grad_scale = float(nodes_here * row_devices * col_devices) ** (-0.5)
    row = lax.axis_index("row")
    col = lax.axis_index("col")
    chips = row_devices // CORES

    x_rings = [[x * CORES + core for x in range(chips)] for core in range(CORES)]
    core_rings = [[x * CORES + core for core in range(CORES)] for x in range(chips)]
    walk = grid_cycle(col_devices)
    place_of = [walk.index(c) for c in range(col_devices)]
    my_place = sum(jnp.where(col == c, place_of[c], 0) for c in range(col_devices))
    x, core = row // CORES, row % CORES

    row_where = jnp.stack(
        [
            ((((r % CORES) - core) % CORES) * chips + ((r // CORES) - x) % chips) * piece + part
            for r in range(row_devices)
            for part in range(piece)
        ]
    )
    col_where = jnp.stack(
        [
            ((place_of[c] - my_place) % col_devices) * piece + part
            for c in range(col_devices)
            for part in range(piece)
        ]
    )

    split_where = jnp.array(
        [part * col_devices + c for c in range(col_devices) for part in range(piece)], jnp.int32
    )

    onehot = permuter(node_order, nodes_here)
    placed = reorder(onehot, features)
    grads_in = reorder(onehot, cotangent)
    tiles_here = tile_vals[0, 0]
    coord_here = tile_coord[0, 0]
    tile_total = tile_count[0, 0]
    row_of = coord_here // block_cols
    col_of = coord_here % block_cols
    places_out, starts_out = tile_lists(col_of, row_of, tile_total, block_rows)
    places_back, starts_back = tile_lists(row_of, col_of, tile_total, block_cols)

    column_group = lax.all_gather(placed, "row", axis=0, tiled=True)
    partial_low = tile_sum(
        False,
        places_out,
        starts_out,
        jnp.arange(block_cols, dtype=jnp.int32),
        col_where,
        tiles_here,
        [column_group],
    )
    chunks = [
        partial_low[k * nodes_here : (k + 1) * nodes_here] for k in range(col_devices)
    ]
    own_rows = ring_scatter(chunks, "col", [walk]).astype(BF16)

    pre_act = jnp.dot(own_rows, weight, preferred_element_type=F32)
    own_act = elu_value(pre_act).astype(BF16)
    own_grad = (grads_in.astype(F32) * elu_slope(pre_act)).astype(BF16)
    own_agg_grad = lax.dot_general(
        own_grad, weight, (((1,), (1,)), ((), ())), preferred_element_type=F32
    ).astype(BF16)
    grad_blocks = []
    for part in range(piece):
        sent = own_agg_grad[part * tile_size : (part + 1) * tile_size]
        if grad_blocks:
            sent, grad_blocks[-1] = lax.optimization_barrier((sent, grad_blocks[-1]))
        grad_blocks.append(lax.all_gather(sent, "col", axis=0, tiled=True))
    weight_part = (
        lax.dot_general(own_rows, own_grad, (((0,), (0,)), ((), ())), preferred_element_type=F32)
        * grad_scale
    )
    weight_grad = summed_everywhere(weight_part)

    column_low = tile_sum(
        True, places_back, starts_back, split_where, row_where, tiles_here, grad_blocks
    )
    half = chips * nodes_here
    from_core = lax.ppermute(column_low[half:], "row", ring_perm(core_rings, 1))
    both = (column_low[:half].astype(F32) + from_core.astype(F32)).astype(BF16)
    placed_grad = ring_scatter(
        [both[k * nodes_here : (k + 1) * nodes_here] for k in range(chips)], "row", x_rings
    ).astype(BF16)
    activations = restore(onehot, own_act)
    feature_grad = restore(onehot, placed_grad)
    return (activations, weight_grad, feature_grad)


def solution(mesh):
    in_specs = (
        P(("row", "col"), None),
        P(("row", "col")),
        P("row", "col", None, None, None),
        P("row", "col", None),
        P("row", "col"),
        P(),
        P(("row", "col"), None),
    )
    out_specs = (P(("row", "col"), None), P(), P(("row", "col"), None))
    return jax.shard_map(
        per_device, mesh=mesh, in_specs=in_specs, out_specs=out_specs, check_vma=False
    )
```

```python
import functools

import jax
import jax.numpy as jnp
from jax import lax
from jax.experimental import pallas as pl
from jax.experimental.pallas import tpu as pltpu
from jax.sharding import PartitionSpec as P

CORES = 2
GROUP = 4
UNROLL = 2
LOADS = 4
PACK_BITS = 8
PACK = 1 << PACK_BITS
VMEM_BYTES = 40 * 1024 * 1024
F32 = jnp.float32
BF16 = jnp.bfloat16


def elu_value(pre_act):
    return jnp.where(pre_act > 0, pre_act, jnp.expm1(jnp.minimum(pre_act, 0.0)))


def elu_slope(pre_act):
    return jnp.where(pre_act > 0, 1.0, jnp.exp(jnp.minimum(pre_act, 0.0)))


def permuter(node_order, nodes_here):
    local_pos = node_order % nodes_here
    return (local_pos[:, None] == jnp.arange(nodes_here, dtype=jnp.int32)[None, :]).astype(BF16)


def reorder(onehot, values):
    return jnp.dot(onehot, values, preferred_element_type=F32).astype(BF16)


def restore(onehot, values):
    moved = lax.dot_general(onehot, values, (((0,), (0,)), ((), ())), preferred_element_type=F32)
    return moved.astype(BF16)


def tile_table(bins, bin_total, sources, tile_total):
    slot_total = bins.shape[0]
    group_total = slot_total // GROUP + bin_total + 1
    slots = jnp.arange(slot_total, dtype=jnp.int32)
    marks = jnp.arange(bin_total, dtype=jnp.int32)
    live = slots < tile_total
    held = jnp.where(live, bins, bin_total)
    same = held[:, None] == held[None, :]
    before = jnp.sum((same & (slots[None, :] < slots[:, None])).astype(jnp.int32), axis=1)
    counts = jnp.sum((held[None, :] == marks[:, None]).astype(jnp.int32), axis=1)
    groups = (counts + GROUP - 1) // GROUP
    edges = jnp.arange(bin_total + 1, dtype=jnp.int32)
    firsts = jnp.sum(jnp.where(marks[None, :] < edges[:, None], groups[None, :], 0), axis=1)
    mine = jnp.sum(jnp.where(marks[None, :] < held[:, None], groups[None, :], 0), axis=1)
    place = jnp.where(live, mine * GROUP + before, -1)
    places = jnp.arange(group_total * GROUP, dtype=jnp.int32)
    empty = slot_total * PACK
    member = (slots * PACK + sources - empty)[None, :]
    members = empty + jnp.sum(jnp.where(place[None, :] == places[:, None], member, 0), axis=1)
    numbers = jnp.arange(group_total, dtype=jnp.int32)
    group_bin = jnp.sum((firsts[None, 1:] <= numbers[:, None]).astype(jnp.int32), axis=1)
    return jnp.concatenate([members, group_bin, firsts])


def load_kernel(tiles_ref, out_ref, sems):
    slot_total = tiles_ref.shape[0]
    share = slot_total // LOADS
    copies = [
        pltpu.make_async_copy(
            tiles_ref.at[pl.ds(k * share, share)], out_ref.at[pl.ds(k * share, share)], sems.at[k]
        )
        for k in range(LOADS)
    ]
    for copy in copies:
        copy.start()
    out_ref[slot_total] = jnp.zeros(out_ref.shape[1:], out_ref.dtype)
    for copy in copies:
        copy.wait()


def load_tiles(tiles):
    slot_total, tile_size, _ = tiles.shape
    nbytes = 2 * slot_total * tile_size * tile_size
    return pl.pallas_call(
        load_kernel,
        out_shape=jax.ShapeDtypeStruct((slot_total + 1, tile_size, tile_size), BF16),
        in_specs=[pl.BlockSpec(memory_space=pl.ANY)],
        out_specs=pl.BlockSpec(memory_space=pltpu.VMEM),
        scratch_shapes=[pltpu.SemaphoreType.DMA((LOADS,))],
        compiler_params=pltpu.CompilerParams(vmem_limit_bytes=VMEM_BYTES),
        cost_estimate=pl.CostEstimate(flops=0, bytes_accessed=nbytes, transcendentals=0),
    )(tiles)


def part_kernel(spec, table_ref, tiles_ref, *refs):
    transposed, first_bin, bin_count, bin_total, source_count, carried, finish = spec
    source_refs = refs[:source_count]
    acc_ref = refs[source_count] if carried is not None else None
    out_refs = refs[source_count + (carried is not None) : -2]
    source, total = refs[-2:]
    slot_total = tiles_ref.shape[0] - 1
    tile_size = tiles_ref.shape[1]
    group_total = slot_total // GROUP + bin_total + 1
    at = 0
    for ref in source_refs:
        source[at : at + ref.shape[0], :] = ref[...]
        at += ref.shape[0]
    if carried is None:
        total[...] = jnp.zeros_like(total)
    else:
        total[...] = acc_ref[carried * tile_size : carried * tile_size + total.shape[0], :]
    bins_at = group_total * GROUP
    firsts_at = bins_at + group_total
    begin = table_ref[firsts_at + first_bin]
    end = table_ref[firsts_at + first_bin + bin_count]
    contract = 0 if transposed else 1

    def step(number, carry):
        products = []
        for member in range(UNROLL):
            group = begin + number * UNROLL + member
            group = jnp.where(group < end, group, group_total - 1)
            left, right = [], []
            for k in range(GROUP):
                packed = table_ref[group * GROUP + k]
                left.append(tiles_ref[packed >> PACK_BITS])
                row = pl.multiple_of((packed & (PACK - 1)) * tile_size, tile_size)
                right.append(source[pl.ds(row, tile_size), :])
            product = lax.dot_general(
                jnp.concatenate(left, axis=contract),
                jnp.concatenate(right, axis=0),
                (((contract,), (0,)), ((), ())),
                preferred_element_type=F32,
            )
            products.append((jnp.minimum(table_ref[bins_at + group] - first_bin, bin_count - 1), product))
        for place, product in products:
            rows = pl.ds(pl.multiple_of(place * tile_size, tile_size), tile_size)
            total[rows, :] += product
        return carry

    lax.fori_loop(0, (end - begin + UNROLL - 1) // UNROLL, step, 0)
    if finish:
        at = 0
        for ref in out_refs:
            ref[...] = total[at : at + ref.shape[0], :].astype(ref.dtype)
            at += ref.shape[0]
    else:
        out_refs[0][...] = total[...]


def tile_part(transposed, table, bins, bin_total, tiles, sources, acc=None, acc_at=0, pieces=None):
    first_bin, bin_count = bins
    slot_total, tile_size = tiles.shape[0] - 1, tiles.shape[1]
    width = sources[0].shape[1]
    rows = bin_count * tile_size
    vmem = pl.BlockSpec(memory_space=pltpu.VMEM)
    if pieces is None:
        out_shape = [jax.ShapeDtypeStruct((rows, width), F32)]
    else:
        out_shape = [jax.ShapeDtypeStruct((pieces, width), BF16)] * (rows // pieces)
    carried = None if acc is None else acc_at
    share = slot_total * bin_count // bin_total
    given = [table, tiles, *sources] + ([] if acc is None else [acc])
    spec = (transposed, first_bin, bin_count, bin_total, len(sources), carried, pieces is not None)
    return pl.pallas_call(
        functools.partial(part_kernel, spec),
        out_shape=out_shape,
        in_specs=[pl.BlockSpec(memory_space=pltpu.SMEM)] + [vmem] * (len(given) - 1),
        out_specs=[vmem] * len(out_shape),
        scratch_shapes=[
            pltpu.VMEM((sum(source.shape[0] for source in sources), width), BF16),
            pltpu.VMEM((rows, width), F32),
        ],
        compiler_params=pltpu.CompilerParams(vmem_limit_bytes=VMEM_BYTES),
        cost_estimate=pl.CostEstimate(
            flops=2 * share * tile_size * tile_size * width,
            bytes_accessed=2 * share * tile_size * tile_size,
            transcendentals=0,
        ),
    )(*given)


def grid_cycle(size):
    ny = 1
    while (2 * ny) ** 2 <= size:
        ny *= 2
    nz = size // ny
    walk = [0]
    for z in range(nz):
        ys = range(1, ny) if z % 2 == 0 else range(ny - 1, 0, -1)
        walk += [z * ny + y for y in ys]
    walk += [z * ny for z in range(nz - 1, 0, -1)]
    return walk


class Grid:
    def __init__(self, rows, cols):
        self.rows, self.cols, self.chips = rows, cols, rows // CORES
        self.walk = grid_cycle(cols)
        self.place_of = [self.walk.index(c) for c in range(cols)]
        self.row, self.col = lax.axis_index("row"), lax.axis_index("col")
        self.x, self.core = self.row // CORES, self.row % CORES
        place = sum(jnp.where(self.col == c, self.place_of[c], 0) for c in range(cols))
        self.ahead_of = [
            jnp.where(self.core == 0, self.place_of[c] - place, place - self.place_of[c]) % cols
            for c in range(cols)
        ]

    def along_walk(self, step):
        pairs = []
        for r in range(self.rows):
            walk = self.walk if r % CORES == 0 else self.walk[::-1]
            for k in range(self.cols):
                pairs.append((r * self.cols + walk[k], r * self.cols + walk[(k + step) % self.cols]))
        return pairs

    def along_x(self, step):
        return [
            (r * self.cols + c, ((r + step * CORES) % self.rows) * self.cols + c)
            for r in range(self.rows)
            for c in range(self.cols)
        ]

    def across(self, row_bit, col_bit):
        return [
            (r * self.cols + c, (r ^ row_bit) * self.cols + (c ^ col_bit))
            for r in range(self.rows)
            for c in range(self.cols)
        ]


def move(value, pairs):
    return lax.ppermute(value, ("row", "col"), pairs)


def ring_gather(own, size, pairs_of):
    found = {0: own}
    ahead = behind = own
    for step in range(1, size // 2 + 1):
        behind = move(behind, pairs_of(1))
        found[size - step] = behind
        if step <= (size - 1) // 2:
            ahead = move(ahead, pairs_of(-1))
            found[step] = ahead
    return [found[k] for k in range(size)]


def ring_scatter(chunks, size, pairs_of):
    def travel(hops, sign):
        running = None
        for hop in range(hops, 0, -1):
            term = chunks[(sign * hop) % size]
            if running is not None:
                term = (running.astype(F32) + term.astype(F32)).astype(BF16)
            running = move(term, pairs_of(sign))
        return running

    total = chunks[0].astype(F32)
    for hops, sign in ((size // 2, 1), ((size - 1) // 2, -1)):
        if hops:
            total = total + travel(hops, sign).astype(F32)
    return total


def summed_everywhere(part, grid):
    row_bits = [1 << k for k in range(grid.rows.bit_length() - 1)]
    col_bits = [1 << k for k in range(grid.cols.bit_length() - 1)]
    held = part.astype(BF16)
    for bit in row_bits:
        half = held.shape[0] // 2
        mine = (grid.row // bit) % 2
        keep = lax.dynamic_slice_in_dim(held, mine * half, half, 0)
        give = lax.dynamic_slice_in_dim(held, (1 - mine) * half, half, 0)
        got = move(give, grid.across(bit, 0))
        held = (keep.astype(F32) + got.astype(F32)).astype(BF16)
    for bit in col_bits:
        got = move(held, grid.across(0, bit))
        held = (held.astype(F32) + got.astype(F32)).astype(BF16)
    for bit in reversed(row_bits):
        got = move(held, grid.across(bit, 0))
        mine = (grid.row // bit) % 2
        held = jnp.where(mine == 0, jnp.concatenate([held, got]), jnp.concatenate([got, held]))
    return held.astype(F32)


def scatter_order(size):
    groups = []
    for step in range(size // 2):
        group = [size // 2 - step]
        back = (size - 1) // 2 - step
        if back > 0:
            group.append(size - back)
        groups.append(group)
    groups[-1].append(0)
    return groups


def ahead_bins(ahead, size):
    order = [k for group in scatter_order(size) for k in group]
    return sum(jnp.where(ahead == k, place, 0) for place, k in enumerate(order))


def arrival_order(size):
    groups = []
    for step in range(1, size // 2 + 1):
        groups.append([size - step] + ([step] if step <= (size - 1) // 2 else []))
    groups[0].append(0)
    return groups


def per_device(features, node_order, tile_vals, tile_coord, tile_count, weight, cotangent):
    nodes_here, feat_width = features.shape
    tile_size = tile_vals.shape[3]
    row_devices = lax.axis_size("row")
    col_devices = lax.axis_size("col")
    piece = nodes_here // tile_size
    block_cols = row_devices * piece
    block_rows = col_devices * piece
    grad_scale = float(nodes_here * row_devices * col_devices) ** (-0.5)
    grid = Grid(row_devices, col_devices)
    chips = grid.chips

    onehot = permuter(node_order, nodes_here)
    placed = reorder(onehot, features)
    tiles = load_tiles(tile_vals[0, 0])
    coord_here = tile_coord[0, 0]
    tile_total = tile_count[0, 0]
    row_of = coord_here // block_cols
    col_of = coord_here % block_cols

    row_dev = col_of // piece
    far = (row_dev // CORES - grid.x) % chips
    swap = (row_dev % CORES - grid.core) % CORES
    col_dev = row_of // piece
    ahead = sum(jnp.where(col_dev == c, grid.ahead_of[c], 0) for c in range(col_devices))
    source_out = (swap * chips + far) * piece + col_of % piece
    table_out = tile_table(ahead_bins(ahead, col_devices) * piece + row_of % piece, block_rows, source_out, tile_total)

    along_x = ring_gather(placed, chips, grid.along_x)
    other_core = [move(block, grid.across(1, 0)) for block in along_x]
    grads_in = reorder(onehot, cotangent)
    chunks = {}
    at = 0
    for group in scatter_order(col_devices):
        made = tile_part(
            False, table_out, (at, len(group) * piece), block_rows, tiles, along_x + other_core, pieces=nodes_here
        )
        chunks.update(zip(group, made))
        at += len(group) * piece
    own_rows = ring_scatter(chunks, col_devices, grid.along_walk).astype(BF16)

    pre_act = jnp.dot(own_rows, weight, preferred_element_type=F32)
    own_act = elu_value(pre_act).astype(BF16)
    own_grad = (grads_in.astype(F32) * elu_slope(pre_act)).astype(BF16)
    own_agg_grad = lax.dot_general(
        own_grad, weight, (((1,), (1,)), ((), ())), preferred_element_type=F32
    ).astype(BF16)
    grad_blocks = ring_gather(own_agg_grad, col_devices, grid.along_walk)
    weight_part = (
        lax.dot_general(own_rows, own_grad, (((0,), (0,)), ((), ())), preferred_element_type=F32)
        * grad_scale
    )
    weight_grad = summed_everywhere(weight_part, grid)

    arrivals = arrival_order(col_devices)
    part_of = sum(jnp.where(ahead == k, p, 0) for p, group in enumerate(arrivals) for k in group)
    block_at = sum(jnp.where(ahead == k, i, 0) for group in arrivals for i, k in enumerate(group))
    place_back = ((far - 1) % chips * CORES + swap) * piece + col_of % piece
    bins_back = len(arrivals) * block_cols
    table_back = tile_table(
        part_of * block_cols + place_back, bins_back, block_at * piece + row_of % piece, tile_total
    )
    acc = None
    for number, group in enumerate(arrivals[:-1]):
        (acc,) = tile_part(
            True,
            table_back,
            (number * block_cols, block_cols),
            bins_back,
            tiles,
            [grad_blocks[k] for k in group],
            acc=acc,
        )
    last = [grad_blocks[k] for k in arrivals[-1]]
    last_bin = (len(arrivals) - 1) * block_cols
    near_bins = CORES * piece
    far_bins = block_cols - near_bins
    far_chunks = tile_part(
        True, table_back, (last_bin, far_bins), bins_back, tiles, last, acc=acc, pieces=nodes_here
    )
    near_chunks = tile_part(
        True,
        table_back,
        (last_bin + far_bins, near_bins),
        bins_back,
        tiles,
        last,
        acc=acc,
        acc_at=far_bins,
        pieces=nodes_here,
    )
    sums = {}
    for distance in range(1, chips):
        mine, theirs = far_chunks[CORES * (distance - 1) : CORES * distance]
        got = move(theirs, grid.across(1, 0))
        sums[distance] = (mine.astype(F32) + got.astype(F32)).astype(BF16)
    got = move(near_chunks[1], grid.across(1, 0))
    sums[0] = near_chunks[0].astype(F32) + got.astype(F32)
    placed_grad = ring_scatter(sums, chips, grid.along_x).astype(BF16)
    activations = restore(onehot, own_act)
    feature_grad = restore(onehot, placed_grad)
    return (activations, weight_grad, feature_grad)


def solution(mesh):
    in_specs = (
        P(("row", "col"), None),
        P(("row", "col")),
        P("row", "col", None, None, None),
        P("row", "col", None),
        P("row", "col"),
        P(),
        P(("row", "col"), None),
    )
    out_specs = (P(("row", "col"), None), P(), P(("row", "col"), None))
    return jax.shard_map(
        per_device, mesh=mesh, in_specs=in_specs, out_specs=out_specs, check_vma=False
    )
```

```python
import functools

import jax
import jax.numpy as jnp
from jax import lax
from jax.experimental import pallas as pl
from jax.experimental.pallas import tpu as pltpu
from jax.sharding import PartitionSpec as P

CORES = 2
GROUP = 4
UNROLL = 2
PACK_BITS = 8
PACK = 1 << PACK_BITS
VMEM_BYTES = 16 * 1024 * 1024
LOAD_BYTES = 45 * 1024 * 1024
LOADS = 4
F32 = jnp.float32
BF16 = jnp.bfloat16


def elu_value(pre_act):
    return jnp.where(pre_act > 0, pre_act, jnp.expm1(jnp.minimum(pre_act, 0.0)))


def elu_slope(pre_act):
    return jnp.where(pre_act > 0, 1.0, jnp.exp(jnp.minimum(pre_act, 0.0)))


def permuter(node_order, nodes_here):
    local_pos = node_order % nodes_here
    return (local_pos[:, None] == jnp.arange(nodes_here, dtype=jnp.int32)[None, :]).astype(BF16)


def reorder(onehot, values):
    return jnp.dot(onehot, values, preferred_element_type=F32).astype(BF16)


def restore(onehot, values):
    moved = lax.dot_general(onehot, values, (((0,), (0,)), ((), ())), preferred_element_type=F32)
    return moved.astype(BF16)


def tile_table(bins, bin_total, sources, tile_total, empty):
    slot_total = bins.shape[0]
    group_total = slot_total // GROUP + bin_total + 1
    slots = jnp.arange(slot_total, dtype=jnp.int32)
    marks = jnp.arange(bin_total, dtype=jnp.int32)
    live = slots < tile_total
    held = jnp.where(live, bins, bin_total)
    same = held[:, None] == held[None, :]
    before = jnp.sum((same & (slots[None, :] < slots[:, None])).astype(jnp.int32), axis=1)
    counts = jnp.sum((held[None, :] == marks[:, None]).astype(jnp.int32), axis=1)
    groups = (counts + GROUP - 1) // GROUP
    edges = jnp.arange(bin_total + 1, dtype=jnp.int32)
    firsts = jnp.sum(jnp.where(marks[None, :] < edges[:, None], groups[None, :], 0), axis=1)
    mine = jnp.sum(jnp.where(marks[None, :] < held[:, None], groups[None, :], 0), axis=1)
    place = jnp.where(live, mine * GROUP + before, -1)
    places = jnp.arange(group_total * GROUP, dtype=jnp.int32)
    member = (slots * PACK + sources - empty)[None, :]
    members = empty + jnp.sum(jnp.where(place[None, :] == places[:, None], member, 0), axis=1)
    numbers = jnp.arange(group_total, dtype=jnp.int32)
    group_bin = jnp.sum((firsts[None, 1:] <= numbers[:, None]).astype(jnp.int32), axis=1)
    return jnp.concatenate([members, group_bin, firsts])


def load_kernel(tiles_ref, out_ref, sems):
    share = tiles_ref.shape[0] // LOADS
    copies = [
        pltpu.make_async_copy(
            tiles_ref.at[pl.ds(k * share, share)], out_ref.at[pl.ds(k * share, share)], sems.at[k]
        )
        for k in range(LOADS)
    ]
    for copy in copies:
        copy.start()
    for copy in copies:
        copy.wait()


def load_tiles(tiles):
    return pl.pallas_call(
        load_kernel,
        out_shape=jax.ShapeDtypeStruct(tiles.shape, tiles.dtype),
        in_specs=[pl.BlockSpec(memory_space=pl.ANY)],
        out_specs=pl.BlockSpec(memory_space=pltpu.VMEM),
        scratch_shapes=[pltpu.SemaphoreType.DMA((LOADS,))],
        compiler_params=pltpu.CompilerParams(vmem_limit_bytes=LOAD_BYTES),
        cost_estimate=pl.CostEstimate(flops=0, bytes_accessed=2 * tiles.size, transcendentals=0),
    )(tiles)


def part_kernel(spec, table_ref, tiles_ref, *refs):
    transposed, first_bin, bin_count, bin_total, source_count, carried, finish = spec
    source_refs = refs[:source_count]
    out_refs = refs[source_count + carried : -2]
    source, total = refs[-2:]
    slot_total, tile_size, _ = tiles_ref.shape
    group_total = slot_total // GROUP + bin_total + 1
    at = 0
    for ref in source_refs:
        source[at : at + ref.shape[0], :] = ref[...]
        at += ref.shape[0]
    source[at:, :] = jnp.zeros((source.shape[0] - at, source.shape[1]), source.dtype)
    total[...] = refs[source_count][...] if carried else jnp.zeros_like(total)
    bins_at = group_total * GROUP
    firsts_at = bins_at + group_total
    begin = table_ref[firsts_at + first_bin]
    end = table_ref[firsts_at + first_bin + bin_count]
    contract = 0 if transposed else 1

    def step(number, carry):
        products = []
        for member in range(UNROLL):
            group = begin + number * UNROLL + member
            group = jnp.where(group < end, group, group_total - 1)
            left, right = [], []
            for k in range(GROUP):
                packed = table_ref[group * GROUP + k]
                left.append(tiles_ref[packed >> PACK_BITS])
                row = pl.multiple_of((packed & (PACK - 1)) * tile_size, tile_size)
                right.append(source[pl.ds(row, tile_size), :])
            product = lax.dot_general(
                jnp.concatenate(left, axis=contract),
                jnp.concatenate(right, axis=0),
                (((contract,), (0,)), ((), ())),
                preferred_element_type=F32,
            )
            products.append((jnp.minimum(table_ref[bins_at + group] - first_bin, bin_count - 1), product))
        for place, product in products:
            rows = pl.ds(pl.multiple_of(place * tile_size, tile_size), tile_size)
            total[rows, :] += product
        return carry

    lax.fori_loop(0, (end - begin + UNROLL - 1) // UNROLL, step, 0)
    if finish:
        at = 0
        for ref in out_refs:
            ref[...] = total[at : at + ref.shape[0], :].astype(ref.dtype)
            at += ref.shape[0]
    else:
        out_refs[0][...] = total[...]


def tile_part(transposed, table, bins, bin_total, tiles, sources, empty, acc=None, pieces=None):
    first_bin, bin_count = bins
    slot_total, tile_size, _ = tiles.shape
    width = sources[0].shape[1]
    rows = bin_count * tile_size
    vmem = pl.BlockSpec(memory_space=pltpu.VMEM)
    if pieces is None:
        out_shape = [jax.ShapeDtypeStruct((rows, width), F32)]
    else:
        out_shape = [jax.ShapeDtypeStruct((pieces, width), BF16)] * (rows // pieces)
    carried = acc is not None
    share = slot_total * bin_count // bin_total
    given = [table, tiles, *sources] + ([] if acc is None else [acc])
    spec = (transposed, first_bin, bin_count, bin_total, len(sources), carried, pieces is not None)
    return pl.pallas_call(
        functools.partial(part_kernel, spec),
        out_shape=out_shape,
        in_specs=[pl.BlockSpec(memory_space=pltpu.SMEM)] + [vmem] * (len(given) - 1),
        out_specs=[vmem] * len(out_shape),
        scratch_shapes=[
            pltpu.VMEM(((empty + 1) * tile_size, width), BF16),
            pltpu.VMEM((rows, width), F32),
        ],
        compiler_params=pltpu.CompilerParams(vmem_limit_bytes=VMEM_BYTES),
        cost_estimate=pl.CostEstimate(
            flops=2 * share * tile_size * tile_size * width,
            bytes_accessed=2 * share * tile_size * tile_size,
            transcendentals=0,
        ),
    )(*given)


def grid_cycle(size):
    ny = 1
    while (2 * ny) ** 2 <= size:
        ny *= 2
    nz = size // ny
    walk = [0]
    for z in range(nz):
        ys = range(1, ny) if z % 2 == 0 else range(ny - 1, 0, -1)
        walk += [z * ny + y for y in ys]
    walk += [z * ny for z in range(nz - 1, 0, -1)]
    return walk


class Grid:
    def __init__(self, rows, cols):
        self.rows, self.cols, self.chips = rows, cols, rows // CORES
        self.walk = grid_cycle(cols)
        self.place_of = [self.walk.index(c) for c in range(cols)]
        self.row, self.col = lax.axis_index("row"), lax.axis_index("col")
        self.x, self.core = self.row // CORES, self.row % CORES
        place = sum(jnp.where(self.col == c, self.place_of[c], 0) for c in range(cols))
        self.ahead_of = [
            jnp.where(self.core == 0, self.place_of[c] - place, place - self.place_of[c]) % cols
            for c in range(cols)
        ]

    def along_walk(self, step):
        pairs = []
        for r in range(self.rows):
            walk = self.walk if r % CORES == 0 else self.walk[::-1]
            for k in range(self.cols):
                pairs.append((r * self.cols + walk[k], r * self.cols + walk[(k + step) % self.cols]))
        return pairs

    def along_x(self, step):
        return [
            (r * self.cols + c, ((r + step * CORES) % self.rows) * self.cols + c)
            for r in range(self.rows)
            for c in range(self.cols)
        ]

    def across(self, row_bit, col_bit):
        return [
            (r * self.cols + c, (r ^ row_bit) * self.cols + (c ^ col_bit))
            for r in range(self.rows)
            for c in range(self.cols)
        ]


def move(value, pairs):
    return lax.ppermute(value, ("row", "col"), pairs)


def after(value, *others):
    return lax.optimization_barrier((value, *others))[0]


def ring_gather(own, size, pairs_of):
    yield {0: own}
    ahead = behind = own
    for step in range(1, size // 2 + 1):
        behind = move(behind, pairs_of(1))
        found = {size - step: behind}
        if step <= (size - 1) // 2:
            ahead = move(ahead, pairs_of(-1))
            found[step] = ahead
        yield found


def scatter_order(size):
    groups = []
    for step in range(size // 2):
        group = [size // 2 - step]
        back = (size - 1) // 2 - step
        if back > 0:
            group.append(size - back)
        groups.append(group)
    groups[-1].append(0)
    return groups


def ahead_bins(ahead, size):
    order = [k for group in scatter_order(size) for k in group]
    return sum(jnp.where(ahead == k, place, 0) for place, k in enumerate(order))


def arrival_order(size):
    groups = [[0]]
    for step in range(1, size // 2 + 1):
        groups.append([size - step] + ([step] if step <= (size - 1) // 2 else []))
    return groups


def ring_scatter(chunks_of, size, pairs_of):
    ahead = behind = None

    def onward(running, term):
        return term if running is None else (running.astype(F32) + term.astype(F32)).astype(BF16)

    for step, group in enumerate(scatter_order(size)):
        terms = dict(zip(group, chunks_of(step, ahead)))
        hop, back = size // 2 - step, (size - 1) // 2 - step
        ahead = move(onward(ahead, terms[hop]), pairs_of(1))
        if back > 0:
            behind = move(onward(behind, terms[size - back]), pairs_of(-1))
    total = terms[0].astype(F32) + ahead.astype(F32)
    return total if behind is None else total + behind.astype(F32)


def summed_everywhere(part, grid, gate):
    held = after(part.astype(BF16), *gate)
    got = move(held, grid.across(1, 0))
    yield None
    half = held.shape[0] // CORES
    chip = (held.astype(F32) + after(got, *gate).astype(F32)).astype(BF16)
    held = jnp.where(grid.core == 0, chip[:half], chip[half:])
    bits = [(1 << k, 0) for k in range(1, grid.rows.bit_length() - 1)]
    bits += [(0, 1 << k) for k in range(grid.cols.bit_length() - 1)]
    for row_bit, col_bit in bits:
        got = move(held, grid.across(row_bit, col_bit))
        yield None
        held = (held.astype(F32) + after(got, *gate).astype(F32)).astype(BF16)
    got = move(held, grid.across(1, 0))
    yield None
    own_first, own_last = jnp.concatenate([held, got]), jnp.concatenate([got, held])
    yield jnp.where(grid.core == 0, own_first, own_last).astype(F32)


def per_device(features, node_order, tile_vals, tile_coord, tile_count, weight, cotangent):
    nodes_here, feat_width = features.shape
    tile_size = tile_vals.shape[3]
    row_devices = lax.axis_size("row")
    col_devices = lax.axis_size("col")
    piece = nodes_here // tile_size
    block_cols = row_devices * piece
    block_rows = col_devices * piece
    grad_scale = float(nodes_here * row_devices * col_devices) ** (-0.5)
    grid = Grid(row_devices, col_devices)
    chips = grid.chips

    onehot = permuter(node_order, nodes_here)
    placed = reorder(onehot, features)
    tiles = load_tiles(tile_vals[0, 0])
    coord_here = tile_coord[0, 0]
    tile_total = tile_count[0, 0]
    row_of = coord_here // block_cols
    col_of = coord_here % block_cols

    row_dev = col_of // piece
    far = (row_dev // CORES - grid.x) % chips
    swap = (row_dev % CORES - grid.core) % CORES
    col_dev = row_of // piece
    ahead = sum(jnp.where(col_dev == c, grid.ahead_of[c], 0) for c in range(col_devices))
    source_out = (swap * chips + far) * piece + col_of % piece
    bins_out = ahead_bins(ahead, col_devices) * piece + row_of % piece
    table_out = tile_table(bins_out, block_rows, source_out, tile_total, block_cols)

    along_x = {}
    for found in ring_gather(placed, chips, grid.along_x):
        along_x.update(found)
    along_x = [along_x[k] for k in range(chips)]
    sources_out = along_x + [move(block, grid.across(1, 0)) for block in along_x]
    grads_in = reorder(onehot, cotangent)
    order = scatter_order(col_devices)
    edges = [sum(len(group) for group in order[:k]) * piece for k in range(len(order) + 1)]

    def chunks_of(step, arrived):
        table = table_out if step < 2 else after(table_out, earlier[step - 1])
        earlier.append(arrived)
        bins = (edges[step], edges[step + 1] - edges[step])
        return tile_part(
            False, table, bins, block_rows, tiles, sources_out, block_cols, pieces=nodes_here
        )

    earlier = []
    own_rows = ring_scatter(chunks_of, col_devices, grid.along_walk).astype(BF16)

    pre_act = jnp.dot(own_rows, weight, preferred_element_type=F32)
    own_act = elu_value(pre_act).astype(BF16)
    own_grad = (grads_in.astype(F32) * elu_slope(pre_act)).astype(BF16)
    own_agg_grad = lax.dot_general(
        own_grad, weight, (((1,), (1,)), ((), ())), preferred_element_type=F32
    ).astype(BF16)
    activations = restore(onehot, own_act)

    arrivals = arrival_order(col_devices)
    part_of = sum(jnp.where(ahead == k, p, 0) for p, group in enumerate(arrivals) for k in group)
    block_at = sum(jnp.where(ahead == k, i, 0) for group in arrivals for i, k in enumerate(group))
    place_back = (swap * chips + far) * piece + col_of % piece
    bins_back = len(arrivals) * block_cols
    empty_back = max(len(group) for group in arrivals) * piece
    table_back = tile_table(
        part_of * block_cols + place_back,
        bins_back,
        block_at * piece + row_of % piece,
        tile_total,
        empty_back,
    )
    weight_part = (
        lax.dot_general(own_rows, own_grad, (((0,), (0,)), ((), ())), preferred_element_type=F32)
        * grad_scale
    )
    acc, gate, weight_grad = None, [], None
    weight_steps = summed_everywhere(weight_part, grid, gate)
    for number, found in enumerate(ring_gather(own_agg_grad, col_devices, grid.along_walk)):
        blocks = [found[k] for k in arrivals[number]]
        if number == len(arrivals) - 1:
            break
        bins = (number * block_cols, block_cols)
        (acc,) = tile_part(True, table_back, bins, bins_back, tiles, blocks, empty_back, acc=acc)
        gate[:] = [found[number]] if number in found and number else []
        if number == 3:
            gate.append(activations)
        weight_grad = next(weight_steps, weight_grad)
    bins = ((len(arrivals) - 1) * block_cols, block_cols)
    mine, theirs = tile_part(
        True, table_back, bins, bins_back, tiles, blocks, empty_back, acc=acc, pieces=chips * nodes_here
    )
    gate[:] = [mine]
    weight_grad = next(weight_steps, weight_grad)
    got = move(theirs, grid.across(1, 0))
    both = mine.astype(F32) + got.astype(F32)
    sums = [both[k * nodes_here : (k + 1) * nodes_here] for k in range(chips)]
    sums = [sums[0]] + [term.astype(BF16) for term in sums[1:]]
    gate[:] = sums[1:]
    while weight_grad is None:
        weight_grad = next(weight_steps)
    order = scatter_order(chips)
    placed_grad = ring_scatter(
        lambda step, arrived: [sums[k] for k in order[step]], chips, grid.along_x
    ).astype(BF16)
    feature_grad = restore(onehot, placed_grad)
    return (activations, weight_grad, feature_grad)


def solution(mesh):
    in_specs = (
        P(("row", "col"), None),
        P(("row", "col")),
        P("row", "col", None, None, None),
        P("row", "col", None),
        P("row", "col"),
        P(),
        P(("row", "col"), None),
    )
    out_specs = (P(("row", "col"), None), P(), P(("row", "col"), None))
    return jax.shard_map(
        per_device, mesh=mesh, in_specs=in_specs, out_specs=out_specs, check_vma=False
    )
```

```python
import functools

import jax
import jax.numpy as jnp
from jax import lax
from jax.experimental import pallas as pl
from jax.experimental.pallas import tpu as pltpu
from jax.sharding import PartitionSpec as P

CORES = 2
GROUP = 4
UNROLL = 2
PACK_BITS = 8
PACK = 1 << PACK_BITS
VMEM_BYTES = 16 * 1024 * 1024
LOAD_BYTES = 45 * 1024 * 1024
LOADS = 4
F32 = jnp.float32
BF16 = jnp.bfloat16


def elu_value(pre_act):
    return jnp.where(pre_act > 0, pre_act, jnp.expm1(jnp.minimum(pre_act, 0.0)))


def elu_slope(pre_act):
    return jnp.where(pre_act > 0, 1.0, jnp.exp(jnp.minimum(pre_act, 0.0)))


def permuter(node_order, nodes_here):
    local_pos = node_order % nodes_here
    return (local_pos[:, None] == jnp.arange(nodes_here, dtype=jnp.int32)[None, :]).astype(BF16)


def reorder(onehot, values):
    return jnp.dot(onehot, values, preferred_element_type=F32).astype(BF16)


def restore(onehot, values):
    moved = lax.dot_general(onehot, values, (((0,), (0,)), ((), ())), preferred_element_type=F32)
    return moved.astype(BF16)


def tile_table(bins, bin_total, sources, tile_total, empty):
    slot_total = bins.shape[0]
    group_total = slot_total // GROUP + bin_total + 1
    slots = jnp.arange(slot_total, dtype=jnp.int32)
    marks = jnp.arange(bin_total, dtype=jnp.int32)
    live = slots < tile_total
    held = jnp.where(live, bins, bin_total)
    same = held[:, None] == held[None, :]
    before = jnp.sum((same & (slots[None, :] < slots[:, None])).astype(jnp.int32), axis=1)
    counts = jnp.sum((held[None, :] == marks[:, None]).astype(jnp.int32), axis=1)
    groups = (counts + GROUP - 1) // GROUP
    edges = jnp.arange(bin_total + 1, dtype=jnp.int32)
    firsts = jnp.sum(jnp.where(marks[None, :] < edges[:, None], groups[None, :], 0), axis=1)
    mine = jnp.sum(jnp.where(marks[None, :] < held[:, None], groups[None, :], 0), axis=1)
    place = jnp.where(live, mine * GROUP + before, -1)
    places = jnp.arange(group_total * GROUP, dtype=jnp.int32)
    member = (slots * PACK + sources - empty)[None, :]
    members = empty + jnp.sum(jnp.where(place[None, :] == places[:, None], member, 0), axis=1)
    numbers = jnp.arange(group_total, dtype=jnp.int32)
    group_bin = jnp.sum((firsts[None, 1:] <= numbers[:, None]).astype(jnp.int32), axis=1)
    return jnp.concatenate([members, group_bin, firsts])


def load_kernel(tiles_ref, out_ref, sems):
    share = tiles_ref.shape[0] // LOADS
    copies = [
        pltpu.make_async_copy(
            tiles_ref.at[pl.ds(k * share, share)], out_ref.at[pl.ds(k * share, share)], sems.at[k]
        )
        for k in range(LOADS)
    ]
    for copy in copies:
        copy.start()
    for copy in copies:
        copy.wait()


def load_tiles(tiles):
    return pl.pallas_call(
        load_kernel,
        out_shape=jax.ShapeDtypeStruct(tiles.shape, tiles.dtype),
        in_specs=[pl.BlockSpec(memory_space=pl.ANY)],
        out_specs=pl.BlockSpec(memory_space=pltpu.VMEM),
        scratch_shapes=[pltpu.SemaphoreType.DMA((LOADS,))],
        compiler_params=pltpu.CompilerParams(vmem_limit_bytes=LOAD_BYTES),
        cost_estimate=pl.CostEstimate(flops=0, bytes_accessed=2 * tiles.size, transcendentals=0),
    )(tiles)


def part_kernel(spec, table_ref, tiles_ref, *refs):
    transposed, first_bin, bin_count, bin_total, source_count, carried, finish = spec
    source_refs = refs[:source_count]
    out_refs = refs[source_count + carried : -2]
    source, total = refs[-2:]
    slot_total, tile_size, _ = tiles_ref.shape
    group_total = slot_total // GROUP + bin_total + 1
    at = 0
    for ref in source_refs:
        source[at : at + ref.shape[0], :] = ref[...]
        at += ref.shape[0]
    source[at:, :] = jnp.zeros((source.shape[0] - at, source.shape[1]), source.dtype)
    total[...] = refs[source_count][...] if carried else jnp.zeros_like(total)
    bins_at = group_total * GROUP
    firsts_at = bins_at + group_total
    begin = table_ref[firsts_at + first_bin]
    end = table_ref[firsts_at + first_bin + bin_count]
    contract = 0 if transposed else 1

    def step(number, carry):
        products = []
        for member in range(UNROLL):
            group = begin + number * UNROLL + member
            group = jnp.where(group < end, group, group_total - 1)
            left, right = [], []
            for k in range(GROUP):
                packed = table_ref[group * GROUP + k]
                left.append(tiles_ref[packed >> PACK_BITS])
                row = pl.multiple_of((packed & (PACK - 1)) * tile_size, tile_size)
                right.append(source[pl.ds(row, tile_size), :])
            product = lax.dot_general(
                jnp.concatenate(left, axis=contract),
                jnp.concatenate(right, axis=0),
                (((contract,), (0,)), ((), ())),
                preferred_element_type=F32,
            )
            products.append((jnp.minimum(table_ref[bins_at + group] - first_bin, bin_count - 1), product))
        for place, product in products:
            rows = pl.ds(pl.multiple_of(place * tile_size, tile_size), tile_size)
            total[rows, :] += product
        return carry

    lax.fori_loop(0, (end - begin + UNROLL - 1) // UNROLL, step, 0)
    if finish:
        at = 0
        for ref in out_refs:
            ref[...] = total[at : at + ref.shape[0], :].astype(ref.dtype)
            at += ref.shape[0]
    else:
        out_refs[0][...] = total[...]


def tile_part(transposed, table, bins, bin_total, tiles, sources, empty, acc=None, pieces=None):
    first_bin, bin_count = bins
    slot_total, tile_size, _ = tiles.shape
    width = sources[0].shape[1]
    rows = bin_count * tile_size
    vmem = pl.BlockSpec(memory_space=pltpu.VMEM)
    if pieces is None:
        out_shape = [jax.ShapeDtypeStruct((rows, width), F32)]
    else:
        out_shape = [jax.ShapeDtypeStruct((pieces, width), BF16)] * (rows // pieces)
    carried = acc is not None
    share = slot_total * bin_count // bin_total
    given = [table, tiles, *sources] + ([] if acc is None else [acc])
    spec = (transposed, first_bin, bin_count, bin_total, len(sources), carried, pieces is not None)
    return pl.pallas_call(
        functools.partial(part_kernel, spec),
        out_shape=out_shape,
        in_specs=[pl.BlockSpec(memory_space=pltpu.SMEM)] + [vmem] * (len(given) - 1),
        out_specs=[vmem] * len(out_shape),
        scratch_shapes=[
            pltpu.VMEM(((empty + 1) * tile_size, width), BF16),
            pltpu.VMEM((rows, width), F32),
        ],
        compiler_params=pltpu.CompilerParams(vmem_limit_bytes=VMEM_BYTES),
        cost_estimate=pl.CostEstimate(
            flops=2 * share * tile_size * tile_size * width,
            bytes_accessed=2 * share * tile_size * tile_size,
            transcendentals=0,
        ),
    )(*given)


def grid_cycle(size):
    ny = 1
    while (2 * ny) ** 2 <= size:
        ny *= 2
    nz = size // ny
    walk = [0]
    for z in range(nz):
        ys = range(1, ny) if z % 2 == 0 else range(ny - 1, 0, -1)
        walk += [z * ny + y for y in ys]
    walk += [z * ny for z in range(nz - 1, 0, -1)]
    return walk


class Grid:
    def __init__(self, rows, cols):
        self.rows, self.cols, self.chips = rows, cols, rows // CORES
        self.walk = grid_cycle(cols)
        self.place_of = [self.walk.index(c) for c in range(cols)]
        self.row, self.col = lax.axis_index("row"), lax.axis_index("col")
        self.x, self.core = self.row // CORES, self.row % CORES
        place = sum(jnp.where(self.col == c, self.place_of[c], 0) for c in range(cols))
        self.ahead_of = [
            jnp.where(self.core == 0, self.place_of[c] - place, place - self.place_of[c]) % cols
            for c in range(cols)
        ]

    def along_walk(self, step):
        pairs = []
        for r in range(self.rows):
            walk = self.walk if r % CORES == 0 else self.walk[::-1]
            for k in range(self.cols):
                pairs.append((r * self.cols + walk[k], r * self.cols + walk[(k + step) % self.cols]))
        return pairs

    def along_x(self, step):
        return [
            (r * self.cols + c, ((r + step * CORES) % self.rows) * self.cols + c)
            for r in range(self.rows)
            for c in range(self.cols)
        ]

    def across(self, row_bit, col_bit):
        return [
            (r * self.cols + c, (r ^ row_bit) * self.cols + (c ^ col_bit))
            for r in range(self.rows)
            for c in range(self.cols)
        ]


def move(value, pairs):
    return lax.ppermute(value, ("row", "col"), pairs)


def after(value, *others):
    return lax.optimization_barrier((value, *others))[0]


def ring_gather(own, size, pairs_of, hold):
    yield {0: own}
    ahead = behind = own
    for step in range(1, size // 2 + 1):
        behind = move(after(behind, *hold.get(step, [])), pairs_of(1))
        found = {size - step: behind}
        if step <= (size - 1) // 2:
            ahead = move(ahead, pairs_of(-1))
            found[step] = ahead
        yield found


def scatter_order(size):
    groups = []
    for step in range(size // 2):
        group = [size // 2 - step]
        back = (size - 1) // 2 - step
        if back > 0:
            group.append(size - back)
        groups.append(group)
    groups[-1].append(0)
    return groups


def ahead_bins(ahead, size):
    order = [k for group in scatter_order(size) for k in group]
    return sum(jnp.where(ahead == k, place, 0) for place, k in enumerate(order))


def arrival_order(size):
    groups = [[0]]
    for step in range(1, size // 2 + 1):
        groups.append([size - step] + ([step] if step <= (size - 1) // 2 else []))
    return groups


def ring_scatter(chunks_of, size, pairs_of):
    ahead = behind = None

    def onward(running, term):
        return term if running is None else (running.astype(F32) + term.astype(F32)).astype(BF16)

    for step, group in enumerate(scatter_order(size)):
        terms = dict(zip(group, chunks_of(step, ahead)))
        hop, back = size // 2 - step, (size - 1) // 2 - step
        ahead = move(onward(ahead, terms[hop]), pairs_of(1))
        if back > 0:
            behind = move(onward(behind, terms[size - back]), pairs_of(-1))
    total = terms[0].astype(F32) + ahead.astype(F32)
    return total if behind is None else total + behind.astype(F32)


def summed_everywhere(part, grid, gate):
    held = after(part.astype(BF16), *gate)
    got = move(held, grid.across(1, 0))
    yield None
    half = held.shape[0] // CORES
    chip = (held.astype(F32) + after(got, *gate).astype(F32)).astype(BF16)
    held = jnp.where(grid.core == 0, chip[:half], chip[half:])
    bits = [(1 << k, 0) for k in range(1, grid.rows.bit_length() - 1)]
    bits += [(0, 1 << k) for k in range(grid.cols.bit_length() - 1)]
    for row_bit, col_bit in bits:
        got = move(held, grid.across(row_bit, col_bit))
        yield None
        held = (held.astype(F32) + after(got, *gate).astype(F32)).astype(BF16)
    got = move(held, grid.across(1, 0))
    yield None
    own_first, own_last = jnp.concatenate([held, got]), jnp.concatenate([got, held])
    yield jnp.where(grid.core == 0, own_first, own_last).astype(F32)


def per_device(features, node_order, tile_vals, tile_coord, tile_count, weight, cotangent):
    nodes_here, feat_width = features.shape
    tile_size = tile_vals.shape[3]
    row_devices = lax.axis_size("row")
    col_devices = lax.axis_size("col")
    piece = nodes_here // tile_size
    block_cols = row_devices * piece
    block_rows = col_devices * piece
    grad_scale = float(nodes_here * row_devices * col_devices) ** (-0.5)
    grid = Grid(row_devices, col_devices)
    chips = grid.chips

    onehot = permuter(node_order, nodes_here)
    placed = reorder(onehot, features)
    tiles = load_tiles(tile_vals[0, 0])
    coord_here = tile_coord[0, 0]
    tile_total = tile_count[0, 0]

    def block_places(coord):
        row_of, col_of = coord // block_cols, coord % block_cols
        row_dev, col_dev = col_of // piece, row_of // piece
        far = (row_dev // CORES - grid.x) % chips
        swap = (row_dev % CORES - grid.core) % CORES
        ahead = sum(jnp.where(col_dev == c, grid.ahead_of[c], 0) for c in range(col_devices))
        return swap * chips + far, col_of % piece, ahead, row_of % piece

    row_place, col_piece, ahead, row_piece = block_places(coord_here)
    bins_out = ahead_bins(ahead, col_devices) * piece + row_piece
    source_out = row_place * piece + col_piece
    table_out = tile_table(bins_out, block_rows, source_out, tile_total, block_cols)

    along_x = {}
    for found in ring_gather(placed, chips, grid.along_x, {}):
        along_x.update(found)
    along_x = [along_x[k] for k in range(chips)]
    sources_out = along_x + [move(block, grid.across(1, 0)) for block in along_x]
    grads_in = reorder(onehot, cotangent)
    order = scatter_order(col_devices)
    edges = [sum(len(group) for group in order[:k]) * piece for k in range(len(order) + 1)]

    def chunks_of(step, arrived):
        table = table_out if step < 2 else after(table_out, earlier[step - 1])
        earlier.append(arrived)
        bins = (edges[step], edges[step + 1] - edges[step])
        made = tile_part(
            False, table, bins, block_rows, tiles, sources_out, block_cols, pieces=nodes_here
        )
        parts.append(made[0])
        return made

    earlier, parts = [], []
    own_rows = ring_scatter(chunks_of, col_devices, grid.along_walk).astype(BF16)

    pre_act = jnp.dot(own_rows, weight, preferred_element_type=F32)
    own_act = elu_value(pre_act).astype(BF16)
    own_grad = (grads_in.astype(F32) * elu_slope(pre_act)).astype(BF16)
    own_agg_grad = lax.dot_general(
        own_grad, weight, (((1,), (1,)), ((), ())), preferred_element_type=F32
    ).astype(BF16)
    arrivals = arrival_order(col_devices)
    row_place, col_piece, ahead, row_piece = block_places(after(coord_here, parts[1]))
    part_of = sum(jnp.where(ahead == k, p, 0) for p, group in enumerate(arrivals) for k in group)
    block_at = sum(jnp.where(ahead == k, i, 0) for group in arrivals for i, k in enumerate(group))
    bins_back = len(arrivals) * block_cols
    empty_back = max(len(group) for group in arrivals) * piece
    table_back = tile_table(
        part_of * block_cols + row_place * piece + col_piece,
        bins_back,
        block_at * piece + row_piece,
        tile_total,
        empty_back,
    )
    weight_part = (
        lax.dot_general(own_rows, own_grad, (((0,), (0,)), ((), ())), preferred_element_type=F32)
        * grad_scale
    )
    acc, gate, hold, weight_grad = None, [], {}, None
    weight_steps = summed_everywhere(weight_part, grid, gate)
    weight_grad = next(weight_steps)
    for number, found in enumerate(ring_gather(own_agg_grad, col_devices, grid.along_walk, hold)):
        blocks = [found[k] for k in arrivals[number]]
        if number == len(arrivals) - 1:
            break
        bins = (number * block_cols, block_cols)
        (acc,) = tile_part(True, table_back, bins, bins_back, tiles, blocks, empty_back, acc=acc)
        hold[number + 2] = [acc]
        gate[:] = [found[number]] if number else [acc]
        weight_grad = next(weight_steps, weight_grad)
    bins = ((len(arrivals) - 1) * block_cols, block_cols)
    mine, theirs = tile_part(
        True, table_back, bins, bins_back, tiles, blocks, empty_back, acc=acc, pieces=chips * nodes_here
    )
    gate[:] = [mine]
    weight_grad = next(weight_steps, weight_grad)
    got = move(theirs, grid.across(1, 0))
    both = mine.astype(F32) + got.astype(F32)
    sums = [both[k * nodes_here : (k + 1) * nodes_here] for k in range(chips)]
    sums = [sums[0]] + [term.astype(BF16) for term in sums[1:]]
    gate[:] = sums[1:]
    while weight_grad is None:
        weight_grad = next(weight_steps)
    order = scatter_order(chips)
    placed_grad = ring_scatter(
        lambda step, arrived: [sums[k] for k in order[step]], chips, grid.along_x
    ).astype(BF16)
    activations = restore(onehot, own_act)
    feature_grad = restore(onehot, placed_grad)
    return (activations, weight_grad, feature_grad)


def solution(mesh):
    in_specs = (
        P(("row", "col"), None),
        P(("row", "col")),
        P("row", "col", None, None, None),
        P("row", "col", None),
        P("row", "col"),
        P(),
        P(("row", "col"), None),
    )
    out_specs = (P(("row", "col"), None), P(), P(("row", "col"), None))
    return jax.shard_map(
        per_device, mesh=mesh, in_specs=in_specs, out_specs=out_specs, check_vma=False
    )
```

```python
import functools

import jax
import jax.numpy as jnp
from jax import lax
from jax.experimental import pallas as pl
from jax.experimental.pallas import tpu as pltpu
from jax.sharding import PartitionSpec as P

CORES = 2
GROUP = 4
UNROLL = 2
PACK_BITS = 8
PACK = 1 << PACK_BITS
VMEM_BYTES = 16 * 1024 * 1024
LOAD_BYTES = 45 * 1024 * 1024
LOADS = 4
F32 = jnp.float32
BF16 = jnp.bfloat16


def elu_value(pre_act):
    return jnp.where(pre_act > 0, pre_act, jnp.expm1(jnp.minimum(pre_act, 0.0)))


def elu_slope(pre_act):
    return jnp.where(pre_act > 0, 1.0, jnp.exp(jnp.minimum(pre_act, 0.0)))


def permuter(node_order, nodes_here):
    local_pos = node_order % nodes_here
    return (local_pos[:, None] == jnp.arange(nodes_here, dtype=jnp.int32)[None, :]).astype(BF16)


def reorder(onehot, values):
    return jnp.dot(onehot, values, preferred_element_type=F32).astype(BF16)


def restore(onehot, values):
    moved = lax.dot_general(onehot, values, (((0,), (0,)), ((), ())), preferred_element_type=F32)
    return moved.astype(BF16)


def tile_table(bins, bin_total, sources, tile_total, empty):
    slot_total = bins.shape[0]
    group_total = slot_total // GROUP + bin_total + 1
    slots = jnp.arange(slot_total, dtype=jnp.int32)
    marks = jnp.arange(bin_total, dtype=jnp.int32)
    live = slots < tile_total
    held = jnp.where(live, bins, bin_total)
    same = held[:, None] == held[None, :]
    before = jnp.sum((same & (slots[None, :] < slots[:, None])).astype(jnp.int32), axis=1)
    counts = jnp.sum((held[None, :] == marks[:, None]).astype(jnp.int32), axis=1)
    groups = (counts + GROUP - 1) // GROUP
    edges = jnp.arange(bin_total + 1, dtype=jnp.int32)
    firsts = jnp.sum(jnp.where(marks[None, :] < edges[:, None], groups[None, :], 0), axis=1)
    mine = jnp.sum(jnp.where(marks[None, :] < held[:, None], groups[None, :], 0), axis=1)
    place = jnp.where(live, mine * GROUP + before, -1)
    places = jnp.arange(group_total * GROUP, dtype=jnp.int32)
    member = (slots * PACK + sources - empty)[None, :]
    members = empty + jnp.sum(jnp.where(place[None, :] == places[:, None], member, 0), axis=1)
    numbers = jnp.arange(group_total, dtype=jnp.int32)
    group_bin = jnp.sum((firsts[None, 1:] <= numbers[:, None]).astype(jnp.int32), axis=1)
    return jnp.concatenate([members, group_bin, firsts])


def load_kernel(tiles_ref, out_ref, sems):
    share = tiles_ref.shape[0] // LOADS
    copies = [
        pltpu.make_async_copy(
            tiles_ref.at[pl.ds(k * share, share)], out_ref.at[pl.ds(k * share, share)], sems.at[k]
        )
        for k in range(LOADS)
    ]
    for copy in copies:
        copy.start()
    for copy in copies:
        copy.wait()


def load_tiles(tiles):
    return pl.pallas_call(
        load_kernel,
        out_shape=jax.ShapeDtypeStruct(tiles.shape, tiles.dtype),
        in_specs=[pl.BlockSpec(memory_space=pl.ANY)],
        out_specs=pl.BlockSpec(memory_space=pltpu.VMEM),
        scratch_shapes=[pltpu.SemaphoreType.DMA((LOADS,))],
        compiler_params=pltpu.CompilerParams(vmem_limit_bytes=LOAD_BYTES),
        cost_estimate=pl.CostEstimate(flops=0, bytes_accessed=2 * tiles.size, transcendentals=0),
    )(tiles)


def part_kernel(spec, table_ref, tiles_ref, *refs):
    transposed, first_bin, bin_count, bin_total, source_count, carried, finish = spec
    source_refs = refs[:source_count]
    out_refs = refs[source_count + carried : -2]
    source, total = refs[-2:]
    slot_total, tile_size, _ = tiles_ref.shape
    group_total = slot_total // GROUP + bin_total + 1
    at = 0
    for ref in source_refs:
        source[at : at + ref.shape[0], :] = ref[...]
        at += ref.shape[0]
    source[at:, :] = jnp.zeros((source.shape[0] - at, source.shape[1]), source.dtype)
    total[...] = refs[source_count][...] if carried else jnp.zeros_like(total)
    bins_at = group_total * GROUP
    firsts_at = bins_at + group_total
    begin = table_ref[firsts_at + first_bin]
    end = table_ref[firsts_at + first_bin + bin_count]
    contract = 0 if transposed else 1

    def step(number, carry):
        products = []
        for member in range(UNROLL):
            group = begin + number * UNROLL + member
            group = jnp.where(group < end, group, group_total - 1)
            left, right = [], []
            for k in range(GROUP):
                packed = table_ref[group * GROUP + k]
                left.append(tiles_ref[packed >> PACK_BITS])
                row = pl.multiple_of((packed & (PACK - 1)) * tile_size, tile_size)
                right.append(source[pl.ds(row, tile_size), :])
            product = lax.dot_general(
                jnp.concatenate(left, axis=contract),
                jnp.concatenate(right, axis=0),
                (((contract,), (0,)), ((), ())),
                preferred_element_type=F32,
            )
            products.append((jnp.minimum(table_ref[bins_at + group] - first_bin, bin_count - 1), product))
        for place, product in products:
            rows = pl.ds(pl.multiple_of(place * tile_size, tile_size), tile_size)
            total[rows, :] += product
        return carry

    lax.fori_loop(0, (end - begin + UNROLL - 1) // UNROLL, step, 0)
    if finish:
        at = 0
        for ref in out_refs:
            ref[...] = total[at : at + ref.shape[0], :].astype(ref.dtype)
            at += ref.shape[0]
    else:
        out_refs[0][...] = total[...]


def tile_part(transposed, table, bins, bin_total, tiles, sources, empty, acc=None, pieces=None):
    first_bin, bin_count = bins
    slot_total, tile_size, _ = tiles.shape
    width = sources[0].shape[1]
    rows = bin_count * tile_size
    vmem = pl.BlockSpec(memory_space=pltpu.VMEM)
    if pieces is None:
        out_shape = [jax.ShapeDtypeStruct((rows, width), F32)]
    else:
        out_shape = [jax.ShapeDtypeStruct((pieces, width), BF16)] * (rows // pieces)
    carried = acc is not None
    share = slot_total * bin_count // bin_total
    given = [table, tiles, *sources] + ([] if acc is None else [acc])
    spec = (transposed, first_bin, bin_count, bin_total, len(sources), carried, pieces is not None)
    return pl.pallas_call(
        functools.partial(part_kernel, spec),
        out_shape=out_shape,
        in_specs=[pl.BlockSpec(memory_space=pltpu.SMEM)] + [vmem] * (len(given) - 1),
        out_specs=[vmem] * len(out_shape),
        scratch_shapes=[
            pltpu.VMEM(((empty + 1) * tile_size, width), BF16),
            pltpu.VMEM((rows, width), F32),
        ],
        compiler_params=pltpu.CompilerParams(vmem_limit_bytes=VMEM_BYTES),
        cost_estimate=pl.CostEstimate(
            flops=2 * share * tile_size * tile_size * width,
            bytes_accessed=2 * share * tile_size * tile_size,
            transcendentals=0,
        ),
    )(*given)


def grid_cycle(size):
    ny = 1
    while (2 * ny) ** 2 <= size:
        ny *= 2
    nz = size // ny
    walk = [0]
    for z in range(nz):
        ys = range(1, ny) if z % 2 == 0 else range(ny - 1, 0, -1)
        walk += [z * ny + y for y in ys]
    walk += [z * ny for z in range(nz - 1, 0, -1)]
    return walk


class Grid:
    def __init__(self, rows, cols):
        self.rows, self.cols, self.chips = rows, cols, rows // CORES
        self.walk = grid_cycle(cols)
        self.place_of = [self.walk.index(c) for c in range(cols)]
        self.row, self.col = lax.axis_index("row"), lax.axis_index("col")
        self.x, self.core = self.row // CORES, self.row % CORES
        place = sum(jnp.where(self.col == c, self.place_of[c], 0) for c in range(cols))
        self.ahead_of = [
            jnp.where(self.core == 0, self.place_of[c] - place, place - self.place_of[c]) % cols
            for c in range(cols)
        ]

    def along_walk(self, step):
        pairs = []
        for r in range(self.rows):
            walk = self.walk if r % CORES == 0 else self.walk[::-1]
            for k in range(self.cols):
                pairs.append((r * self.cols + walk[k], r * self.cols + walk[(k + step) % self.cols]))
        return pairs

    def along_x(self, step):
        return [
            (r * self.cols + c, ((r + step * CORES) % self.rows) * self.cols + c)
            for r in range(self.rows)
            for c in range(self.cols)
        ]

    def across(self, row_bit, col_bit):
        return [
            (r * self.cols + c, (r ^ row_bit) * self.cols + (c ^ col_bit))
            for r in range(self.rows)
            for c in range(self.cols)
        ]


def move(value, pairs):
    return lax.ppermute(value, ("row", "col"), pairs)


def after(value, *others):
    return lax.optimization_barrier((value, *others))[0]


def ring_hops(size):
    return (size - 1) // 2


def arrival_order(size):
    hops = ring_hops(size)
    groups = [[0]] + [[size - step, step] for step in range(1, hops + 1)]
    if size % 2 == 0:
        if hops:
            groups[min(2, hops)].append(size // 2)
        else:
            groups.append([size // 2])
    return groups


def ring_gather(own, size, pairs_of, hold):
    yield {0: own}
    ahead = behind = own
    for step, group in enumerate(arrival_order(size)[1:], 1):
        found = {}
        if step == 1:
            opposite = move(own, pairs_of(size // 2)) if size % 2 == 0 else None
        if step <= ring_hops(size):
            behind = move(after(behind, *hold.get(step, [])), pairs_of(1))
            ahead = move(ahead, pairs_of(-1))
            found = {size - step: behind, step: ahead}
        if size // 2 in group and size % 2 == 0:
            found[size // 2] = opposite
        yield found


def scatter_order(size):
    hops = ring_hops(size)
    groups = [[hop, size - hop] for hop in range(hops, 0, -1)] or [[]]
    if size % 2 == 0:
        groups[min(1, len(groups) - 1)].insert(0, size // 2)
    groups[-1].append(0)
    return groups


def ahead_bins(ahead, size):
    order = [k for group in scatter_order(size) for k in group]
    return sum(jnp.where(ahead == k, place, 0) for place, k in enumerate(order))


def ring_scatter(chunks_of, size, pairs_of):
    ahead = behind = opposite = None

    def onward(running, term):
        return term if running is None else (running.astype(F32) + term.astype(F32)).astype(BF16)

    for step, group in enumerate(scatter_order(size)):
        terms = dict(zip(group, chunks_of(step, ahead)))
        hop = ring_hops(size) - step
        if hop > 0:
            ahead = move(onward(ahead, terms[hop]), pairs_of(1))
            behind = move(onward(behind, terms[size - hop]), pairs_of(-1))
        if size // 2 in group and size % 2 == 0:
            opposite = move(terms[size // 2], pairs_of(size // 2))
    total = terms[0].astype(F32)
    for part in (opposite, ahead, behind):
        if part is not None:
            total = total + part.astype(F32)
    return total


def summed_everywhere(part, grid, gate):
    held = after(part.astype(BF16), *gate)
    got = move(held, grid.across(1, 0))
    yield None
    half = held.shape[0] // CORES
    chip = (held.astype(F32) + after(got, *gate).astype(F32)).astype(BF16)
    held = jnp.where(grid.core == 0, chip[:half], chip[half:])
    bits = [(1 << k, 0) for k in range(1, grid.rows.bit_length() - 1)]
    bits += [(0, 1 << k) for k in range(grid.cols.bit_length() - 1)]
    for row_bit, col_bit in bits:
        got = move(held, grid.across(row_bit, col_bit))
        yield None
        held = (held.astype(F32) + after(got, *gate).astype(F32)).astype(BF16)
    got = move(held, grid.across(1, 0))
    yield None
    own_first, own_last = jnp.concatenate([held, got]), jnp.concatenate([got, held])
    yield jnp.where(grid.core == 0, own_first, own_last).astype(F32)


def per_device(features, node_order, tile_vals, tile_coord, tile_count, weight, cotangent):
    nodes_here, feat_width = features.shape
    tile_size = tile_vals.shape[3]
    row_devices = lax.axis_size("row")
    col_devices = lax.axis_size("col")
    piece = nodes_here // tile_size
    block_cols = row_devices * piece
    block_rows = col_devices * piece
    grad_scale = float(nodes_here * row_devices * col_devices) ** (-0.5)
    grid = Grid(row_devices, col_devices)
    chips = grid.chips

    onehot = permuter(node_order, nodes_here)
    placed = reorder(onehot, features)
    tiles = load_tiles(tile_vals[0, 0])
    coord_here = after(tile_coord[0, 0], tiles)
    tile_total = tile_count[0, 0]

    def block_places(coord):
        row_of, col_of = coord // block_cols, coord % block_cols
        row_dev, col_dev = col_of // piece, row_of // piece
        far = (row_dev // CORES - grid.x) % chips
        swap = (row_dev % CORES - grid.core) % CORES
        ahead = sum(jnp.where(col_dev == c, grid.ahead_of[c], 0) for c in range(col_devices))
        return swap * chips + far, col_of % piece, ahead, row_of % piece

    row_place, col_piece, ahead, row_piece = block_places(coord_here)
    bins_out = ahead_bins(ahead, col_devices) * piece + row_piece
    source_out = row_place * piece + col_piece
    table_out = tile_table(bins_out, block_rows, source_out, tile_total, block_cols)

    along_x = {}
    for found in ring_gather(placed, chips, grid.along_x, {}):
        along_x.update(found)
    along_x = [along_x[k] for k in range(chips)]
    sources_out = along_x + [move(block, grid.across(1, 0)) for block in along_x]
    grads_in = reorder(onehot, cotangent)
    order = scatter_order(col_devices)
    edges = [sum(len(group) for group in order[:k]) * piece for k in range(len(order) + 1)]

    def chunks_of(step, arrived):
        table = table_out if step < 2 else after(table_out, earlier[step - 1])
        earlier.append(arrived)
        bins = (edges[step], edges[step + 1] - edges[step])
        return tile_part(
            False, table, bins, block_rows, tiles, sources_out, block_cols, pieces=nodes_here
        )

    earlier = []
    own_rows = ring_scatter(chunks_of, col_devices, grid.along_walk).astype(BF16)

    pre_act = jnp.dot(own_rows, weight, preferred_element_type=F32)
    own_act = elu_value(pre_act).astype(BF16)
    own_grad = (grads_in.astype(F32) * elu_slope(pre_act)).astype(BF16)
    own_agg_grad = lax.dot_general(
        own_grad, weight, (((1,), (1,)), ((), ())), preferred_element_type=F32
    ).astype(BF16)
    arrivals = arrival_order(col_devices)
    row_place, col_piece, ahead, row_piece = block_places(after(tile_coord[0, 0], *earlier[1:2]))
    part_of = sum(jnp.where(ahead == k, p, 0) for p, group in enumerate(arrivals) for k in group)
    block_at = sum(jnp.where(ahead == k, i, 0) for group in arrivals for i, k in enumerate(group))
    bins_back = len(arrivals) * block_cols
    empty_back = max(len(group) for group in arrivals) * piece
    table_back = tile_table(
        part_of * block_cols + row_place * piece + col_piece,
        bins_back,
        block_at * piece + row_piece,
        tile_total,
        empty_back,
    )
    weight_part = (
        lax.dot_general(own_rows, own_grad, (((0,), (0,)), ((), ())), preferred_element_type=F32)
        * grad_scale
    )
    acc, gate, hold, weight_grad = None, [], {}, None
    weight_steps = summed_everywhere(weight_part, grid, gate)
    weight_grad = next(weight_steps)
    for number, found in enumerate(ring_gather(own_agg_grad, col_devices, grid.along_walk, hold)):
        blocks = [found[k] for k in arrivals[number]]
        if number == len(arrivals) - 1:
            break
        bins = (number * block_cols, block_cols)
        (acc,) = tile_part(True, table_back, bins, bins_back, tiles, blocks, empty_back, acc=acc)
        hold[number + 2] = [acc]
        gate[:] = [found[number]] if number else [acc]
        weight_grad = next(weight_steps, weight_grad)
    gate[:] = blocks
    weight_grad = next(weight_steps, weight_grad)
    bins = ((len(arrivals) - 1) * block_cols, block_cols)
    mine, theirs = tile_part(
        True, table_back, bins, bins_back, tiles, blocks, empty_back, acc=acc, pieces=chips * nodes_here
    )
    got = move(theirs, grid.across(1, 0))
    both = mine.astype(F32) + got.astype(F32)
    sums = [both[k * nodes_here : (k + 1) * nodes_here] for k in range(chips)]
    sums = [sums[0]] + [term.astype(BF16) for term in sums[1:]]
    gate[:] = sums[1:]
    while weight_grad is None:
        weight_grad = next(weight_steps)
    order = scatter_order(chips)
    placed_grad = ring_scatter(
        lambda step, arrived: [sums[k] for k in order[step]], chips, grid.along_x
    ).astype(BF16)
    activations = restore(onehot, own_act)
    feature_grad = restore(onehot, placed_grad)
    return (activations, weight_grad, feature_grad)


def solution(mesh):
    in_specs = (
        P(("row", "col"), None),
        P(("row", "col")),
        P("row", "col", None, None, None),
        P("row", "col", None),
        P("row", "col"),
        P(),
        P(("row", "col"), None),
    )
    out_specs = (P(("row", "col"), None), P(), P(("row", "col"), None))
    return jax.shard_map(
        per_device, mesh=mesh, in_specs=in_specs, out_specs=out_specs, check_vma=False
    )
```

```python
import functools

import jax
import jax.numpy as jnp
from jax import lax
from jax.experimental import pallas as pl
from jax.experimental.pallas import tpu as pltpu
from jax.sharding import PartitionSpec as P

CORES = 2
GROUP = 4
UNROLL = 4
PACK_BITS = 8
PACK = 1 << PACK_BITS
VMEM_BYTES = 16 * 1024 * 1024
LOAD_BYTES = 45 * 1024 * 1024
LOADS = 4
F32 = jnp.float32
BF16 = jnp.bfloat16


def elu_value(pre_act):
    return jnp.where(pre_act > 0, pre_act, jnp.expm1(jnp.minimum(pre_act, 0.0)))


def elu_slope(pre_act):
    return jnp.where(pre_act > 0, 1.0, jnp.exp(jnp.minimum(pre_act, 0.0)))


def permuter(node_order, nodes_here):
    local_pos = node_order % nodes_here
    return (local_pos[:, None] == jnp.arange(nodes_here, dtype=jnp.int32)[None, :]).astype(BF16)


def reorder(onehot, values):
    return jnp.dot(onehot, values, preferred_element_type=F32).astype(BF16)


def restore(onehot, values):
    moved = lax.dot_general(onehot, values, (((0,), (0,)), ((), ())), preferred_element_type=F32)
    return moved.astype(BF16)


def tile_table(bins, bin_total, sources, tile_total, empty):
    slot_total = bins.shape[0]
    group_total = slot_total // GROUP + bin_total + 1
    slots = jnp.arange(slot_total, dtype=jnp.int32)
    marks = jnp.arange(bin_total, dtype=jnp.int32)
    live = slots < tile_total
    held = jnp.where(live, bins, bin_total)
    same = held[:, None] == held[None, :]
    before = jnp.sum((same & (slots[None, :] < slots[:, None])).astype(jnp.int32), axis=1)
    counts = jnp.sum((held[None, :] == marks[:, None]).astype(jnp.int32), axis=1)
    groups = (counts + GROUP - 1) // GROUP
    edges = jnp.arange(bin_total + 1, dtype=jnp.int32)
    firsts = jnp.sum(jnp.where(marks[None, :] < edges[:, None], groups[None, :], 0), axis=1)
    mine = jnp.sum(jnp.where(marks[None, :] < held[:, None], groups[None, :], 0), axis=1)
    place = jnp.where(live, mine * GROUP + before, -1)
    places = jnp.arange(group_total * GROUP, dtype=jnp.int32)
    member = (slots * PACK + sources - empty)[None, :]
    members = empty + jnp.sum(jnp.where(place[None, :] == places[:, None], member, 0), axis=1)
    numbers = jnp.arange(group_total, dtype=jnp.int32)
    group_bin = jnp.sum((firsts[None, 1:] <= numbers[:, None]).astype(jnp.int32), axis=1)
    return jnp.concatenate([members, group_bin, firsts])


def load_kernel(tiles_ref, out_ref, token_ref, sems):
    share = tiles_ref.shape[0] // LOADS
    copies = [
        pltpu.make_async_copy(
            tiles_ref.at[pl.ds(k * share, share)], out_ref.at[pl.ds(k * share, share)], sems.at[k]
        )
        for k in range(LOADS)
    ]
    for copy in copies:
        copy.start()
    token_ref[...] = jnp.zeros_like(token_ref)
    for copy in copies:
        copy.wait()


def load_tiles(tiles):
    return pl.pallas_call(
        load_kernel,
        out_shape=[
            jax.ShapeDtypeStruct(tiles.shape, tiles.dtype),
            jax.ShapeDtypeStruct((8, 128), F32),
        ],
        in_specs=[pl.BlockSpec(memory_space=pl.ANY)],
        out_specs=[pl.BlockSpec(memory_space=pltpu.VMEM)] * 2,
        scratch_shapes=[pltpu.SemaphoreType.DMA((LOADS,))],
        compiler_params=pltpu.CompilerParams(vmem_limit_bytes=LOAD_BYTES),
        cost_estimate=pl.CostEstimate(flops=0, bytes_accessed=2 * tiles.size, transcendentals=0),
    )(tiles)


def part_kernel(spec, table_ref, tiles_ref, *refs):
    transposed, first_bin, bin_count, bin_total, source_count, carried, finish = spec
    source_refs = refs[:source_count]
    out_refs = refs[source_count + carried : -2]
    source, total = refs[-2:]
    slot_total, tile_size, _ = tiles_ref.shape
    group_total = slot_total // GROUP + bin_total + 1
    at = 0
    for ref in source_refs:
        source[at : at + ref.shape[0], :] = ref[...]
        at += ref.shape[0]
    source[at:, :] = jnp.zeros((source.shape[0] - at, source.shape[1]), source.dtype)
    total[...] = refs[source_count][...] if carried else jnp.zeros_like(total)
    bins_at = group_total * GROUP
    firsts_at = bins_at + group_total
    begin = table_ref[firsts_at + first_bin]
    end = table_ref[firsts_at + first_bin + bin_count]
    contract = 0 if transposed else 1

    def step(number, carry):
        products = []
        for member in range(UNROLL):
            group = begin + number * UNROLL + member
            group = jnp.where(group < end, group, group_total - 1)
            left, right = [], []
            for k in range(GROUP):
                packed = table_ref[group * GROUP + k]
                left.append(tiles_ref[packed >> PACK_BITS])
                row = pl.multiple_of((packed & (PACK - 1)) * tile_size, tile_size)
                right.append(source[pl.ds(row, tile_size), :])
            product = lax.dot_general(
                jnp.concatenate(left, axis=contract),
                jnp.concatenate(right, axis=0),
                (((contract,), (0,)), ((), ())),
                preferred_element_type=F32,
            )
            products.append((jnp.minimum(table_ref[bins_at + group] - first_bin, bin_count - 1), product))
        for place, product in products:
            rows = pl.ds(pl.multiple_of(place * tile_size, tile_size), tile_size)
            total[rows, :] += product
        return carry

    lax.fori_loop(0, (end - begin + UNROLL - 1) // UNROLL, step, 0)
    if finish:
        at = 0
        for ref in out_refs:
            ref[...] = total[at : at + ref.shape[0], :].astype(ref.dtype)
            at += ref.shape[0]
    else:
        out_refs[0][...] = total[...]


def tile_part(transposed, table, bins, bin_total, tiles, sources, empty, acc=None, pieces=None):
    first_bin, bin_count = bins
    slot_total, tile_size, _ = tiles.shape
    width = sources[0].shape[1]
    rows = bin_count * tile_size
    vmem = pl.BlockSpec(memory_space=pltpu.VMEM)
    if pieces is None:
        out_shape = [jax.ShapeDtypeStruct((rows, width), F32)]
    else:
        out_shape = [jax.ShapeDtypeStruct((pieces, width), BF16)] * (rows // pieces)
    carried = acc is not None
    share = slot_total * bin_count // bin_total
    given = [table, tiles, *sources] + ([] if acc is None else [acc])
    spec = (transposed, first_bin, bin_count, bin_total, len(sources), carried, pieces is not None)
    return pl.pallas_call(
        functools.partial(part_kernel, spec),
        out_shape=out_shape,
        in_specs=[pl.BlockSpec(memory_space=pltpu.SMEM)] + [vmem] * (len(given) - 1),
        out_specs=[vmem] * len(out_shape),
        scratch_shapes=[
            pltpu.VMEM(((empty + 1) * tile_size, width), BF16),
            pltpu.VMEM((rows, width), F32),
        ],
        compiler_params=pltpu.CompilerParams(vmem_limit_bytes=VMEM_BYTES),
        cost_estimate=pl.CostEstimate(
            flops=2 * share * tile_size * tile_size * width,
            bytes_accessed=2 * share * tile_size * tile_size,
            transcendentals=0,
        ),
    )(*given)


def grid_cycle(size):
    ny = 1
    while (2 * ny) ** 2 <= size:
        ny *= 2
    nz = size // ny
    walk = [0]
    for z in range(nz):
        ys = range(1, ny) if z % 2 == 0 else range(ny - 1, 0, -1)
        walk += [z * ny + y for y in ys]
    walk += [z * ny for z in range(nz - 1, 0, -1)]
    return walk


class Grid:
    def __init__(self, rows, cols):
        self.rows, self.cols, self.chips = rows, cols, rows // CORES
        self.walk = grid_cycle(cols)
        self.place_of = [self.walk.index(c) for c in range(cols)]
        self.row, self.col = lax.axis_index("row"), lax.axis_index("col")
        self.x, self.core = self.row // CORES, self.row % CORES
        place = sum(jnp.where(self.col == c, self.place_of[c], 0) for c in range(cols))
        self.ahead_of = [
            jnp.where(self.core == 0, self.place_of[c] - place, place - self.place_of[c]) % cols
            for c in range(cols)
        ]

    def along_walk(self, step):
        pairs = []
        for r in range(self.rows):
            walk = self.walk if r % CORES == 0 else self.walk[::-1]
            for k in range(self.cols):
                pairs.append((r * self.cols + walk[k], r * self.cols + walk[(k + step) % self.cols]))
        return pairs

    def along_x(self, step):
        return [
            (r * self.cols + c, ((r + step * CORES) % self.rows) * self.cols + c)
            for r in range(self.rows)
            for c in range(self.cols)
        ]

    def across(self, row_bit, col_bit):
        return [
            (r * self.cols + c, (r ^ row_bit) * self.cols + (c ^ col_bit))
            for r in range(self.rows)
            for c in range(self.cols)
        ]


def move(value, pairs):
    return lax.ppermute(value, ("row", "col"), pairs)


def after(value, *others):
    return lax.optimization_barrier((value, *others))[0]


def ring_hops(size):
    return (size - 1) // 2


def arrival_order(size):
    hops = ring_hops(size)
    groups = [[0]] + [[size - step, step] for step in range(1, hops + 1)]
    if size % 2 == 0:
        if hops:
            groups[min(2, hops)].append(size // 2)
        else:
            groups.append([size // 2])
    return groups


def ring_gather(own, size, pairs_of, hold):
    yield {0: own}
    ahead = behind = own
    for step, group in enumerate(arrival_order(size)[1:], 1):
        found = {}
        if step == 1:
            opposite = move(own, pairs_of(size // 2)) if size % 2 == 0 else None
        if step <= ring_hops(size):
            behind = move(after(behind, *hold.get(step, [])), pairs_of(1))
            ahead = move(ahead, pairs_of(-1))
            found = {size - step: behind, step: ahead}
        if size // 2 in group and size % 2 == 0:
            found[size // 2] = opposite
        yield found


def scatter_order(size):
    hops = ring_hops(size)
    groups = [[hop, size - hop] for hop in range(hops, 0, -1)] or [[]]
    if size % 2 == 0:
        groups[min(1, len(groups) - 1)].insert(0, size // 2)
    groups[-1].append(0)
    return groups


def ahead_bins(ahead, size):
    order = [k for group in scatter_order(size) for k in group]
    return sum(jnp.where(ahead == k, place, 0) for place, k in enumerate(order))


def ring_scatter(chunks_of, size, pairs_of):
    ahead = behind = opposite = None

    def onward(running, term):
        return term if running is None else (running.astype(F32) + term.astype(F32)).astype(BF16)

    for step, group in enumerate(scatter_order(size)):
        terms = dict(zip(group, chunks_of(step, ahead)))
        hop = ring_hops(size) - step
        if hop > 0:
            ahead = move(onward(ahead, terms[hop]), pairs_of(1))
            behind = move(onward(behind, terms[size - hop]), pairs_of(-1))
        if size // 2 in group and size % 2 == 0:
            opposite = move(terms[size // 2], pairs_of(size // 2))
    total = terms[0].astype(F32)
    for part in (opposite, ahead, behind):
        if part is not None:
            total = total + part.astype(F32)
    return total


def summed_everywhere(part, grid, gate):
    held = after(part.astype(BF16), *gate)
    got = move(held, grid.across(1, 0))
    yield None
    half = held.shape[0] // CORES
    chip = (held.astype(F32) + after(got, *gate).astype(F32)).astype(BF16)
    held = jnp.where(grid.core == 0, chip[:half], chip[half:])
    bits = [(1 << k, 0) for k in range(1, grid.rows.bit_length() - 1)]
    bits += [(0, 1 << k) for k in range(grid.cols.bit_length() - 1)]
    for row_bit, col_bit in bits:
        got = move(held, grid.across(row_bit, col_bit))
        yield None
        held = (held.astype(F32) + after(got, *gate).astype(F32)).astype(BF16)
    got = move(held, grid.across(1, 0))
    yield None
    own_first, own_last = jnp.concatenate([held, got]), jnp.concatenate([got, held])
    yield jnp.where(grid.core == 0, own_first, own_last).astype(F32)


def per_device(features, node_order, tile_vals, tile_coord, tile_count, weight, cotangent):
    nodes_here, feat_width = features.shape
    tile_size = tile_vals.shape[3]
    row_devices = lax.axis_size("row")
    col_devices = lax.axis_size("col")
    piece = nodes_here // tile_size
    block_cols = row_devices * piece
    block_rows = col_devices * piece
    grad_scale = float(nodes_here * row_devices * col_devices) ** (-0.5)
    grid = Grid(row_devices, col_devices)
    chips = grid.chips

    onehot = permuter(node_order, nodes_here)
    placed = reorder(onehot, features)
    tiles, token = load_tiles(tile_vals[0, 0])
    coord_here = tile_coord[0, 0]
    tile_total = tile_count[0, 0]

    def block_places(coord):
        row_of, col_of = coord // block_cols, coord % block_cols
        row_dev, col_dev = col_of // piece, row_of // piece
        far = (row_dev // CORES - grid.x) % chips
        swap = (row_dev % CORES - grid.core) % CORES
        ahead = sum(jnp.where(col_dev == c, grid.ahead_of[c], 0) for c in range(col_devices))
        return swap * chips + far, col_of % piece, ahead, row_of % piece

    row_place, col_piece, ahead, row_piece = block_places(coord_here)
    bins_out = ahead_bins(ahead, col_devices) * piece + row_piece
    source_out = row_place * piece + col_piece
    table_out = tile_table(bins_out, block_rows, source_out, tile_total, block_cols)

    along_x = {}
    for found in ring_gather(placed, chips, grid.along_x, {}):
        along_x.update(found)
    along_x = [along_x[k] for k in range(chips)]
    other_core = [move(along_x[0], grid.across(1, 0))]
    other_core += [
        move(jnp.where(token[0, 0] == 0, block, 0), grid.across(1, 0)) for block in along_x[1:]
    ]
    sources_out = along_x + other_core
    grads_in = reorder(onehot, cotangent)
    order = scatter_order(col_devices)
    edges = [sum(len(group) for group in order[:k]) * piece for k in range(len(order) + 1)]

    def chunks_of(step, arrived):
        table = table_out if step < 2 else after(table_out, earlier[step - 1])
        earlier.append(arrived)
        bins = (edges[step], edges[step + 1] - edges[step])
        return tile_part(
            False, table, bins, block_rows, tiles, sources_out, block_cols, pieces=nodes_here
        )

    earlier = []
    own_rows = ring_scatter(chunks_of, col_devices, grid.along_walk).astype(BF16)

    pre_act = jnp.dot(own_rows, weight, preferred_element_type=F32)
    own_act = elu_value(pre_act).astype(BF16)
    own_grad = (grads_in.astype(F32) * elu_slope(pre_act)).astype(BF16)
    own_agg_grad = lax.dot_general(
        own_grad, weight, (((1,), (1,)), ((), ())), preferred_element_type=F32
    ).astype(BF16)
    arrivals = arrival_order(col_devices)
    row_place, col_piece, ahead, row_piece = block_places(after(coord_here, *earlier[1:2]))
    part_of = sum(jnp.where(ahead == k, p, 0) for p, group in enumerate(arrivals) for k in group)
    block_at = sum(jnp.where(ahead == k, i, 0) for group in arrivals for i, k in enumerate(group))
    bins_back = len(arrivals) * block_cols
    empty_back = max(len(group) for group in arrivals) * piece
    table_back = tile_table(
        part_of * block_cols + row_place * piece + col_piece,
        bins_back,
        block_at * piece + row_piece,
        tile_total,
        empty_back,
    )
    weight_part = (
        lax.dot_general(own_rows, own_grad, (((0,), (0,)), ((), ())), preferred_element_type=F32)
        * grad_scale
    )
    acc, gate, hold, weight_grad = None, [], {}, None
    weight_steps = summed_everywhere(weight_part, grid, gate)
    weight_grad = next(weight_steps)
    for number, found in enumerate(ring_gather(own_agg_grad, col_devices, grid.along_walk, hold)):
        blocks = [found[k] for k in arrivals[number]]
        if number == len(arrivals) - 1:
            break
        bins = (number * block_cols, block_cols)
        (acc,) = tile_part(True, table_back, bins, bins_back, tiles, blocks, empty_back, acc=acc)
        hold[number + 2] = [acc]
        gate[:] = [found[number]] if number else [acc]
        weight_grad = next(weight_steps, weight_grad)
    gate[:] = blocks
    weight_grad = next(weight_steps, weight_grad)
    bins = ((len(arrivals) - 1) * block_cols, block_cols)
    mine, theirs = tile_part(
        True, table_back, bins, bins_back, tiles, blocks, empty_back, acc=acc, pieces=chips * nodes_here
    )
    got = move(theirs, grid.across(1, 0))
    both = mine.astype(F32) + got.astype(F32)
    sums = [both[k * nodes_here : (k + 1) * nodes_here] for k in range(chips)]
    sums = [sums[0]] + [term.astype(BF16) for term in sums[1:]]
    gate[:] = sums[1:]
    while weight_grad is None:
        weight_grad = next(weight_steps)
    order = scatter_order(chips)
    placed_grad = ring_scatter(
        lambda step, arrived: [sums[k] for k in order[step]], chips, grid.along_x
    ).astype(BF16)
    activations = restore(onehot, own_act)
    feature_grad = restore(onehot, placed_grad)
    return (activations, weight_grad, feature_grad)


def solution(mesh):
    in_specs = (
        P(("row", "col"), None),
        P(("row", "col")),
        P("row", "col", None, None, None),
        P("row", "col", None),
        P("row", "col"),
        P(),
        P(("row", "col"), None),
    )
    out_specs = (P(("row", "col"), None), P(), P(("row", "col"), None))
    return jax.shard_map(
        per_device, mesh=mesh, in_specs=in_specs, out_specs=out_specs, check_vma=False
    )
```

```python
import functools

import jax
import jax.numpy as jnp
from jax import lax
from jax.experimental import pallas as pl
from jax.experimental.pallas import tpu as pltpu
from jax.sharding import PartitionSpec as P

CORES = 2
GROUP = 4
UNROLL = 4
LANES = 128
PACK_BITS = 8
PACK = 1 << PACK_BITS
VMEM_BYTES = 16 * 1024 * 1024
LOAD_BYTES = 45 * 1024 * 1024
LOADS = 4
F32 = jnp.float32
BF16 = jnp.bfloat16


def elu_value(pre_act):
    return jnp.where(pre_act > 0, pre_act, jnp.expm1(jnp.minimum(pre_act, 0.0)))


def elu_slope(pre_act):
    return jnp.where(pre_act > 0, 1.0, jnp.exp(jnp.minimum(pre_act, 0.0)))


def permuter(node_order, nodes_here):
    local_pos = node_order % nodes_here
    return (local_pos[:, None] == jnp.arange(nodes_here, dtype=jnp.int32)[None, :]).astype(BF16)


def reorder(onehot, values):
    return jnp.dot(onehot, values, preferred_element_type=F32).astype(BF16)


def restore(onehot, values):
    moved = lax.dot_general(onehot, values, (((0,), (0,)), ((), ())), preferred_element_type=F32)
    return moved.astype(BF16)


def bits_of(size):
    return size.bit_length() - 1


def block_places(coord, here_ref, chips, cols, piece):
    block_cols = chips * CORES * piece
    row_of, col_of = coord >> bits_of(block_cols), coord & (block_cols - 1)
    row_dev, col_dev = col_of >> bits_of(piece), row_of >> bits_of(piece)
    far = ((row_dev >> bits_of(CORES)) - here_ref[cols]) & (chips - 1)
    swap = ((row_dev & (CORES - 1)) - here_ref[cols + 1]) & (CORES - 1)
    ahead = jnp.zeros_like(coord)
    for c in range(cols):
        ahead = jnp.where(col_dev == c, here_ref[c], ahead)
    return swap * chips + far, col_of & (piece - 1), ahead, row_of & (piece - 1)


def exact_dot(left, right, contract):
    return lax.dot_general(
        left.astype(F32).astype(BF16),
        right.astype(F32).astype(BF16),
        (contract, ((), ())),
        preferred_element_type=F32,
    )


def table_width(slot_total, bin_total):
    group_total = slot_total // GROUP + bin_total + 1
    return -(-max(group_total * GROUP, bin_total + 1) // LANES) * LANES


def write_table(out_ref, bins, bin_total, sources, slots, tile_total, empty):
    lanes = slots.shape[1]
    width = out_ref.shape[1]
    bin_rows = -(-bin_total // 8) * 8
    live = slots < tile_total
    of_bin = lax.broadcasted_iota(jnp.int32, (bin_rows, lanes), 0)
    mine = ((of_bin == bins) & live).astype(jnp.int32)
    earlier = lax.broadcasted_iota(jnp.int32, (lanes, lanes), 0) < lax.broadcasted_iota(
        jnp.int32, (lanes, lanes), 1
    )
    before = exact_dot(mine, earlier.astype(jnp.int32), ((1,), (0,)))
    counts = jnp.sum(mine.astype(F32), axis=1, keepdims=True)
    groups = (counts.astype(jnp.int32) + GROUP - 1) >> bits_of(GROUP)
    bin_at = lax.broadcasted_iota(jnp.int32, (bin_rows, width), 0)
    lane_at = lax.broadcasted_iota(jnp.int32, (bin_rows, width), 1)
    firsts = jnp.sum(jnp.where(bin_at < lane_at, groups, 0).astype(F32), axis=0, keepdims=True)
    here = lax.broadcasted_iota(jnp.int32, (bin_rows, bin_rows), 0)
    other = lax.broadcasted_iota(jnp.int32, (bin_rows, bin_rows), 1)
    firsts_of = exact_dot((other < here).astype(jnp.int32), groups, ((1,), (0,))).astype(jnp.int32)
    group_bin = jnp.sum((firsts_of + groups <= lane_at).astype(F32), axis=0, keepdims=True)
    place = jnp.sum(
        mine.astype(F32) * (before + (firsts_of * GROUP).astype(F32)), axis=0, keepdims=True
    ).astype(jnp.int32)
    place = jnp.where(live, place, -1)
    hit = (lax.broadcasted_iota(jnp.int32, (width, lanes), 0) == place).astype(jnp.int32)
    row = lax.broadcasted_iota(jnp.int32, (8, lanes), 0)
    facts = jnp.where(row == 0, slots, jnp.where(row == 1, sources, 1))
    found = exact_dot(facts, hit, ((1,), (1,))).astype(jnp.int32)
    members = jnp.where(found[2:3] > 0, found[0:1] * PACK + found[1:2], empty)
    rows = lax.broadcasted_iota(jnp.int32, (8, width), 0)
    out_ref[...] = jnp.where(
        rows == 0,
        members,
        jnp.where(rows == 1, group_bin.astype(jnp.int32), firsts.astype(jnp.int32)),
    )


def load_kernel(sizes, count_ref, here_ref, coord_ref, tiles_ref, out_ref, ahead_ref, back_ref, sems):
    chips, cols, piece = sizes
    slot_total = tiles_ref.shape[0]
    share = slot_total // LOADS
    copies = [
        pltpu.make_async_copy(
            tiles_ref.at[pl.ds(k * share, share)], out_ref.at[pl.ds(k * share, share)], sems.at[k]
        )
        for k in range(LOADS)
    ]
    for copy in copies:
        copy.start()
    coord = coord_ref[...]
    slots = lax.broadcasted_iota(jnp.int32, coord.shape, 1)
    tile_total = count_ref[0]
    row_place, col_piece, ahead, row_piece = block_places(coord, here_ref, chips, cols, piece)
    block_rows, block_cols = cols * piece, chips * CORES * piece

    order = [k for group in scatter_order(cols) for k in group]
    bins = jnp.zeros_like(coord)
    for place, k in enumerate(order):
        bins = jnp.where(ahead == k, place, bins)
    bins = bins * piece + row_piece
    write_table(
        ahead_ref, bins, block_rows, row_place * piece + col_piece, slots, tile_total, block_cols
    )

    arrivals = arrival_order(cols)
    part_of, block_at = jnp.zeros_like(coord), jnp.zeros_like(coord)
    for part, group in enumerate(arrivals):
        for at, k in enumerate(group):
            part_of = jnp.where(ahead == k, part, part_of)
            block_at = jnp.where(ahead == k, at, block_at)
    bins = part_of * block_cols + row_place * piece + col_piece
    write_table(
        back_ref,
        bins,
        len(arrivals) * block_cols,
        block_at * piece + row_piece,
        slots,
        tile_total,
        max(len(group) for group in arrivals) * piece,
    )
    for copy in copies:
        copy.wait()


def load_tiles(tiles, coord, count, here, sizes):
    chips, cols, piece = sizes
    slot_total = tiles.shape[0]
    lanes = -(-slot_total // LANES) * LANES
    bins_back = len(arrival_order(cols)) * chips * CORES * piece
    coord = jnp.pad(coord, (0, lanes - slot_total))[None, :]
    smem = pl.BlockSpec(memory_space=pltpu.SMEM)
    vmem = pl.BlockSpec(memory_space=pltpu.VMEM)
    return pl.pallas_call(
        functools.partial(load_kernel, sizes),
        out_shape=[
            jax.ShapeDtypeStruct(tiles.shape, tiles.dtype),
            jax.ShapeDtypeStruct((8, table_width(slot_total, cols * piece)), jnp.int32),
            jax.ShapeDtypeStruct((8, table_width(slot_total, bins_back)), jnp.int32),
        ],
        in_specs=[smem, smem, vmem, pl.BlockSpec(memory_space=pl.ANY)],
        out_specs=[vmem] * 3,
        scratch_shapes=[pltpu.SemaphoreType.DMA((LOADS,))],
        compiler_params=pltpu.CompilerParams(vmem_limit_bytes=LOAD_BYTES),
        cost_estimate=pl.CostEstimate(flops=0, bytes_accessed=2 * tiles.size, transcendentals=0),
    )(count, here, coord, tiles)


def part_kernel(spec, table_ref, tiles_ref, *refs):
    transposed, first_bin, bin_count, bin_total, source_count, carried, finish = spec
    source_refs = refs[:source_count]
    out_refs = refs[source_count + carried : -2]
    source, total = refs[-2:]
    slot_total, tile_size, _ = tiles_ref.shape
    group_total = slot_total // GROUP + bin_total + 1
    at = 0
    for ref in source_refs:
        source[at : at + ref.shape[0], :] = ref[...]
        at += ref.shape[0]
    source[at:, :] = jnp.zeros((source.shape[0] - at, source.shape[1]), source.dtype)
    total[...] = refs[source_count][...] if carried else jnp.zeros_like(total)
    begin = table_ref[2, first_bin]
    end = table_ref[2, first_bin + bin_count]
    contract = 0 if transposed else 1

    def step(number, carry):
        products = []
        for member in range(UNROLL):
            group = begin + number * UNROLL + member
            group = jnp.where(group < end, group, group_total - 1)
            left, right = [], []
            for k in range(GROUP):
                packed = table_ref[0, group * GROUP + k]
                left.append(tiles_ref[packed >> PACK_BITS])
                row = pl.multiple_of((packed & (PACK - 1)) * tile_size, tile_size)
                right.append(source[pl.ds(row, tile_size), :])
            product = lax.dot_general(
                jnp.concatenate(left, axis=contract),
                jnp.concatenate(right, axis=0),
                (((contract,), (0,)), ((), ())),
                preferred_element_type=F32,
            )
            products.append((jnp.minimum(table_ref[1, group] - first_bin, bin_count - 1), product))
        for place, product in products:
            rows = pl.ds(pl.multiple_of(place * tile_size, tile_size), tile_size)
            total[rows, :] += product
        return carry

    lax.fori_loop(0, (end - begin + UNROLL - 1) // UNROLL, step, 0)
    if finish:
        at = 0
        for ref in out_refs:
            ref[...] = total[at : at + ref.shape[0], :].astype(ref.dtype)
            at += ref.shape[0]
    else:
        out_refs[0][...] = total[...]


def tile_part(transposed, table, bins, bin_total, tiles, sources, empty, acc=None, pieces=None):
    first_bin, bin_count = bins
    slot_total, tile_size, _ = tiles.shape
    width = sources[0].shape[1]
    rows = bin_count * tile_size
    vmem = pl.BlockSpec(memory_space=pltpu.VMEM)
    if pieces is None:
        out_shape = [jax.ShapeDtypeStruct((rows, width), F32)]
    else:
        out_shape = [jax.ShapeDtypeStruct((pieces, width), BF16)] * (rows // pieces)
    carried = acc is not None
    share = slot_total * bin_count // bin_total
    given = [table, tiles, *sources] + ([] if acc is None else [acc])
    spec = (transposed, first_bin, bin_count, bin_total, len(sources), carried, pieces is not None)
    return pl.pallas_call(
        functools.partial(part_kernel, spec),
        out_shape=out_shape,
        in_specs=[pl.BlockSpec(memory_space=pltpu.SMEM)] + [vmem] * (len(given) - 1),
        out_specs=[vmem] * len(out_shape),
        scratch_shapes=[
            pltpu.VMEM(((empty + 1) * tile_size, width), BF16),
            pltpu.VMEM((rows, width), F32),
        ],
        compiler_params=pltpu.CompilerParams(vmem_limit_bytes=VMEM_BYTES),
        cost_estimate=pl.CostEstimate(
            flops=2 * share * tile_size * tile_size * width,
            bytes_accessed=2 * share * tile_size * tile_size,
            transcendentals=0,
        ),
    )(*given)


def grid_cycle(size):
    ny = 1
    while (2 * ny) ** 2 <= size:
        ny *= 2
    nz = size // ny
    walk = [0]
    for z in range(nz):
        ys = range(1, ny) if z % 2 == 0 else range(ny - 1, 0, -1)
        walk += [z * ny + y for y in ys]
    walk += [z * ny for z in range(nz - 1, 0, -1)]
    return walk


class Grid:
    def __init__(self, rows, cols):
        self.rows, self.cols, self.chips = rows, cols, rows // CORES
        self.walk = grid_cycle(cols)
        self.place_of = [self.walk.index(c) for c in range(cols)]
        self.row, self.col = lax.axis_index("row"), lax.axis_index("col")
        self.x, self.core = self.row // CORES, self.row % CORES
        place = sum(jnp.where(self.col == c, self.place_of[c], 0) for c in range(cols))
        self.ahead_of = [
            jnp.where(self.core == 0, self.place_of[c] - place, place - self.place_of[c]) % cols
            for c in range(cols)
        ]

    def along_walk(self, step):
        pairs = []
        for r in range(self.rows):
            walk = self.walk if r % CORES == 0 else self.walk[::-1]
            for k in range(self.cols):
                pairs.append((r * self.cols + walk[k], r * self.cols + walk[(k + step) % self.cols]))
        return pairs

    def along_x(self, step):
        return [
            (r * self.cols + c, ((r + step * CORES) % self.rows) * self.cols + c)
            for r in range(self.rows)
            for c in range(self.cols)
        ]

    def across(self, row_bit, col_bit):
        return [
            (r * self.cols + c, (r ^ row_bit) * self.cols + (c ^ col_bit))
            for r in range(self.rows)
            for c in range(self.cols)
        ]


def move(value, pairs):
    return lax.ppermute(value, ("row", "col"), pairs)


def after(value, *others):
    return lax.optimization_barrier((value, *others))[0]


def ring_hops(size):
    return (size - 1) // 2


def arrival_order(size):
    hops = ring_hops(size)
    groups = [[0]] + [[size - step, step] for step in range(1, hops + 1)]
    if size % 2 == 0:
        if hops:
            groups[1].append(size // 2)
        else:
            groups.append([size // 2])
    return groups


def ring_gather(own, size, pairs_of, hold):
    yield {0: own}
    ahead = behind = own
    for step, group in enumerate(arrival_order(size)[1:], 1):
        found = {}
        if step == 1:
            opposite = move(own, pairs_of(size // 2)) if size % 2 == 0 else None
        if step <= ring_hops(size):
            behind = move(after(behind, *hold.get(step, [])), pairs_of(1))
            ahead = move(ahead, pairs_of(-1))
            found = {size - step: behind, step: ahead}
        if size // 2 in group and size % 2 == 0:
            found[size // 2] = opposite
        yield found


def scatter_order(size):
    hops = ring_hops(size)
    groups = [[hop, size - hop] for hop in range(hops, 0, -1)] or [[]]
    if size % 2 == 0:
        groups[min(1, len(groups) - 1)].insert(0, size // 2)
    groups[-1].append(0)
    return groups


def ring_scatter(chunks_of, size, pairs_of):
    ahead = behind = opposite = None

    def onward(running, term):
        return term if running is None else (running.astype(F32) + term.astype(F32)).astype(BF16)

    for step, group in enumerate(scatter_order(size)):
        terms = dict(zip(group, chunks_of(step, ahead)))
        hop = ring_hops(size) - step
        if hop > 0:
            ahead = move(onward(ahead, terms[hop]), pairs_of(1))
            behind = move(onward(behind, terms[size - hop]), pairs_of(-1))
        if size // 2 in group and size % 2 == 0:
            opposite = move(terms[size // 2], pairs_of(size // 2))
    total = terms[0].astype(F32)
    for part in (opposite, ahead, behind):
        if part is not None:
            total = total + part.astype(F32)
    return total


def summed_everywhere(part, grid, gate):
    held = after(part.astype(BF16), *gate)
    got = move(held, grid.across(1, 0))
    yield None
    half = held.shape[0] // CORES
    chip = (held.astype(F32) + after(got, *gate).astype(F32)).astype(BF16)
    held = jnp.where(grid.core == 0, chip[:half], chip[half:])
    bits = [(0, 1 << k) for k in reversed(range(bits_of(grid.cols)))]
    bits += [(1 << k, 0) for k in range(1, bits_of(grid.rows))]
    for row_bit, col_bit in bits:
        got = move(held, grid.across(row_bit, col_bit))
        yield None
        held = (held.astype(F32) + after(got, *gate).astype(F32)).astype(BF16)
    got = move(held, grid.across(1, 0))
    yield None
    own_first, own_last = jnp.concatenate([held, got]), jnp.concatenate([got, held])
    yield jnp.where(grid.core == 0, own_first, own_last).astype(F32)


def per_device(features, node_order, tile_vals, tile_coord, tile_count, weight, cotangent):
    nodes_here, feat_width = features.shape
    tile_size = tile_vals.shape[3]
    row_devices = lax.axis_size("row")
    col_devices = lax.axis_size("col")
    piece = nodes_here // tile_size
    block_cols = row_devices * piece
    block_rows = col_devices * piece
    grad_scale = float(nodes_here * row_devices * col_devices) ** (-0.5)
    grid = Grid(row_devices, col_devices)
    chips = grid.chips

    onehot = permuter(node_order, nodes_here)
    placed = reorder(onehot, features)
    here = jnp.stack([*grid.ahead_of, grid.x, grid.core]).astype(jnp.int32)
    tiles, table_out, table_back = load_tiles(
        tile_vals[0, 0], tile_coord[0, 0], tile_count[0], here, (chips, col_devices, piece)
    )

    along_x = {}
    for found in ring_gather(placed, chips, grid.along_x, {}):
        along_x.update(found)
    along_x = [along_x[k] for k in range(chips)]
    other_core = [move(along_x[0], grid.across(1, 0))]
    other_core += [
        move(jnp.where(table_out[0, 0] < 0, 0, block), grid.across(1, 0)) for block in along_x[1:]
    ]
    sources_out = along_x + other_core
    grads_in = reorder(onehot, cotangent)
    order = scatter_order(col_devices)
    edges = [sum(len(group) for group in order[:k]) * piece for k in range(len(order) + 1)]

    def chunks_of(step, arrived):
        table = table_out if step < 2 else after(table_out, earlier[step - 1])
        earlier.append(arrived)
        bins = (edges[step], edges[step + 1] - edges[step])
        return tile_part(
            False, table, bins, block_rows, tiles, sources_out, block_cols, pieces=nodes_here
        )

    earlier = []
    own_rows = ring_scatter(chunks_of, col_devices, grid.along_walk).astype(BF16)

    pre_act = jnp.dot(own_rows, weight, preferred_element_type=F32)
    own_act = elu_value(pre_act).astype(BF16)
    own_grad = (grads_in.astype(F32) * elu_slope(pre_act)).astype(BF16)
    own_agg_grad = lax.dot_general(
        own_grad, weight, (((1,), (1,)), ((), ())), preferred_element_type=F32
    ).astype(BF16)
    activations = restore(onehot, own_act)

    arrivals = arrival_order(col_devices)
    bins_back = len(arrivals) * block_cols
    empty_back = max(len(group) for group in arrivals) * piece
    weight_part = (
        lax.dot_general(own_rows, own_grad, (((0,), (0,)), ((), ())), preferred_element_type=F32)
        * grad_scale
    )
    acc, gate, hold, weight_grad = None, [], {}, None
    weight_steps = summed_everywhere(weight_part, grid, gate)
    weight_grad = next(weight_steps)
    for number, found in enumerate(ring_gather(own_agg_grad, col_devices, grid.along_walk, hold)):
        blocks = [found[k] for k in arrivals[number]]
        if number == len(arrivals) - 1:
            break
        bins = (number * block_cols, block_cols)
        (acc,) = tile_part(True, table_back, bins, bins_back, tiles, blocks, empty_back, acc=acc)
        hold[number + 2] = [acc]
        gate[:] = [found[number]] if number else [acc]
        if number == 1:
            gate.append(activations)
        weight_grad = next(weight_steps, weight_grad)
    gate[:] = blocks
    weight_grad = next(weight_steps, weight_grad)
    bins = ((len(arrivals) - 1) * block_cols, block_cols)
    mine, theirs = tile_part(
        True, table_back, bins, bins_back, tiles, blocks, empty_back, acc=acc, pieces=chips * nodes_here
    )
    got = move(theirs, grid.across(1, 0))
    both = mine.astype(F32) + got.astype(F32)
    sums = [both[k * nodes_here : (k + 1) * nodes_here] for k in range(chips)]
    sums = [sums[0]] + [term.astype(BF16) for term in sums[1:]]
    gate[:] = sums[1:]
    while weight_grad is None:
        weight_grad = next(weight_steps)
    order = scatter_order(chips)
    placed_grad = ring_scatter(
        lambda step, arrived: [sums[k] for k in order[step]], chips, grid.along_x
    ).astype(BF16)
    feature_grad = restore(onehot, placed_grad)
    return (activations, weight_grad, feature_grad)


def solution(mesh):
    in_specs = (
        P(("row", "col"), None),
        P(("row", "col")),
        P("row", "col", None, None, None),
        P("row", "col", None),
        P("row", "col"),
        P(),
        P(("row", "col"), None),
    )
    out_specs = (P(("row", "col"), None), P(), P(("row", "col"), None))
    return jax.shard_map(
        per_device, mesh=mesh, in_specs=in_specs, out_specs=out_specs, check_vma=False
    )
```

```python
import functools

import jax
import jax.numpy as jnp
from jax import lax
from jax.experimental import pallas as pl
from jax.experimental.pallas import tpu as pltpu
from jax.sharding import PartitionSpec as P

CORES = 2
GROUP = 4
UNROLL = 4
LANES = 128
PACK_BITS = 8
PACK = 1 << PACK_BITS
VMEM_BYTES = 16 * 1024 * 1024
LOAD_BYTES = 45 * 1024 * 1024
LOADS = 4
F32 = jnp.float32
BF16 = jnp.bfloat16


def elu_value(pre_act):
    return jnp.where(pre_act > 0, pre_act, jnp.expm1(jnp.minimum(pre_act, 0.0)))


def elu_slope(pre_act):
    return jnp.where(pre_act > 0, 1.0, jnp.exp(jnp.minimum(pre_act, 0.0)))


def row_moves(node_order, first_node, nodes_here):
    own = first_node + jnp.arange(nodes_here, dtype=jnp.int32)
    return (node_order[:, None] == own[None, :]).astype(BF16)


def reorder(moves, values):
    return jnp.dot(moves, values, preferred_element_type=F32).astype(BF16)


def restore(moves, values):
    moved = lax.dot_general(moves, values, (((0,), (0,)), ((), ())), preferred_element_type=F32)
    return moved.astype(BF16)


def bits_of(size):
    return size.bit_length() - 1


def block_places(coord, here_ref, chips, cols, piece):
    block_cols = chips * CORES * piece
    row_of, col_of = coord >> bits_of(block_cols), coord & (block_cols - 1)
    row_dev, col_dev = col_of >> bits_of(piece), row_of >> bits_of(piece)
    far = ((row_dev >> bits_of(CORES)) - here_ref[cols]) & (chips - 1)
    swap = ((row_dev & (CORES - 1)) - here_ref[cols + 1]) & (CORES - 1)
    ahead = jnp.zeros_like(coord)
    for c in range(cols):
        ahead = jnp.where(col_dev == c, here_ref[c], ahead)
    return swap * chips + far, col_of & (piece - 1), ahead, row_of & (piece - 1)


def exact_dot(left, right, contract):
    return lax.dot_general(
        left.astype(F32).astype(BF16),
        right.astype(F32).astype(BF16),
        (contract, ((), ())),
        preferred_element_type=F32,
    )


def table_width(slot_total, bin_total):
    group_total = slot_total // GROUP + bin_total + 1
    return -(-max(group_total * GROUP, bin_total + 1) // LANES) * LANES


def write_table(out_ref, bins, bin_total, sources, slots, tile_total, empty):
    lanes = slots.shape[1]
    width = out_ref.shape[1]
    bin_rows = -(-bin_total // 8) * 8
    live = slots < tile_total
    of_bin = lax.broadcasted_iota(jnp.int32, (bin_rows, lanes), 0)
    mine = ((of_bin == bins) & live).astype(jnp.int32)
    earlier = lax.broadcasted_iota(jnp.int32, (lanes, lanes), 0) < lax.broadcasted_iota(
        jnp.int32, (lanes, lanes), 1
    )
    before = exact_dot(mine, earlier.astype(jnp.int32), ((1,), (0,)))
    counts = jnp.sum(mine.astype(F32), axis=1, keepdims=True)
    groups = (counts.astype(jnp.int32) + GROUP - 1) >> bits_of(GROUP)
    bin_at = lax.broadcasted_iota(jnp.int32, (bin_rows, width), 0)
    lane_at = lax.broadcasted_iota(jnp.int32, (bin_rows, width), 1)
    firsts = jnp.sum(jnp.where(bin_at < lane_at, groups, 0).astype(F32), axis=0, keepdims=True)
    here = lax.broadcasted_iota(jnp.int32, (bin_rows, bin_rows), 0)
    other = lax.broadcasted_iota(jnp.int32, (bin_rows, bin_rows), 1)
    firsts_of = exact_dot((other < here).astype(jnp.int32), groups, ((1,), (0,))).astype(jnp.int32)
    group_bin = jnp.sum((firsts_of + groups <= lane_at).astype(F32), axis=0, keepdims=True)
    place = jnp.sum(
        mine.astype(F32) * (before + (firsts_of * GROUP).astype(F32)), axis=0, keepdims=True
    ).astype(jnp.int32)
    place = jnp.where(live, place, -1)
    hit = (lax.broadcasted_iota(jnp.int32, (width, lanes), 0) == place).astype(jnp.int32)
    row = lax.broadcasted_iota(jnp.int32, (8, lanes), 0)
    facts = jnp.where(row == 0, slots, jnp.where(row == 1, sources, 1))
    found = exact_dot(facts, hit, ((1,), (1,))).astype(jnp.int32)
    members = jnp.where(found[2:3] > 0, found[0:1] * PACK + found[1:2], empty)
    rows = lax.broadcasted_iota(jnp.int32, (8, width), 0)
    out_ref[...] = jnp.where(
        rows == 0,
        members,
        jnp.where(rows == 1, group_bin.astype(jnp.int32), firsts.astype(jnp.int32)),
    )


def load_kernel(sizes, here_ref, facts_ref, tiles_ref, out_ref, ahead_ref, back_ref, gate_ref, sems):
    chips, cols, piece = sizes
    slot_total = tiles_ref.shape[0]
    share = slot_total // LOADS
    copies = [
        pltpu.make_async_copy(
            tiles_ref.at[pl.ds(k * share, share)], out_ref.at[pl.ds(k * share, share)], sems.at[k]
        )
        for k in range(LOADS)
    ]
    for copy in copies:
        copy.start()
    gate_ref[...] = jnp.zeros_like(gate_ref)
    coord = facts_ref[0:1, :]
    slots = lax.broadcasted_iota(jnp.int32, coord.shape, 1)
    tile_total = facts_ref[1:2, 0:1]
    row_place, col_piece, ahead, row_piece = block_places(coord, here_ref, chips, cols, piece)
    block_rows, block_cols = cols * piece, chips * CORES * piece

    order = [k for group in scatter_order(cols) for k in group]
    bins = jnp.zeros_like(coord)
    for place, k in enumerate(order):
        bins = jnp.where(ahead == k, place, bins)
    bins = bins * piece + row_piece
    write_table(
        ahead_ref, bins, block_rows, row_place * piece + col_piece, slots, tile_total, block_cols
    )

    arrivals = arrival_order(cols)
    part_of, block_at = jnp.zeros_like(coord), jnp.zeros_like(coord)
    for part, group in enumerate(arrivals):
        for at, k in enumerate(group):
            part_of = jnp.where(ahead == k, part, part_of)
            block_at = jnp.where(ahead == k, at, block_at)
    bins = part_of * block_cols + row_place * piece + col_piece
    write_table(
        back_ref,
        bins,
        len(arrivals) * block_cols,
        block_at * piece + row_piece,
        slots,
        tile_total,
        max(len(group) for group in arrivals) * piece,
    )
    for copy in copies:
        copy.wait()


def load_tiles(tiles, coord, count, here, sizes, gate_shape):
    chips, cols, piece = sizes
    slot_total = tiles.shape[0]
    bins_back = len(arrival_order(cols)) * chips * CORES * piece
    lanes = -(-slot_total // LANES) * LANES
    facts = jnp.concatenate([jnp.pad(row, ((0, 0), (0, lanes - row.shape[1]))) for row in (coord, count)])
    vmem = pl.BlockSpec(memory_space=pltpu.VMEM)
    return pl.pallas_call(
        functools.partial(load_kernel, sizes),
        out_shape=[
            jax.ShapeDtypeStruct(tiles.shape, tiles.dtype),
            jax.ShapeDtypeStruct((8, table_width(slot_total, cols * piece)), jnp.int32),
            jax.ShapeDtypeStruct((8, table_width(slot_total, bins_back)), jnp.int32),
            jax.ShapeDtypeStruct(gate_shape, BF16),
        ],
        in_specs=[pl.BlockSpec(memory_space=pltpu.SMEM), vmem, pl.BlockSpec(memory_space=pl.ANY)],
        out_specs=[vmem] * 4,
        scratch_shapes=[pltpu.SemaphoreType.DMA((LOADS,))],
        compiler_params=pltpu.CompilerParams(vmem_limit_bytes=LOAD_BYTES),
        cost_estimate=pl.CostEstimate(flops=0, bytes_accessed=2 * tiles.size, transcendentals=0),
    )(here, facts, tiles)


def part_kernel(spec, table_ref, tiles_ref, *refs):
    transposed, first_bin, bin_count, bin_total, source_count, carried, finish = spec
    source_refs = refs[:source_count]
    out_refs = refs[source_count + carried : -2]
    source, total = refs[-2:]
    slot_total, tile_size, _ = tiles_ref.shape
    group_total = slot_total // GROUP + bin_total + 1
    at = 0
    for ref in source_refs:
        source[at : at + ref.shape[0], :] = ref[...]
        at += ref.shape[0]
    source[at:, :] = jnp.zeros((source.shape[0] - at, source.shape[1]), source.dtype)
    total[...] = refs[source_count][...] if carried else jnp.zeros_like(total)
    begin = table_ref[2, first_bin]
    end = table_ref[2, first_bin + bin_count]
    contract = 0 if transposed else 1

    def step(number, carry):
        products = []
        for member in range(UNROLL):
            group = begin + number * UNROLL + member
            group = jnp.where(group < end, group, group_total - 1)
            left, right = [], []
            for k in range(GROUP):
                packed = table_ref[0, group * GROUP + k]
                left.append(tiles_ref[packed >> PACK_BITS])
                row = pl.multiple_of((packed & (PACK - 1)) * tile_size, tile_size)
                right.append(source[pl.ds(row, tile_size), :])
            product = lax.dot_general(
                jnp.concatenate(left, axis=contract),
                jnp.concatenate(right, axis=0),
                (((contract,), (0,)), ((), ())),
                preferred_element_type=F32,
            )
            products.append((jnp.minimum(table_ref[1, group] - first_bin, bin_count - 1), product))
        for place, product in products:
            rows = pl.ds(pl.multiple_of(place * tile_size, tile_size), tile_size)
            total[rows, :] += product
        return carry

    lax.fori_loop(0, (end - begin + UNROLL - 1) // UNROLL, step, 0)
    if finish:
        at = 0
        for ref in out_refs:
            ref[...] = total[at : at + ref.shape[0], :].astype(ref.dtype)
            at += ref.shape[0]
    else:
        out_refs[0][...] = total[...]


def tile_part(transposed, table, bins, bin_total, tiles, sources, empty, acc=None, pieces=None):
    first_bin, bin_count = bins
    slot_total, tile_size, _ = tiles.shape
    width = sources[0].shape[1]
    rows = bin_count * tile_size
    vmem = pl.BlockSpec(memory_space=pltpu.VMEM)
    if pieces is None:
        out_shape = [jax.ShapeDtypeStruct((rows, width), F32)]
    else:
        out_shape = [jax.ShapeDtypeStruct((pieces, width), BF16)] * (rows // pieces)
    carried = acc is not None
    share = slot_total * bin_count // bin_total
    given = [table, tiles, *sources] + ([] if acc is None else [acc])
    spec = (transposed, first_bin, bin_count, bin_total, len(sources), carried, pieces is not None)
    return pl.pallas_call(
        functools.partial(part_kernel, spec),
        out_shape=out_shape,
        in_specs=[pl.BlockSpec(memory_space=pltpu.SMEM)] + [vmem] * (len(given) - 1),
        out_specs=[vmem] * len(out_shape),
        scratch_shapes=[
            pltpu.VMEM(((empty + 1) * tile_size, width), BF16),
            pltpu.VMEM((rows, width), F32),
        ],
        compiler_params=pltpu.CompilerParams(vmem_limit_bytes=VMEM_BYTES),
        cost_estimate=pl.CostEstimate(
            flops=2 * share * tile_size * tile_size * width,
            bytes_accessed=2 * share * tile_size * tile_size,
            transcendentals=0,
        ),
    )(*given)


def grid_cycle(size):
    ny = 1
    while (2 * ny) ** 2 <= size:
        ny *= 2
    nz = size // ny
    walk = [0]
    for z in range(nz):
        ys = range(1, ny) if z % 2 == 0 else range(ny - 1, 0, -1)
        walk += [z * ny + y for y in ys]
    walk += [z * ny for z in range(nz - 1, 0, -1)]
    return walk


class Grid:
    def __init__(self, rows, cols):
        self.rows, self.cols, self.chips = rows, cols, rows // CORES
        self.walk = grid_cycle(cols)
        self.place_of = [self.walk.index(c) for c in range(cols)]
        self.row, self.col = lax.axis_index("row"), lax.axis_index("col")
        self.x, self.core = self.row // CORES, self.row % CORES
        place = sum(jnp.where(self.col == c, self.place_of[c], 0) for c in range(cols))
        self.ahead_of = [
            jnp.where(self.core == 0, self.place_of[c] - place, place - self.place_of[c]) % cols
            for c in range(cols)
        ]

    def along_walk(self, step):
        pairs = []
        for r in range(self.rows):
            walk = self.walk if r % CORES == 0 else self.walk[::-1]
            for k in range(self.cols):
                pairs.append((r * self.cols + walk[k], r * self.cols + walk[(k + step) % self.cols]))
        return pairs

    def along_x(self, step):
        return [
            (r * self.cols + c, ((r + step * CORES) % self.rows) * self.cols + c)
            for r in range(self.rows)
            for c in range(self.cols)
        ]

    def across(self, row_bit, col_bit):
        return [
            (r * self.cols + c, (r ^ row_bit) * self.cols + (c ^ col_bit))
            for r in range(self.rows)
            for c in range(self.cols)
        ]


def move(value, pairs):
    return lax.ppermute(value, ("row", "col"), pairs)


def after(value, *others):
    return lax.optimization_barrier((value, *others))[0]


def ring_hops(size):
    return (size - 1) // 2


def arrival_order(size):
    hops = ring_hops(size)
    groups = [[0]] + [[size - step, step] for step in range(1, hops + 1)]
    if size % 2 == 0:
        if hops:
            groups[min(2, hops)].append(size // 2)
        else:
            groups.append([size // 2])
    return groups


def ring_gather(own, size, pairs_of, hold):
    yield {0: own}
    ahead = behind = own
    for step, group in enumerate(arrival_order(size)[1:], 1):
        found = {}
        if step == 1:
            opposite = move(own, pairs_of(size // 2)) if size % 2 == 0 else None
        if step <= ring_hops(size):
            behind = move(after(behind, *hold.get(step, [])), pairs_of(1))
            ahead = move(ahead, pairs_of(-1))
            found = {size - step: behind, step: ahead}
        if size // 2 in group and size % 2 == 0:
            found[size // 2] = opposite
        yield found


def scatter_order(size):
    hops = ring_hops(size)
    groups = [[hop, size - hop] for hop in range(hops, 0, -1)] or [[]]
    if size % 2 == 0:
        groups[min(1, len(groups) - 1)].insert(0, size // 2)
    groups[-1].append(0)
    return groups


def ring_scatter(chunks_of, size, pairs_of):
    ahead = behind = opposite = None

    def onward(running, term):
        return term if running is None else (running.astype(F32) + term.astype(F32)).astype(BF16)

    for step, group in enumerate(scatter_order(size)):
        terms = dict(zip(group, chunks_of(step, ahead)))
        hop = ring_hops(size) - step
        if hop > 0:
            ahead = move(onward(ahead, terms[hop]), pairs_of(1))
            behind = move(onward(behind, terms[size - hop]), pairs_of(-1))
        if size // 2 in group and size % 2 == 0:
            opposite = move(terms[size // 2], pairs_of(size // 2))
    total = terms[0].astype(F32)
    for part in (opposite, ahead, behind):
        if part is not None:
            total = total + part.astype(F32)
    return total


def summed_everywhere(part, grid, gate):
    held = after(part.astype(BF16), *gate)
    got = move(held, grid.across(1, 0))
    yield None
    half = held.shape[0] // CORES
    chip = (held.astype(F32) + after(got, *gate).astype(F32)).astype(BF16)
    held = jnp.where(grid.core == 0, chip[:half], chip[half:])
    bits = [(0, 1 << k) for k in reversed(range(bits_of(grid.cols)))]
    bits += [(1 << k, 0) for k in range(1, bits_of(grid.rows))]
    for row_bit, col_bit in bits:
        got = move(held, grid.across(row_bit, col_bit))
        yield None
        held = (held.astype(F32) + after(got, *gate).astype(F32)).astype(BF16)
    got = move(held, grid.across(1, 0))
    yield None
    own_first, own_last = jnp.concatenate([held, got]), jnp.concatenate([got, held])
    yield jnp.where(grid.core == 0, own_first, own_last).astype(F32)


def per_device(features, node_order, tile_vals, tile_coord, tile_count, weight, cotangent):
    nodes_here, feat_width = features.shape
    tile_size = tile_vals.shape[3]
    row_devices = lax.axis_size("row")
    col_devices = lax.axis_size("col")
    piece = nodes_here // tile_size
    block_cols = row_devices * piece
    block_rows = col_devices * piece
    grad_scale = float(nodes_here * row_devices * col_devices) ** (-0.5)
    grid = Grid(row_devices, col_devices)
    chips = grid.chips

    first_node = (grid.row * col_devices + grid.col) * nodes_here
    moves = row_moves(node_order, first_node, nodes_here)
    placed = reorder(moves, features)
    here = jnp.stack([*grid.ahead_of, grid.x, grid.core]).astype(jnp.int32)
    tiles, table_out, table_back, loaded = load_tiles(
        tile_vals[0, 0], tile_coord[0], tile_count, here, (chips, col_devices, piece), placed.shape
    )

    along_x = {}
    for found in ring_gather(placed, chips, grid.along_x, {}):
        along_x.update(found)
    along_x = [along_x[k] for k in range(chips)]
    other_core = [move(along_x[0], grid.across(1, 0))]
    other_core += [
        move(jnp.where(loaded == 0, block, 0), grid.across(1, 0)) for block in along_x[1:]
    ]
    sources_out = along_x + other_core
    grads_in = reorder(moves, cotangent)
    order = scatter_order(col_devices)
    edges = [sum(len(group) for group in order[:k]) * piece for k in range(len(order) + 1)]

    def chunks_of(step, arrived):
        table = table_out if step < 2 else after(table_out, earlier[step - 1])
        earlier.append(arrived)
        bins = (edges[step], edges[step + 1] - edges[step])
        return tile_part(
            False, table, bins, block_rows, tiles, sources_out, block_cols, pieces=nodes_here
        )

    earlier = []
    own_rows = ring_scatter(chunks_of, col_devices, grid.along_walk).astype(BF16)

    pre_act = jnp.dot(own_rows, weight, preferred_element_type=F32)
    own_act = elu_value(pre_act).astype(BF16)
    own_grad = (grads_in.astype(F32) * elu_slope(pre_act)).astype(BF16)
    own_agg_grad = lax.dot_general(
        own_grad, weight, (((1,), (1,)), ((), ())), preferred_element_type=F32
    ).astype(BF16)
    arrivals = arrival_order(col_devices)
    bins_back = len(arrivals) * block_cols
    empty_back = max(len(group) for group in arrivals) * piece
    weight_part = (
        lax.dot_general(own_rows, own_grad, (((0,), (0,)), ((), ())), preferred_element_type=F32)
        * grad_scale
    )
    acc, gate, hold, weight_grad = None, [], {}, None
    weight_steps = summed_everywhere(weight_part, grid, gate)
    weight_grad = next(weight_steps)
    for number, found in enumerate(ring_gather(own_agg_grad, col_devices, grid.along_walk, hold)):
        blocks = [found[k] for k in arrivals[number]]
        if number == len(arrivals) - 1:
            break
        bins = (number * block_cols, block_cols)
        (acc,) = tile_part(True, table_back, bins, bins_back, tiles, blocks, empty_back, acc=acc)
        hold[number + 2] = [acc]
        gate[:] = [found[number]] if number else [acc]
        weight_grad = next(weight_steps, weight_grad)
    gate[:] = blocks
    weight_grad = next(weight_steps, weight_grad)
    bins = ((len(arrivals) - 1) * block_cols, block_cols)
    mine, theirs = tile_part(
        True, table_back, bins, bins_back, tiles, blocks, empty_back, acc=acc, pieces=chips * nodes_here
    )
    got = move(theirs, grid.across(1, 0))
    both = mine.astype(F32) + got.astype(F32)
    sums = [both[k * nodes_here : (k + 1) * nodes_here] for k in range(chips)]
    sums = [sums[0]] + [term.astype(BF16) for term in sums[1:]]
    gate[:] = sums[1:]
    while weight_grad is None:
        weight_grad = next(weight_steps)
    order = scatter_order(chips)
    placed_grad = ring_scatter(
        lambda step, arrived: [sums[k] for k in order[step]], chips, grid.along_x
    ).astype(BF16)
    activations = restore(moves, own_act)
    feature_grad = restore(moves, placed_grad)
    return (activations, weight_grad, feature_grad)


def solution(mesh):
    in_specs = (
        P(("row", "col"), None),
        P(("row", "col")),
        P("row", "col", None, None, None),
        P("row", "col", None),
        P("row", "col"),
        P(),
        P(("row", "col"), None),
    )
    out_specs = (P(("row", "col"), None), P(), P(("row", "col"), None))
    return jax.shard_map(
        per_device, mesh=mesh, in_specs=in_specs, out_specs=out_specs, check_vma=False
    )
```

```python
import functools

import jax
import jax.numpy as jnp
from jax import lax
from jax.experimental import pallas as pl
from jax.experimental.pallas import tpu as pltpu
from jax.sharding import PartitionSpec as P

CORES = 2
GROUP = 4
UNROLL = 8
LANES = 128
PACK_BITS = 8
PACK = 1 << PACK_BITS
VMEM_BYTES = 16 * 1024 * 1024
LOAD_BYTES = 45 * 1024 * 1024
LOADS = 16
F32 = jnp.float32
BF16 = jnp.bfloat16


def elu_value(pre_act):
    return jnp.where(pre_act > 0, pre_act, jnp.expm1(jnp.minimum(pre_act, 0.0)))


def elu_slope(pre_act):
    return jnp.where(pre_act > 0, 1.0, jnp.exp(jnp.minimum(pre_act, 0.0)))


def row_moves(node_order, first_node, nodes_here):
    own = first_node + jnp.arange(nodes_here, dtype=jnp.int32)
    return (node_order[:, None] == own[None, :]).astype(BF16)


def reorder(moves, values):
    return jnp.dot(moves, values, preferred_element_type=F32).astype(BF16)


def restore(moves, values):
    moved = lax.dot_general(moves, values, (((0,), (0,)), ((), ())), preferred_element_type=F32)
    return moved.astype(BF16)


def bits_of(size):
    return size.bit_length() - 1


def block_places(coord, here_ref, chips, cols, piece):
    block_cols = chips * CORES * piece
    row_of, col_of = coord >> bits_of(block_cols), coord & (block_cols - 1)
    row_dev, col_dev = col_of >> bits_of(piece), row_of >> bits_of(piece)
    far = ((row_dev >> bits_of(CORES)) - here_ref[cols]) & (chips - 1)
    swap = ((row_dev & (CORES - 1)) - here_ref[cols + 1]) & (CORES - 1)
    ahead = jnp.zeros_like(coord)
    for c in range(cols):
        ahead = jnp.where(col_dev == c, here_ref[c], ahead)
    return swap * chips + far, col_of & (piece - 1), ahead, row_of & (piece - 1)


def exact_dot(left, right, contract):
    return lax.dot_general(
        left.astype(F32).astype(BF16),
        right.astype(F32).astype(BF16),
        (contract, ((), ())),
        preferred_element_type=F32,
    )


def table_width(slot_total, bin_total):
    group_total = slot_total // GROUP + bin_total + 1
    return -(-max(group_total * GROUP, bin_total + 1) // LANES) * LANES


def write_table(out_ref, bins, bin_total, sources, slots, tile_total, empty):
    lanes = slots.shape[1]
    width = out_ref.shape[1]
    bin_rows = -(-bin_total // 8) * 8
    live = slots < tile_total
    of_bin = lax.broadcasted_iota(jnp.int32, (bin_rows, lanes), 0)
    mine = ((of_bin == bins) & live).astype(jnp.int32)
    earlier = lax.broadcasted_iota(jnp.int32, (lanes, lanes), 0) < lax.broadcasted_iota(
        jnp.int32, (lanes, lanes), 1
    )
    before = exact_dot(mine, earlier.astype(jnp.int32), ((1,), (0,)))
    counts = jnp.sum(mine.astype(F32), axis=1, keepdims=True)
    groups = (counts.astype(jnp.int32) + GROUP - 1) >> bits_of(GROUP)
    bin_at = lax.broadcasted_iota(jnp.int32, (bin_rows, width), 0)
    lane_at = lax.broadcasted_iota(jnp.int32, (bin_rows, width), 1)
    firsts = jnp.sum(jnp.where(bin_at < lane_at, groups, 0).astype(F32), axis=0, keepdims=True)
    here = lax.broadcasted_iota(jnp.int32, (bin_rows, bin_rows), 0)
    other = lax.broadcasted_iota(jnp.int32, (bin_rows, bin_rows), 1)
    firsts_of = exact_dot((other < here).astype(jnp.int32), groups, ((1,), (0,))).astype(jnp.int32)
    group_bin = jnp.sum((firsts_of + groups <= lane_at).astype(F32), axis=0, keepdims=True)
    place = jnp.sum(
        mine.astype(F32) * (before + (firsts_of * GROUP).astype(F32)), axis=0, keepdims=True
    ).astype(jnp.int32)
    place = jnp.where(live, place, -1)
    hit = (lax.broadcasted_iota(jnp.int32, (width, lanes), 0) == place).astype(jnp.int32)
    row = lax.broadcasted_iota(jnp.int32, (8, lanes), 0)
    facts = jnp.where(row == 0, slots, jnp.where(row == 1, sources, 1))
    found = exact_dot(facts, hit, ((1,), (1,))).astype(jnp.int32)
    members = jnp.where(found[2:3] > 0, found[0:1] * PACK + found[1:2], empty)
    rows = lax.broadcasted_iota(jnp.int32, (8, width), 0)
    out_ref[...] = jnp.where(
        rows == 0,
        members,
        jnp.where(rows == 1, group_bin.astype(jnp.int32), firsts.astype(jnp.int32)),
    )


def load_kernel(sizes, here_ref, facts_ref, tiles_ref, out_ref, ahead_ref, back_ref, gate_ref, sems):
    chips, cols, piece = sizes
    slot_total = tiles_ref.shape[0]
    share = slot_total // LOADS
    copies = [
        pltpu.make_async_copy(
            tiles_ref.at[pl.ds(k * share, share)], out_ref.at[pl.ds(k * share, share)], sems.at[k]
        )
        for k in range(LOADS)
    ]
    for copy in copies:
        copy.start()
    gate_ref[...] = jnp.zeros_like(gate_ref)
    coord = facts_ref[0:1, :]
    slots = lax.broadcasted_iota(jnp.int32, coord.shape, 1)
    tile_total = facts_ref[1:2, 0:1]
    row_place, col_piece, ahead, row_piece = block_places(coord, here_ref, chips, cols, piece)
    block_rows, block_cols = cols * piece, chips * CORES * piece

    order = [k for group in scatter_order(cols) for k in group]
    bins = jnp.zeros_like(coord)
    for place, k in enumerate(order):
        bins = jnp.where(ahead == k, place, bins)
    bins = bins * piece + row_piece
    write_table(
        ahead_ref, bins, block_rows, row_place * piece + col_piece, slots, tile_total, block_cols
    )

    arrivals = arrival_order(cols)
    part_of, block_at = jnp.zeros_like(coord), jnp.zeros_like(coord)
    for part, group in enumerate(arrivals):
        for at, k in enumerate(group):
            part_of = jnp.where(ahead == k, part, part_of)
            block_at = jnp.where(ahead == k, at, block_at)
    bins = part_of * block_cols + row_place * piece + col_piece
    write_table(
        back_ref,
        bins,
        len(arrivals) * block_cols,
        block_at * piece + row_piece,
        slots,
        tile_total,
        max(len(group) for group in arrivals) * piece,
    )
    for copy in copies:
        copy.wait()


def load_tiles(tiles, coord, count, here, sizes, gate_shape):
    chips, cols, piece = sizes
    slot_total = tiles.shape[0]
    bins_back = len(arrival_order(cols)) * chips * CORES * piece
    lanes = -(-slot_total // LANES) * LANES
    facts = jnp.concatenate([jnp.pad(row, ((0, 0), (0, lanes - row.shape[1]))) for row in (coord, count)])
    vmem = pl.BlockSpec(memory_space=pltpu.VMEM)
    return pl.pallas_call(
        functools.partial(load_kernel, sizes),
        out_shape=[
            jax.ShapeDtypeStruct(tiles.shape, tiles.dtype),
            jax.ShapeDtypeStruct((8, table_width(slot_total, cols * piece)), jnp.int32),
            jax.ShapeDtypeStruct((8, table_width(slot_total, bins_back)), jnp.int32),
            jax.ShapeDtypeStruct(gate_shape, BF16),
        ],
        in_specs=[pl.BlockSpec(memory_space=pltpu.SMEM), vmem, pl.BlockSpec(memory_space=pl.ANY)],
        out_specs=[vmem] * 4,
        scratch_shapes=[pltpu.SemaphoreType.DMA((LOADS,))],
        compiler_params=pltpu.CompilerParams(vmem_limit_bytes=LOAD_BYTES),
        cost_estimate=pl.CostEstimate(flops=0, bytes_accessed=2 * tiles.size, transcendentals=0),
    )(here, facts, tiles)


def part_kernel(spec, table_ref, tiles_ref, *refs):
    transposed, first_bin, bin_count, bin_total, source_count, carried, finish = spec
    source_refs = refs[:source_count]
    out_refs = refs[source_count + carried : -2]
    source, total = refs[-2:]
    slot_total, tile_size, _ = tiles_ref.shape
    group_total = slot_total // GROUP + bin_total + 1
    at = 0
    for ref in source_refs:
        source[at : at + ref.shape[0], :] = ref[...]
        at += ref.shape[0]
    source[at:, :] = jnp.zeros((source.shape[0] - at, source.shape[1]), source.dtype)
    total[...] = refs[source_count][...] if carried else jnp.zeros_like(total)
    begin = table_ref[2, first_bin]
    end = table_ref[2, first_bin + bin_count]
    contract = 0 if transposed else 1

    def step(number, carry):
        products = []
        for member in range(UNROLL):
            group = begin + number * UNROLL + member
            group = jnp.where(group < end, group, group_total - 1)
            left, right = [], []
            for k in range(GROUP):
                packed = table_ref[0, group * GROUP + k]
                left.append(tiles_ref[packed >> PACK_BITS])
                row = pl.multiple_of((packed & (PACK - 1)) * tile_size, tile_size)
                right.append(source[pl.ds(row, tile_size), :])
            product = lax.dot_general(
                jnp.concatenate(left, axis=contract),
                jnp.concatenate(right, axis=0),
                (((contract,), (0,)), ((), ())),
                preferred_element_type=F32,
            )
            products.append((jnp.minimum(table_ref[1, group] - first_bin, bin_count - 1), product))
        for place, product in products:
            rows = pl.ds(pl.multiple_of(place * tile_size, tile_size), tile_size)
            total[rows, :] += product
        return carry

    lax.fori_loop(0, (end - begin + UNROLL - 1) // UNROLL, step, 0)
    if finish:
        at = 0
        for ref in out_refs:
            ref[...] = total[at : at + ref.shape[0], :].astype(ref.dtype)
            at += ref.shape[0]
    else:
        out_refs[0][...] = total[...]


def tile_part(transposed, table, bins, bin_total, tiles, sources, empty, acc=None, pieces=None):
    first_bin, bin_count = bins
    slot_total, tile_size, _ = tiles.shape
    width = sources[0].shape[1]
    rows = bin_count * tile_size
    vmem = pl.BlockSpec(memory_space=pltpu.VMEM)
    if pieces is None:
        out_shape = [jax.ShapeDtypeStruct((rows, width), F32)]
    else:
        out_shape = [jax.ShapeDtypeStruct((pieces, width), BF16)] * (rows // pieces)
    carried = acc is not None
    share = slot_total * bin_count // bin_total
    given = [table, tiles, *sources] + ([] if acc is None else [acc])
    spec = (transposed, first_bin, bin_count, bin_total, len(sources), carried, pieces is not None)
    return pl.pallas_call(
        functools.partial(part_kernel, spec),
        out_shape=out_shape,
        in_specs=[pl.BlockSpec(memory_space=pltpu.SMEM)] + [vmem] * (len(given) - 1),
        out_specs=[vmem] * len(out_shape),
        scratch_shapes=[
            pltpu.VMEM(((empty + 1) * tile_size, width), BF16),
            pltpu.VMEM((rows, width), F32),
        ],
        compiler_params=pltpu.CompilerParams(vmem_limit_bytes=VMEM_BYTES),
        cost_estimate=pl.CostEstimate(
            flops=2 * share * tile_size * tile_size * width,
            bytes_accessed=2 * share * tile_size * tile_size,
            transcendentals=0,
        ),
    )(*given)


def grid_cycle(size):
    ny = 1
    while (2 * ny) ** 2 <= size:
        ny *= 2
    nz = size // ny
    walk = [0]
    for z in range(nz):
        ys = range(1, ny) if z % 2 == 0 else range(ny - 1, 0, -1)
        walk += [z * ny + y for y in ys]
    walk += [z * ny for z in range(nz - 1, 0, -1)]
    return walk


class Grid:
    def __init__(self, rows, cols):
        self.rows, self.cols, self.chips = rows, cols, rows // CORES
        self.walk = grid_cycle(cols)
        self.place_of = [self.walk.index(c) for c in range(cols)]
        self.row, self.col = lax.axis_index("row"), lax.axis_index("col")
        self.x, self.core = self.row // CORES, self.row % CORES
        place = sum(jnp.where(self.col == c, self.place_of[c], 0) for c in range(cols))
        self.ahead_of = [
            jnp.where(self.core == 0, self.place_of[c] - place, place - self.place_of[c]) % cols
            for c in range(cols)
        ]

    def along_walk(self, step):
        pairs = []
        for r in range(self.rows):
            walk = self.walk if r % CORES == 0 else self.walk[::-1]
            for k in range(self.cols):
                pairs.append((r * self.cols + walk[k], r * self.cols + walk[(k + step) % self.cols]))
        return pairs

    def along_x(self, step):
        return [
            (r * self.cols + c, ((r + step * CORES) % self.rows) * self.cols + c)
            for r in range(self.rows)
            for c in range(self.cols)
        ]

    def across(self, row_bit, col_bit):
        return [
            (r * self.cols + c, (r ^ row_bit) * self.cols + (c ^ col_bit))
            for r in range(self.rows)
            for c in range(self.cols)
        ]


def move(value, pairs):
    return lax.ppermute(value, ("row", "col"), pairs)


def after(value, *others):
    return lax.optimization_barrier((value, *others))[0]


def ring_hops(size):
    return (size - 1) // 2


def arrival_order(size):
    hops = ring_hops(size)
    groups = [[0]] + [[size - step, step] for step in range(1, hops + 1)]
    if size % 2 == 0:
        if hops:
            groups[min(2, hops)].append(size // 2)
        else:
            groups.append([size // 2])
    return groups


def ring_gather(own, size, pairs_of, hold):
    yield {0: own}
    ahead = behind = own
    for step, group in enumerate(arrival_order(size)[1:], 1):
        found = {}
        if step == 1:
            opposite = move(own, pairs_of(size // 2)) if size % 2 == 0 else None
        if step <= ring_hops(size):
            behind = move(after(behind, *hold.get(step, [])), pairs_of(1))
            ahead = move(ahead, pairs_of(-1))
            found = {size - step: behind, step: ahead}
        if size // 2 in group and size % 2 == 0:
            found[size // 2] = opposite
        yield found


def scatter_order(size):
    hops = ring_hops(size)
    groups = [[hop, size - hop] for hop in range(hops, 0, -1)] or [[]]
    if size % 2 == 0:
        groups[min(1, len(groups) - 1)].insert(0, size // 2)
    groups[-1].append(0)
    return groups


def ring_scatter(chunks_of, size, pairs_of):
    ahead = behind = opposite = None

    def onward(running, term):
        return term if running is None else (running.astype(F32) + term.astype(F32)).astype(BF16)

    for step, group in enumerate(scatter_order(size)):
        terms = dict(zip(group, chunks_of(step, ahead)))
        hop = ring_hops(size) - step
        if hop > 0:
            ahead = move(onward(ahead, terms[hop]), pairs_of(1))
            behind = move(onward(behind, terms[size - hop]), pairs_of(-1))
        if size // 2 in group and size % 2 == 0:
            opposite = move(terms[size // 2], pairs_of(size // 2))
    total = terms[0].astype(F32)
    for part in (opposite, ahead, behind):
        if part is not None:
            total = total + part.astype(F32)
    return total


def summed_everywhere(part, grid, gate):
    held = after(part.astype(BF16), *gate)
    got = move(held, grid.across(1, 0))
    yield None
    half = held.shape[0] // CORES
    chip = (held.astype(F32) + after(got, *gate).astype(F32)).astype(BF16)
    held = jnp.where(grid.core == 0, chip[:half], chip[half:])
    bits = [(0, 1 << k) for k in range(bits_of(grid.cols))]
    bits += [(1 << k, 0) for k in range(1, bits_of(grid.rows))]
    for row_bit, col_bit in bits:
        got = move(held, grid.across(row_bit, col_bit))
        yield None
        held = (held.astype(F32) + after(got, *gate).astype(F32)).astype(BF16)
    got = move(held, grid.across(1, 0))
    yield None
    own_first, own_last = jnp.concatenate([held, got]), jnp.concatenate([got, held])
    yield jnp.where(grid.core == 0, own_first, own_last).astype(F32)


def per_device(features, node_order, tile_vals, tile_coord, tile_count, weight, cotangent):
    nodes_here, feat_width = features.shape
    tile_size = tile_vals.shape[3]
    row_devices = lax.axis_size("row")
    col_devices = lax.axis_size("col")
    piece = nodes_here // tile_size
    block_cols = row_devices * piece
    block_rows = col_devices * piece
    grad_scale = float(nodes_here * row_devices * col_devices) ** (-0.5)
    grid = Grid(row_devices, col_devices)
    chips = grid.chips

    first_node = (grid.row * col_devices + grid.col) * nodes_here
    moves = row_moves(node_order, first_node, nodes_here)
    placed = reorder(moves, features)
    here = jnp.stack([*grid.ahead_of, grid.x, grid.core]).astype(jnp.int32)
    tiles, table_out, table_back, loaded = load_tiles(
        tile_vals[0, 0], tile_coord[0], tile_count, here, (chips, col_devices, piece), placed.shape
    )

    along_x = {}
    for found in ring_gather(placed, chips, grid.along_x, {}):
        along_x.update(found)
    along_x = [along_x[k] for k in range(chips)]
    other_core = [move(along_x[0], grid.across(1, 0))]
    other_core += [
        move(jnp.where(loaded == 0, block, 0), grid.across(1, 0)) for block in along_x[1:]
    ]
    sources_out = along_x + other_core
    grads_in = reorder(moves, cotangent)
    order = scatter_order(col_devices)
    edges = [sum(len(group) for group in order[:k]) * piece for k in range(len(order) + 1)]

    def chunks_of(step, arrived):
        table = table_out if step < 2 else after(table_out, earlier[step - 1])
        earlier.append(arrived)
        bins = (edges[step], edges[step + 1] - edges[step])
        return tile_part(
            False, table, bins, block_rows, tiles, sources_out, block_cols, pieces=nodes_here
        )

    earlier = []
    own_rows = ring_scatter(chunks_of, col_devices, grid.along_walk).astype(BF16)

    pre_act = jnp.dot(own_rows, weight, preferred_element_type=F32)
    own_act = elu_value(pre_act).astype(BF16)
    own_grad = (grads_in.astype(F32) * elu_slope(pre_act)).astype(BF16)
    own_agg_grad = lax.dot_general(
        own_grad, weight, (((1,), (1,)), ((), ())), preferred_element_type=F32
    ).astype(BF16)
    arrivals = arrival_order(col_devices)
    bins_back = len(arrivals) * block_cols
    empty_back = max(len(group) for group in arrivals) * piece
    weight_part = (
        lax.dot_general(own_rows, own_grad, (((0,), (0,)), ((), ())), preferred_element_type=F32)
        * grad_scale
    )
    acc, gate, hold, weight_grad = None, [], {}, None
    weight_steps = summed_everywhere(weight_part, grid, gate)
    weight_grad = next(weight_steps)
    for number, found in enumerate(ring_gather(own_agg_grad, col_devices, grid.along_walk, hold)):
        blocks = [found[k] for k in arrivals[number]]
        if number == len(arrivals) - 1:
            break
        bins = (number * block_cols, block_cols)
        (acc,) = tile_part(True, table_back, bins, bins_back, tiles, blocks, empty_back, acc=acc)
        hold[number + 2] = [acc]
        gate[:] = [found[number]] if number else [acc]
        weight_grad = next(weight_steps, weight_grad)
    gate[:] = blocks
    weight_grad = next(weight_steps, weight_grad)
    bins = ((len(arrivals) - 1) * block_cols, block_cols)
    mine, theirs = tile_part(
        True, table_back, bins, bins_back, tiles, blocks, empty_back, acc=acc, pieces=chips * nodes_here
    )
    got = move(theirs, grid.across(1, 0))
    both = mine.astype(F32) + got.astype(F32)
    sums = [both[k * nodes_here : (k + 1) * nodes_here] for k in range(chips)]
    sums = [sums[0]] + [term.astype(BF16) for term in sums[1:]]
    gate[:] = sums[1:]
    while weight_grad is None:
        weight_grad = next(weight_steps)
    order = scatter_order(chips)
    placed_grad = ring_scatter(
        lambda step, arrived: [sums[k] for k in order[step]], chips, grid.along_x
    ).astype(BF16)
    activations = restore(moves, own_act)
    feature_grad = restore(moves, placed_grad)
    return (activations, weight_grad, feature_grad)


def solution(mesh):
    in_specs = (
        P(("row", "col"), None),
        P(("row", "col")),
        P("row", "col", None, None, None),
        P("row", "col", None),
        P("row", "col"),
        P(),
        P(("row", "col"), None),
    )
    out_specs = (P(("row", "col"), None), P(), P(("row", "col"), None))
    return jax.shard_map(
        per_device, mesh=mesh, in_specs=in_specs, out_specs=out_specs, check_vma=False
    )
```

```python
import functools

import jax
import jax.numpy as jnp
from jax import lax
from jax.experimental import pallas as pl
from jax.experimental.pallas import tpu as pltpu
from jax.sharding import PartitionSpec as P

CORES = 2
GROUP = 4
UNROLL = 8
LANES = 128
PACK_BITS = 8
PACK = 1 << PACK_BITS
VMEM_BYTES = 16 * 1024 * 1024
LOAD_BYTES = 45 * 1024 * 1024
LOADS = 4
F32 = jnp.float32
BF16 = jnp.bfloat16


def elu_value(pre_act):
    return jnp.where(pre_act > 0, pre_act, jnp.expm1(jnp.minimum(pre_act, 0.0)))


def elu_slope(pre_act):
    return jnp.where(pre_act > 0, 1.0, jnp.exp(jnp.minimum(pre_act, 0.0)))


def row_moves(node_order, first_node, nodes_here):
    own = first_node + jnp.arange(nodes_here, dtype=jnp.int32)
    return (node_order[:, None] == own[None, :]).astype(BF16)


def reorder(moves, values):
    return jnp.dot(moves, values, preferred_element_type=F32).astype(BF16)


def restore(moves, values):
    moved = lax.dot_general(moves, values, (((0,), (0,)), ((), ())), preferred_element_type=F32)
    return moved.astype(BF16)


def bits_of(size):
    return size.bit_length() - 1


def block_places(coord, here_ref, chips, cols, piece):
    block_cols = chips * CORES * piece
    row_of, col_of = coord >> bits_of(block_cols), coord & (block_cols - 1)
    row_dev, col_dev = col_of >> bits_of(piece), row_of >> bits_of(piece)
    far = ((row_dev >> bits_of(CORES)) - here_ref[cols]) & (chips - 1)
    swap = ((row_dev & (CORES - 1)) - here_ref[cols + 1]) & (CORES - 1)
    ahead = jnp.zeros_like(coord)
    for c in range(cols):
        ahead = jnp.where(col_dev == c, here_ref[c], ahead)
    return swap * chips + far, col_of & (piece - 1), ahead, row_of & (piece - 1)


def exact_dot(left, right, contract):
    return lax.dot_general(
        left.astype(F32).astype(BF16),
        right.astype(F32).astype(BF16),
        (contract, ((), ())),
        preferred_element_type=F32,
    )


def table_width(slot_total, bin_total):
    group_total = slot_total // GROUP + bin_total + 1
    return -(-max(group_total * GROUP, bin_total + 1) // LANES) * LANES


def write_table(out_ref, bins, bin_total, sources, slots, tile_total, empty):
    lanes = slots.shape[1]
    width = out_ref.shape[1]
    bin_rows = -(-bin_total // 8) * 8
    live = slots < tile_total
    of_bin = lax.broadcasted_iota(jnp.int32, (bin_rows, lanes), 0)
    mine = ((of_bin == bins) & live).astype(jnp.int32)
    earlier = lax.broadcasted_iota(jnp.int32, (lanes, lanes), 0) < lax.broadcasted_iota(
        jnp.int32, (lanes, lanes), 1
    )
    before = exact_dot(mine, earlier.astype(jnp.int32), ((1,), (0,)))
    counts = jnp.sum(mine.astype(F32), axis=1, keepdims=True)
    groups = (counts.astype(jnp.int32) + GROUP - 1) >> bits_of(GROUP)
    bin_at = lax.broadcasted_iota(jnp.int32, (bin_rows, width), 0)
    lane_at = lax.broadcasted_iota(jnp.int32, (bin_rows, width), 1)
    firsts = jnp.sum(jnp.where(bin_at < lane_at, groups, 0).astype(F32), axis=0, keepdims=True)
    here = lax.broadcasted_iota(jnp.int32, (bin_rows, bin_rows), 0)
    other = lax.broadcasted_iota(jnp.int32, (bin_rows, bin_rows), 1)
    firsts_of = exact_dot((other < here).astype(jnp.int32), groups, ((1,), (0,))).astype(jnp.int32)
    group_bin = jnp.sum((firsts_of + groups <= lane_at).astype(F32), axis=0, keepdims=True)
    place = jnp.sum(
        mine.astype(F32) * (before + (firsts_of * GROUP).astype(F32)), axis=0, keepdims=True
    ).astype(jnp.int32)
    place = jnp.where(live, place, -1)
    hit = (lax.broadcasted_iota(jnp.int32, (width, lanes), 0) == place).astype(jnp.int32)
    row = lax.broadcasted_iota(jnp.int32, (8, lanes), 0)
    facts = jnp.where(row == 0, slots, jnp.where(row == 1, sources, 1))
    found = exact_dot(facts, hit, ((1,), (1,))).astype(jnp.int32)
    members = jnp.where(found[2:3] > 0, found[0:1] * PACK + found[1:2], empty)
    rows = lax.broadcasted_iota(jnp.int32, (8, width), 0)
    out_ref[...] = jnp.where(
        rows == 0,
        members,
        jnp.where(rows == 1, group_bin.astype(jnp.int32), firsts.astype(jnp.int32)),
    )


def load_kernel(sizes, here_ref, facts_ref, tiles_ref, out_ref, ahead_ref, back_ref, gate_ref, sems):
    chips, cols, piece = sizes
    slot_total = tiles_ref.shape[0]
    share = slot_total // LOADS
    copies = [
        pltpu.make_async_copy(
            tiles_ref.at[pl.ds(k * share, share)], out_ref.at[pl.ds(k * share, share)], sems.at[k]
        )
        for k in range(LOADS)
    ]
    for copy in copies:
        copy.start()
    gate_ref[...] = jnp.zeros_like(gate_ref)
    coord = facts_ref[0:1, :]
    slots = lax.broadcasted_iota(jnp.int32, coord.shape, 1)
    tile_total = facts_ref[1:2, 0:1]
    row_place, col_piece, ahead, row_piece = block_places(coord, here_ref, chips, cols, piece)
    block_rows, block_cols = cols * piece, chips * CORES * piece

    order = [k for group in scatter_order(cols) for k in group]
    bins = jnp.zeros_like(coord)
    for place, k in enumerate(order):
        bins = jnp.where(ahead == k, place, bins)
    bins = bins * piece + row_piece
    write_table(
        ahead_ref, bins, block_rows, row_place * piece + col_piece, slots, tile_total, block_cols
    )

    arrivals = arrival_order(cols)
    part_of, block_at = jnp.zeros_like(coord), jnp.zeros_like(coord)
    for part, group in enumerate(arrivals):
        for at, k in enumerate(group):
            part_of = jnp.where(ahead == k, part, part_of)
            block_at = jnp.where(ahead == k, at, block_at)
    bins = part_of * block_cols + row_place * piece + col_piece
    write_table(
        back_ref,
        bins,
        len(arrivals) * block_cols,
        block_at * piece + row_piece,
        slots,
        tile_total,
        max(len(group) for group in arrivals) * piece,
    )
    for copy in copies:
        copy.wait()


def load_tiles(tiles, coord, count, here, sizes, gate_shape):
    chips, cols, piece = sizes
    slot_total = tiles.shape[0]
    bins_back = len(arrival_order(cols)) * chips * CORES * piece
    lanes = -(-slot_total // LANES) * LANES
    facts = jnp.concatenate([jnp.pad(row, ((0, 0), (0, lanes - row.shape[1]))) for row in (coord, count)])
    vmem = pl.BlockSpec(memory_space=pltpu.VMEM)
    return pl.pallas_call(
        functools.partial(load_kernel, sizes),
        out_shape=[
            jax.ShapeDtypeStruct(tiles.shape, tiles.dtype),
            jax.ShapeDtypeStruct((8, table_width(slot_total, cols * piece)), jnp.int32),
            jax.ShapeDtypeStruct((8, table_width(slot_total, bins_back)), jnp.int32),
            jax.ShapeDtypeStruct(gate_shape, BF16),
        ],
        in_specs=[pl.BlockSpec(memory_space=pltpu.SMEM), vmem, pl.BlockSpec(memory_space=pl.ANY)],
        out_specs=[vmem] * 4,
        scratch_shapes=[pltpu.SemaphoreType.DMA((LOADS,))],
        compiler_params=pltpu.CompilerParams(vmem_limit_bytes=LOAD_BYTES),
        cost_estimate=pl.CostEstimate(flops=0, bytes_accessed=2 * tiles.size, transcendentals=0),
    )(here, facts, tiles)


def part_kernel(spec, table_ref, tiles_ref, *refs):
    transposed, first_bin, bin_count, bin_total, source_count, carried, finish = spec
    source_refs = refs[:source_count]
    out_refs = refs[source_count + carried : -2]
    source, total = refs[-2:]
    slot_total, tile_size, _ = tiles_ref.shape
    group_total = slot_total // GROUP + bin_total + 1
    at = 0
    for ref in source_refs:
        source[at : at + ref.shape[0], :] = ref[...]
        at += ref.shape[0]
    source[at:, :] = jnp.zeros((source.shape[0] - at, source.shape[1]), source.dtype)
    total[...] = refs[source_count][...] if carried else jnp.zeros_like(total)
    begin = table_ref[2, first_bin]
    end = table_ref[2, first_bin + bin_count]
    contract = 0 if transposed else 1

    def step(number, carry):
        products = []
        for member in range(UNROLL):
            group = begin + number * UNROLL + member
            group = jnp.where(group < end, group, group_total - 1)
            left, right = [], []
            for k in range(GROUP):
                packed = table_ref[0, group * GROUP + k]
                left.append(tiles_ref[packed >> PACK_BITS])
                row = pl.multiple_of((packed & (PACK - 1)) * tile_size, tile_size)
                right.append(source[pl.ds(row, tile_size), :])
            product = lax.dot_general(
                jnp.concatenate(left, axis=contract),
                jnp.concatenate(right, axis=0),
                (((contract,), (0,)), ((), ())),
                preferred_element_type=F32,
            )
            products.append((jnp.minimum(table_ref[1, group] - first_bin, bin_count - 1), product))
        for place, product in products:
            rows = pl.ds(pl.multiple_of(place * tile_size, tile_size), tile_size)
            total[rows, :] += product
        return carry

    lax.fori_loop(0, (end - begin + UNROLL - 1) // UNROLL, step, 0)
    if finish:
        at = 0
        for ref in out_refs:
            ref[...] = total[at : at + ref.shape[0], :].astype(ref.dtype)
            at += ref.shape[0]
    else:
        out_refs[0][...] = total[...]


def tile_part(transposed, table, bins, bin_total, tiles, sources, empty, acc=None, pieces=None):
    first_bin, bin_count = bins
    slot_total, tile_size, _ = tiles.shape
    width = sources[0].shape[1]
    rows = bin_count * tile_size
    vmem = pl.BlockSpec(memory_space=pltpu.VMEM)
    if pieces is None:
        out_shape = [jax.ShapeDtypeStruct((rows, width), F32)]
    else:
        out_shape = [jax.ShapeDtypeStruct((pieces, width), BF16)] * (rows // pieces)
    carried = acc is not None
    share = slot_total * bin_count // bin_total
    given = [table, tiles, *sources] + ([] if acc is None else [acc])
    spec = (transposed, first_bin, bin_count, bin_total, len(sources), carried, pieces is not None)
    return pl.pallas_call(
        functools.partial(part_kernel, spec),
        out_shape=out_shape,
        in_specs=[pl.BlockSpec(memory_space=pltpu.SMEM)] + [vmem] * (len(given) - 1),
        out_specs=[vmem] * len(out_shape),
        scratch_shapes=[
            pltpu.VMEM(((empty + 1) * tile_size, width), BF16),
            pltpu.VMEM((rows, width), F32),
        ],
        compiler_params=pltpu.CompilerParams(vmem_limit_bytes=VMEM_BYTES),
        cost_estimate=pl.CostEstimate(
            flops=2 * share * tile_size * tile_size * width,
            bytes_accessed=2 * share * tile_size * tile_size,
            transcendentals=0,
        ),
    )(*given)


def grid_cycle(size):
    ny = 1
    while (2 * ny) ** 2 <= size:
        ny *= 2
    nz = size // ny
    walk = [0]
    for z in range(nz):
        ys = range(1, ny) if z % 2 == 0 else range(ny - 1, 0, -1)
        walk += [z * ny + y for y in ys]
    walk += [z * ny for z in range(nz - 1, 0, -1)]
    return walk


class Grid:
    def __init__(self, rows, cols):
        self.rows, self.cols, self.chips = rows, cols, rows // CORES
        self.walk = grid_cycle(cols)
        self.place_of = [self.walk.index(c) for c in range(cols)]
        self.row, self.col = lax.axis_index("row"), lax.axis_index("col")
        self.x, self.core = self.row // CORES, self.row % CORES
        place = sum(jnp.where(self.col == c, self.place_of[c], 0) for c in range(cols))
        self.ahead_of = [
            jnp.where(self.core == 0, self.place_of[c] - place, place - self.place_of[c]) % cols
            for c in range(cols)
        ]

    def along_walk(self, step):
        pairs = []
        for r in range(self.rows):
            walk = self.walk if r % CORES == 0 else self.walk[::-1]
            for k in range(self.cols):
                pairs.append((r * self.cols + walk[k], r * self.cols + walk[(k + step) % self.cols]))
        return pairs

    def along_x(self, step):
        return [
            (r * self.cols + c, ((r + step * CORES) % self.rows) * self.cols + c)
            for r in range(self.rows)
            for c in range(self.cols)
        ]

    def across(self, row_bit, col_bit):
        return [
            (r * self.cols + c, (r ^ row_bit) * self.cols + (c ^ col_bit))
            for r in range(self.rows)
            for c in range(self.cols)
        ]


def move(value, pairs):
    return lax.ppermute(value, ("row", "col"), pairs)


def after(value, *others):
    return lax.optimization_barrier((value, *others))[0]


def ring_hops(size):
    return (size - 1) // 2


def arrival_order(size):
    hops = ring_hops(size)
    groups = [[0]] + [[size - step, step] for step in range(1, hops + 1)]
    if size % 2 == 0:
        if hops:
            groups[min(2, hops)].append(size // 2)
        else:
            groups.append([size // 2])
    return groups


def ring_gather(own, size, pairs_of, hold):
    yield {0: own}
    ahead = behind = own
    for step, group in enumerate(arrival_order(size)[1:], 1):
        found = {}
        if step == 1:
            opposite = move(own, pairs_of(size // 2)) if size % 2 == 0 else None
        if step <= ring_hops(size):
            behind = move(after(behind, *hold.get(step, [])), pairs_of(1))
            ahead = move(ahead, pairs_of(-1))
            found = {size - step: behind, step: ahead}
        if size // 2 in group and size % 2 == 0:
            found[size // 2] = opposite
        yield found


def scatter_order(size):
    hops = ring_hops(size)
    groups = [[hop, size - hop] for hop in range(hops, 0, -1)] or [[]]
    if size % 2 == 0:
        groups[0].append(size // 2)
    groups[-1].append(0)
    return groups


def ring_scatter(chunks_of, size, pairs_of):
    ahead = behind = opposite = None

    def onward(running, term):
        return term if running is None else (running.astype(F32) + term.astype(F32)).astype(BF16)

    for step, group in enumerate(scatter_order(size)):
        terms = dict(zip(group, chunks_of(step, ahead)))
        hop = ring_hops(size) - step
        if hop > 0:
            ahead = move(onward(ahead, terms[hop]), pairs_of(1))
            behind = move(onward(behind, terms[size - hop]), pairs_of(-1))
        if size // 2 in group and size % 2 == 0:
            opposite = move(terms[size // 2], pairs_of(size // 2))
    total = terms[0].astype(F32)
    for part in (opposite, ahead, behind):
        if part is not None:
            total = total + part.astype(F32)
    return total


def summed_everywhere(part, grid, gate):
    held = after(part.astype(BF16), *gate)
    got = move(held, grid.across(1, 0))
    yield None
    half = held.shape[0] // CORES
    chip = (held.astype(F32) + after(got, *gate).astype(F32)).astype(BF16)
    held = jnp.where(grid.core == 0, chip[:half], chip[half:])
    bits = [(0, 1)] + [(0, 1 << k) for k in range(bits_of(grid.cols) - 1, 0, -1)]
    bits += [(1 << k, 0) for k in range(1, bits_of(grid.rows))]
    for row_bit, col_bit in bits:
        got = move(held, grid.across(row_bit, col_bit))
        yield None
        held = (held.astype(F32) + after(got, *gate).astype(F32)).astype(BF16)
    got = move(held, grid.across(1, 0))
    yield None
    own_first, own_last = jnp.concatenate([held, got]), jnp.concatenate([got, held])
    yield jnp.where(grid.core == 0, own_first, own_last).astype(F32)


def per_device(features, node_order, tile_vals, tile_coord, tile_count, weight, cotangent):
    nodes_here, feat_width = features.shape
    tile_size = tile_vals.shape[3]
    row_devices = lax.axis_size("row")
    col_devices = lax.axis_size("col")
    piece = nodes_here // tile_size
    block_cols = row_devices * piece
    block_rows = col_devices * piece
    grad_scale = float(nodes_here * row_devices * col_devices) ** (-0.5)
    grid = Grid(row_devices, col_devices)
    chips = grid.chips

    first_node = (grid.row * col_devices + grid.col) * nodes_here
    moves = row_moves(node_order, first_node, nodes_here)
    placed = reorder(moves, features)
    here = jnp.stack([*grid.ahead_of, grid.x, grid.core]).astype(jnp.int32)
    tiles, table_out, table_back, loaded = load_tiles(
        tile_vals[0, 0], tile_coord[0], tile_count, here, (chips, col_devices, piece), placed.shape
    )

    along_x = {}
    for found in ring_gather(placed, chips, grid.along_x, {}):
        along_x.update(found)
    along_x = [along_x[k] for k in range(chips)]
    other_core = [move(along_x[0], grid.across(1, 0))]
    other_core += [
        move(jnp.where(loaded == 0, block, 0), grid.across(1, 0)) for block in along_x[1:]
    ]
    sources_out = along_x + other_core
    grads_in = reorder(moves, cotangent)
    order = scatter_order(col_devices)
    edges = [sum(len(group) for group in order[:k]) * piece for k in range(len(order) + 1)]

    def chunks_of(step, arrived):
        table = table_out if step < 2 else after(table_out, earlier[step - 1])
        earlier.append(arrived)
        bins = (edges[step], edges[step + 1] - edges[step])
        return tile_part(
            False, table, bins, block_rows, tiles, sources_out, block_cols, pieces=nodes_here
        )

    earlier = []
    own_rows = ring_scatter(chunks_of, col_devices, grid.along_walk).astype(BF16)

    pre_act = jnp.dot(own_rows, weight, preferred_element_type=F32)
    own_act = elu_value(pre_act).astype(BF16)
    own_grad = (grads_in.astype(F32) * elu_slope(pre_act)).astype(BF16)
    own_agg_grad = lax.dot_general(
        own_grad, weight, (((1,), (1,)), ((), ())), preferred_element_type=F32
    ).astype(BF16)
    arrivals = arrival_order(col_devices)
    bins_back = len(arrivals) * block_cols
    empty_back = max(len(group) for group in arrivals) * piece
    weight_part = (
        lax.dot_general(own_rows, own_grad, (((0,), (0,)), ((), ())), preferred_element_type=F32)
        * grad_scale
    )
    acc, gate, hold, weight_grad = None, [], {}, None
    weight_steps = summed_everywhere(weight_part, grid, gate)
    weight_grad = next(weight_steps)
    for number, found in enumerate(ring_gather(own_agg_grad, col_devices, grid.along_walk, hold)):
        blocks = [found[k] for k in arrivals[number]]
        if number == len(arrivals) - 1:
            break
        bins = (number * block_cols, block_cols)
        (acc,) = tile_part(True, table_back, bins, bins_back, tiles, blocks, empty_back, acc=acc)
        hold[number + 2] = [acc]
        gate[:] = [found[number]] if number else [acc]
        weight_grad = next(weight_steps, weight_grad)
    gate[:] = blocks
    weight_grad = next(weight_steps, weight_grad)
    bins = ((len(arrivals) - 1) * block_cols, block_cols)
    mine, theirs = tile_part(
        True, table_back, bins, bins_back, tiles, blocks, empty_back, acc=acc, pieces=chips * nodes_here
    )
    got = move(theirs, grid.across(1, 0))
    both = mine.astype(F32) + got.astype(F32)
    sums = [both[k * nodes_here : (k + 1) * nodes_here] for k in range(chips)]
    sums = [sums[0]] + [term.astype(BF16) for term in sums[1:]]
    gate[:] = sums[1:]
    while weight_grad is None:
        weight_grad = next(weight_steps)
    order = scatter_order(chips)
    placed_grad = ring_scatter(
        lambda step, arrived: [sums[k] for k in order[step]], chips, grid.along_x
    ).astype(BF16)
    activations = restore(moves, own_act)
    feature_grad = restore(moves, placed_grad)
    return (activations, weight_grad, feature_grad)


def solution(mesh):
    in_specs = (
        P(("row", "col"), None),
        P(("row", "col")),
        P("row", "col", None, None, None),
        P("row", "col", None),
        P("row", "col"),
        P(),
        P(("row", "col"), None),
    )
    out_specs = (P(("row", "col"), None), P(), P(("row", "col"), None))
    return jax.shard_map(
        per_device, mesh=mesh, in_specs=in_specs, out_specs=out_specs, check_vma=False
    )
```

```python
import functools

import jax
import jax.numpy as jnp
from jax import lax
from jax.experimental import pallas as pl
from jax.experimental.pallas import tpu as pltpu
from jax.sharding import PartitionSpec as P

CORES = 2
GROUP = 4
UNROLL = 8
LANES = 128
PACK_BITS = 8
PACK = 1 << PACK_BITS
VMEM_BYTES = 16 * 1024 * 1024
LOAD_BYTES = 45 * 1024 * 1024
LOADS = 4
F32 = jnp.float32
BF16 = jnp.bfloat16


def elu_value(pre_act):
    return jnp.where(pre_act > 0, pre_act, jnp.expm1(jnp.minimum(pre_act, 0.0)))


def elu_slope(pre_act):
    return jnp.where(pre_act > 0, 1.0, jnp.exp(jnp.minimum(pre_act, 0.0)))


def row_moves(node_order, first_node, nodes_here):
    own = first_node + jnp.arange(nodes_here, dtype=jnp.int32)
    return (node_order[:, None] == own[None, :]).astype(BF16)


def reorder(moves, values):
    return jnp.dot(moves, values, preferred_element_type=F32).astype(BF16)


def restore(moves, values):
    moved = lax.dot_general(moves, values, (((0,), (0,)), ((), ())), preferred_element_type=F32)
    return moved.astype(BF16)


def bits_of(size):
    return size.bit_length() - 1


def block_places(coord, here_ref, chips, cols, piece):
    block_cols = chips * CORES * piece
    row_of, col_of = coord >> bits_of(block_cols), coord & (block_cols - 1)
    row_dev, col_dev = col_of >> bits_of(piece), row_of >> bits_of(piece)
    far = ((row_dev >> bits_of(CORES)) - here_ref[cols]) & (chips - 1)
    swap = ((row_dev & (CORES - 1)) - here_ref[cols + 1]) & (CORES - 1)
    ahead = jnp.zeros_like(coord)
    for c in range(cols):
        ahead = jnp.where(col_dev == c, here_ref[c], ahead)
    return swap * chips + far, col_of & (piece - 1), ahead, row_of & (piece - 1)


def exact_dot(left, right, contract):
    return lax.dot_general(
        left.astype(F32).astype(BF16),
        right.astype(F32).astype(BF16),
        (contract, ((), ())),
        preferred_element_type=F32,
    )


def table_width(slot_total, bin_total):
    group_total = slot_total // GROUP + bin_total + 1
    return -(-max(group_total * GROUP, bin_total + 1) // LANES) * LANES


def write_table(out_ref, bins, bin_total, sources, slots, tile_total, empty):
    lanes = slots.shape[1]
    width = out_ref.shape[1]
    bin_rows = -(-bin_total // 8) * 8
    live = slots < tile_total
    of_bin = lax.broadcasted_iota(jnp.int32, (bin_rows, lanes), 0)
    mine = ((of_bin == bins) & live).astype(jnp.int32)
    earlier = lax.broadcasted_iota(jnp.int32, (lanes, lanes), 0) < lax.broadcasted_iota(
        jnp.int32, (lanes, lanes), 1
    )
    before = exact_dot(mine, earlier.astype(jnp.int32), ((1,), (0,)))
    counts = jnp.sum(mine.astype(F32), axis=1, keepdims=True)
    groups = (counts.astype(jnp.int32) + GROUP - 1) >> bits_of(GROUP)
    bin_at = lax.broadcasted_iota(jnp.int32, (bin_rows, width), 0)
    lane_at = lax.broadcasted_iota(jnp.int32, (bin_rows, width), 1)
    firsts = jnp.sum(jnp.where(bin_at < lane_at, groups, 0).astype(F32), axis=0, keepdims=True)
    here = lax.broadcasted_iota(jnp.int32, (bin_rows, bin_rows), 0)
    other = lax.broadcasted_iota(jnp.int32, (bin_rows, bin_rows), 1)
    firsts_of = exact_dot((other < here).astype(jnp.int32), groups, ((1,), (0,))).astype(jnp.int32)
    group_bin = jnp.sum((firsts_of + groups <= lane_at).astype(F32), axis=0, keepdims=True)
    place = jnp.sum(
        mine.astype(F32) * (before + (firsts_of * GROUP).astype(F32)), axis=0, keepdims=True
    ).astype(jnp.int32)
    place = jnp.where(live, place, -1)
    hit = (lax.broadcasted_iota(jnp.int32, (width, lanes), 0) == place).astype(jnp.int32)
    row = lax.broadcasted_iota(jnp.int32, (8, lanes), 0)
    facts = jnp.where(row == 0, slots, jnp.where(row == 1, sources, 1))
    found = exact_dot(facts, hit, ((1,), (1,))).astype(jnp.int32)
    members = jnp.where(found[2:3] > 0, found[0:1] * PACK + found[1:2], empty)
    rows = lax.broadcasted_iota(jnp.int32, (8, width), 0)
    out_ref[...] = jnp.where(
        rows == 0,
        members,
        jnp.where(rows == 1, group_bin.astype(jnp.int32), firsts.astype(jnp.int32)),
    )


def load_kernel(sizes, here_ref, facts_ref, tiles_ref, out_ref, ahead_ref, back_ref, gate_ref, sems):
    chips, cols, piece = sizes
    slot_total = tiles_ref.shape[0]
    share = slot_total // LOADS
    copies = [
        pltpu.make_async_copy(
            tiles_ref.at[pl.ds(k * share, share)], out_ref.at[pl.ds(k * share, share)], sems.at[k]
        )
        for k in range(LOADS)
    ]
    for copy in copies:
        copy.start()
    gate_ref[...] = jnp.zeros_like(gate_ref)
    coord = facts_ref[0:1, :]
    slots = lax.broadcasted_iota(jnp.int32, coord.shape, 1)
    tile_total = facts_ref[1:2, 0:1]
    row_place, col_piece, ahead, row_piece = block_places(coord, here_ref, chips, cols, piece)
    block_rows, block_cols = cols * piece, chips * CORES * piece

    order = [k for group in scatter_order(cols) for k in group]
    bins = jnp.zeros_like(coord)
    for place, k in enumerate(order):
        bins = jnp.where(ahead == k, place, bins)
    bins = bins * piece + row_piece
    write_table(
        ahead_ref, bins, block_rows, row_place * piece + col_piece, slots, tile_total, block_cols
    )

    arrivals = arrival_order(cols)
    part_of, block_at = jnp.zeros_like(coord), jnp.zeros_like(coord)
    for part, group in enumerate(arrivals):
        for at, k in enumerate(group):
            part_of = jnp.where(ahead == k, part, part_of)
            block_at = jnp.where(ahead == k, at, block_at)
    bins = part_of * block_cols + row_place * piece + col_piece
    write_table(
        back_ref,
        bins,
        len(arrivals) * block_cols,
        block_at * piece + row_piece,
        slots,
        tile_total,
        max(len(group) for group in arrivals) * piece,
    )
    for copy in copies:
        copy.wait()


def load_tiles(tiles, coord, count, here, sizes, gate_shape):
    chips, cols, piece = sizes
    slot_total = tiles.shape[0]
    bins_back = len(arrival_order(cols)) * chips * CORES * piece
    lanes = -(-slot_total // LANES) * LANES
    facts = jnp.concatenate([jnp.pad(row, ((0, 0), (0, lanes - row.shape[1]))) for row in (coord, count)])
    vmem = pl.BlockSpec(memory_space=pltpu.VMEM)
    return pl.pallas_call(
        functools.partial(load_kernel, sizes),
        out_shape=[
            jax.ShapeDtypeStruct(tiles.shape, tiles.dtype),
            jax.ShapeDtypeStruct((8, table_width(slot_total, cols * piece)), jnp.int32),
            jax.ShapeDtypeStruct((8, table_width(slot_total, bins_back)), jnp.int32),
            jax.ShapeDtypeStruct(gate_shape, BF16),
        ],
        in_specs=[pl.BlockSpec(memory_space=pltpu.SMEM), vmem, pl.BlockSpec(memory_space=pl.ANY)],
        out_specs=[vmem] * 4,
        scratch_shapes=[pltpu.SemaphoreType.DMA((LOADS,))],
        compiler_params=pltpu.CompilerParams(vmem_limit_bytes=LOAD_BYTES),
        cost_estimate=pl.CostEstimate(flops=0, bytes_accessed=2 * tiles.size, transcendentals=0),
    )(here, facts, tiles)


def part_kernel(spec, table_ref, tiles_ref, *refs):
    transposed, first_bin, bin_count, bin_total, source_count, carried, finish = spec
    source_refs = refs[:source_count]
    out_refs = refs[source_count + carried : -2]
    source, total = refs[-2:]
    slot_total, tile_size, _ = tiles_ref.shape
    group_total = slot_total // GROUP + bin_total + 1
    at = 0
    for ref in source_refs:
        source[at : at + ref.shape[0], :] = ref[...]
        at += ref.shape[0]
    source[at:, :] = jnp.zeros((source.shape[0] - at, source.shape[1]), source.dtype)
    total[...] = refs[source_count][...] if carried else jnp.zeros_like(total)
    begin = table_ref[2, first_bin]
    end = table_ref[2, first_bin + bin_count]
    contract = 0 if transposed else 1

    def step(number, carry):
        products = []
        for member in range(UNROLL):
            group = begin + number * UNROLL + member
            group = jnp.where(group < end, group, group_total - 1)
            left, right = [], []
            for k in range(GROUP):
                packed = table_ref[0, group * GROUP + k]
                left.append(tiles_ref[packed >> PACK_BITS])
                row = pl.multiple_of((packed & (PACK - 1)) * tile_size, tile_size)
                right.append(source[pl.ds(row, tile_size), :])
            product = lax.dot_general(
                jnp.concatenate(left, axis=contract),
                jnp.concatenate(right, axis=0),
                (((contract,), (0,)), ((), ())),
                preferred_element_type=F32,
            )
            products.append((jnp.minimum(table_ref[1, group] - first_bin, bin_count - 1), product))
        for place, product in products:
            rows = pl.ds(pl.multiple_of(place * tile_size, tile_size), tile_size)
            total[rows, :] += product
        return carry

    lax.fori_loop(0, (end - begin + UNROLL - 1) // UNROLL, step, 0)
    if finish:
        at = 0
        for ref in out_refs:
            ref[...] = total[at : at + ref.shape[0], :].astype(ref.dtype)
            at += ref.shape[0]
    else:
        out_refs[0][...] = total[...]


def tile_part(transposed, table, bins, bin_total, tiles, sources, empty, acc=None, pieces=None):
    first_bin, bin_count = bins
    slot_total, tile_size, _ = tiles.shape
    width = sources[0].shape[1]
    rows = bin_count * tile_size
    vmem = pl.BlockSpec(memory_space=pltpu.VMEM)
    if pieces is None:
        out_shape = [jax.ShapeDtypeStruct((rows, width), F32)]
    else:
        out_shape = [jax.ShapeDtypeStruct((pieces, width), BF16)] * (rows // pieces)
    carried = acc is not None
    share = slot_total * bin_count // bin_total
    given = [table, tiles, *sources] + ([] if acc is None else [acc])
    spec = (transposed, first_bin, bin_count, bin_total, len(sources), carried, pieces is not None)
    return pl.pallas_call(
        functools.partial(part_kernel, spec),
        out_shape=out_shape,
        in_specs=[pl.BlockSpec(memory_space=pltpu.SMEM)] + [vmem] * (len(given) - 1),
        out_specs=[vmem] * len(out_shape),
        scratch_shapes=[
            pltpu.VMEM(((empty + 1) * tile_size, width), BF16),
            pltpu.VMEM((rows, width), F32),
        ],
        compiler_params=pltpu.CompilerParams(vmem_limit_bytes=VMEM_BYTES),
        cost_estimate=pl.CostEstimate(
            flops=2 * share * tile_size * tile_size * width,
            bytes_accessed=2 * share * tile_size * tile_size,
            transcendentals=0,
        ),
    )(*given)


def grid_cycle(size):
    ny = 1
    while (2 * ny) ** 2 <= size:
        ny *= 2
    nz = size // ny
    walk = [0]
    for z in range(nz):
        ys = range(1, ny) if z % 2 == 0 else range(ny - 1, 0, -1)
        walk += [z * ny + y for y in ys]
    walk += [z * ny for z in range(nz - 1, 0, -1)]
    return walk


class Grid:
    def __init__(self, rows, cols):
        self.rows, self.cols, self.chips = rows, cols, rows // CORES
        self.walk = grid_cycle(cols)
        self.place_of = [self.walk.index(c) for c in range(cols)]
        self.row, self.col = lax.axis_index("row"), lax.axis_index("col")
        self.x, self.core = self.row // CORES, self.row % CORES
        place = sum(jnp.where(self.col == c, self.place_of[c], 0) for c in range(cols))
        self.ahead_of = [
            jnp.where(self.core == 0, self.place_of[c] - place, place - self.place_of[c]) % cols
            for c in range(cols)
        ]

    def along_walk(self, step):
        pairs = []
        for r in range(self.rows):
            walk = self.walk if r % CORES == 0 else self.walk[::-1]
            for k in range(self.cols):
                pairs.append((r * self.cols + walk[k], r * self.cols + walk[(k + step) % self.cols]))
        return pairs

    def along_x(self, step):
        return [
            (r * self.cols + c, ((r + step * CORES) % self.rows) * self.cols + c)
            for r in range(self.rows)
            for c in range(self.cols)
        ]

    def across(self, row_bit, col_bit):
        return [
            (r * self.cols + c, (r ^ row_bit) * self.cols + (c ^ col_bit))
            for r in range(self.rows)
            for c in range(self.cols)
        ]


def move(value, pairs):
    return lax.ppermute(value, ("row", "col"), pairs)


def after(value, *others):
    return lax.optimization_barrier((value, *others))[0]


def ring_hops(size):
    return (size - 1) // 2


def arrival_order(size):
    hops = ring_hops(size)
    groups = [[0]] + [[size - step, step] for step in range(1, hops + 1)]
    if size % 2 == 0:
        if hops:
            groups[min(2, hops)].append(size // 2)
        else:
            groups.append([size // 2])
    return groups


def ring_gather(own, size, pairs_of, hold):
    yield {0: own}
    ahead = behind = own
    for step, group in enumerate(arrival_order(size)[1:], 1):
        found = {}
        if step == 1:
            opposite = move(own, pairs_of(size // 2)) if size % 2 == 0 else None
        if step <= ring_hops(size):
            behind = move(after(behind, *hold.get(step, [])), pairs_of(1))
            ahead = move(ahead, pairs_of(-1))
            found = {size - step: behind, step: ahead}
        if size // 2 in group and size % 2 == 0:
            found[size // 2] = opposite
        yield found


def scatter_order(size):
    hops = ring_hops(size)
    groups = [[hop, size - hop] for hop in range(hops, 0, -1)] or [[]]
    if size % 2 == 0:
        groups[0].append(size // 2)
    groups[-1].append(0)
    return groups


def ring_scatter(chunks_of, size, pairs_of):
    ahead = behind = opposite = None

    def onward(running, term):
        return term if running is None else (running.astype(F32) + term.astype(F32)).astype(BF16)

    for step, group in enumerate(scatter_order(size)):
        terms = dict(zip(group, chunks_of(step, ahead)))
        hop = ring_hops(size) - step
        if hop > 0:
            ahead = move(onward(ahead, terms[hop]), pairs_of(1))
            behind = move(onward(behind, terms[size - hop]), pairs_of(-1))
        if size // 2 in group and size % 2 == 0:
            opposite = move(terms[size // 2], pairs_of(size // 2))
    total = terms[0].astype(F32)
    for part in (opposite, ahead, behind):
        if part is not None:
            total = total + part.astype(F32)
    return total


def summed_everywhere(part, grid, gate):
    held = after(part.astype(BF16), *gate)
    got = move(held, grid.across(1, 0))
    yield None
    half = held.shape[0] // CORES
    chip = (held.astype(F32) + after(got, *gate).astype(F32)).astype(BF16)
    held = jnp.where(grid.core == 0, chip[:half], chip[half:])
    bits = [(0, 1 << k) for k in range(bits_of(grid.cols))]
    bits += [(1 << k, 0) for k in range(1, bits_of(grid.rows))]
    for row_bit, col_bit in bits:
        got = move(held, grid.across(row_bit, col_bit))
        yield None
        held = (held.astype(F32) + after(got, *gate).astype(F32)).astype(BF16)
    got = move(held, grid.across(1, 0))
    yield None
    own_first, own_last = jnp.concatenate([held, got]), jnp.concatenate([got, held])
    yield jnp.where(grid.core == 0, own_first, own_last).astype(F32)


def per_device(features, node_order, tile_vals, tile_coord, tile_count, weight, cotangent):
    nodes_here, feat_width = features.shape
    tile_size = tile_vals.shape[3]
    row_devices = lax.axis_size("row")
    col_devices = lax.axis_size("col")
    piece = nodes_here // tile_size
    block_cols = row_devices * piece
    block_rows = col_devices * piece
    grad_scale = float(nodes_here * row_devices * col_devices) ** (-0.5)
    grid = Grid(row_devices, col_devices)
    chips = grid.chips

    first_node = (grid.row * col_devices + grid.col) * nodes_here
    moves = row_moves(node_order, first_node, nodes_here)
    placed = reorder(moves, features)
    here = jnp.stack([*grid.ahead_of, grid.x, grid.core]).astype(jnp.int32)
    tiles, table_out, table_back, loaded = load_tiles(
        tile_vals[0, 0], tile_coord[0], tile_count, here, (chips, col_devices, piece), placed.shape
    )

    along_x = {}
    for found in ring_gather(placed, chips, grid.along_x, {}):
        along_x.update(found)
    along_x = [along_x[k] for k in range(chips)]
    other_core = [move(along_x[0], grid.across(1, 0))]
    other_core += [
        move(jnp.where(loaded == 0, block, 0), grid.across(1, 0)) for block in along_x[1:]
    ]
    sources_out = along_x + other_core
    grads_in = reorder(moves, cotangent)
    order = scatter_order(col_devices)
    edges = [sum(len(group) for group in order[:k]) * piece for k in range(len(order) + 1)]

    def chunks_of(step, arrived):
        table = table_out if step < 2 else after(table_out, earlier[step - 1])
        earlier.append(arrived)
        bins = (edges[step], edges[step + 1] - edges[step])
        return tile_part(
            False, table, bins, block_rows, tiles, sources_out, block_cols, pieces=nodes_here
        )

    earlier = []
    own_rows = ring_scatter(chunks_of, col_devices, grid.along_walk).astype(BF16)

    pre_act = jnp.dot(own_rows, weight, preferred_element_type=F32)
    own_act = elu_value(pre_act).astype(BF16)
    own_grad = (grads_in.astype(F32) * elu_slope(pre_act)).astype(BF16)
    own_agg_grad = lax.dot_general(
        own_grad, weight, (((1,), (1,)), ((), ())), preferred_element_type=F32
    ).astype(BF16)
    arrivals = arrival_order(col_devices)
    bins_back = len(arrivals) * block_cols
    empty_back = max(len(group) for group in arrivals) * piece
    weight_part = (
        lax.dot_general(own_rows, own_grad, (((0,), (0,)), ((), ())), preferred_element_type=F32)
        * grad_scale
    )
    acc, gate, hold, weight_grad = None, [], {}, None
    weight_steps = summed_everywhere(weight_part, grid, gate)
    weight_grad = next(weight_steps)
    for number, found in enumerate(ring_gather(own_agg_grad, col_devices, grid.along_walk, hold)):
        blocks = [found[k] for k in arrivals[number]]
        if number == len(arrivals) - 1:
            break
        bins = (number * block_cols, block_cols)
        (acc,) = tile_part(True, table_back, bins, bins_back, tiles, blocks, empty_back, acc=acc)
        hold[number + 2] = [acc]
        gate[:] = [found[number]] if number else [acc]
        weight_grad = next(weight_steps, weight_grad)
    gate[:] = blocks
    weight_grad = next(weight_steps, weight_grad)
    bins = ((len(arrivals) - 1) * block_cols, block_cols)
    mine, theirs = tile_part(
        True, table_back, bins, bins_back, tiles, blocks, empty_back, acc=acc, pieces=chips * nodes_here
    )
    got = move(theirs, grid.across(1, 0))
    both = mine.astype(F32) + got.astype(F32)
    sums = [both[k * nodes_here : (k + 1) * nodes_here] for k in range(chips)]
    sums = [sums[0]] + [term.astype(BF16) for term in sums[1:]]
    gate[:] = sums[1:]
    while weight_grad is None:
        weight_grad = next(weight_steps)
    order = scatter_order(chips)
    placed_grad = ring_scatter(
        lambda step, arrived: [sums[k] for k in order[step]], chips, grid.along_x
    ).astype(BF16)
    activations = restore(moves, own_act)
    feature_grad = restore(moves, placed_grad)
    return (activations, weight_grad, feature_grad)


def solution(mesh):
    in_specs = (
        P(("row", "col"), None),
        P(("row", "col")),
        P("row", "col", None, None, None),
        P("row", "col", None),
        P("row", "col"),
        P(),
        P(("row", "col"), None),
    )
    out_specs = (P(("row", "col"), None), P(), P(("row", "col"), None))
    return jax.shard_map(
        per_device, mesh=mesh, in_specs=in_specs, out_specs=out_specs, check_vma=False
    )
```

```python
import functools

import jax
import jax.numpy as jnp
from jax import lax
from jax.experimental import pallas as pl
from jax.experimental.pallas import tpu as pltpu
from jax.sharding import PartitionSpec as P

CORES = 2
GROUP = 4
UNROLL = 8
LANES = 128
PACK_BITS = 8
PACK = 1 << PACK_BITS
VMEM_BYTES = 16 * 1024 * 1024
LOAD_BYTES = 45 * 1024 * 1024
LOADS = 4
F32 = jnp.float32
BF16 = jnp.bfloat16


def elu_value(pre_act):
    return jnp.where(pre_act > 0, pre_act, jnp.expm1(jnp.minimum(pre_act, 0.0)))


def elu_slope(pre_act):
    return jnp.where(pre_act > 0, 1.0, jnp.exp(jnp.minimum(pre_act, 0.0)))


def row_moves(node_order, first_node, nodes_here):
    own = first_node + jnp.arange(nodes_here, dtype=jnp.int32)
    return (node_order[:, None] == own[None, :]).astype(BF16)


def reorder(moves, values):
    return jnp.dot(moves, values, preferred_element_type=F32).astype(BF16)


def restore(moves, values):
    moved = lax.dot_general(moves, values, (((0,), (0,)), ((), ())), preferred_element_type=F32)
    return moved.astype(BF16)


def bits_of(size):
    return size.bit_length() - 1


def block_places(coord, here_ref, chips, cols, piece):
    block_cols = chips * CORES * piece
    row_of, col_of = coord >> bits_of(block_cols), coord & (block_cols - 1)
    row_dev, col_dev = col_of >> bits_of(piece), row_of >> bits_of(piece)
    far = ((row_dev >> bits_of(CORES)) - here_ref[cols]) & (chips - 1)
    swap = ((row_dev & (CORES - 1)) - here_ref[cols + 1]) & (CORES - 1)
    ahead = jnp.zeros_like(coord)
    for c in range(cols):
        ahead = jnp.where(col_dev == c, here_ref[c], ahead)
    return swap * chips + far, col_of & (piece - 1), ahead, row_of & (piece - 1)


def exact_dot(left, right, contract):
    return lax.dot_general(
        left.astype(F32).astype(BF16),
        right.astype(F32).astype(BF16),
        (contract, ((), ())),
        preferred_element_type=F32,
    )


def table_width(slot_total, bin_total):
    group_total = slot_total // GROUP + bin_total + 1
    return -(-max(group_total * GROUP, bin_total + 1) // LANES) * LANES


def write_table(out_ref, bins, bin_total, sources, slots, tile_total, empty):
    lanes = slots.shape[1]
    width = out_ref.shape[1]
    bin_rows = -(-bin_total // 8) * 8
    live = slots < tile_total
    of_bin = lax.broadcasted_iota(jnp.int32, (bin_rows, lanes), 0)
    mine = ((of_bin == bins) & live).astype(jnp.int32)
    earlier = lax.broadcasted_iota(jnp.int32, (lanes, lanes), 0) < lax.broadcasted_iota(
        jnp.int32, (lanes, lanes), 1
    )
    before = exact_dot(mine, earlier.astype(jnp.int32), ((1,), (0,)))
    counts = jnp.sum(mine.astype(F32), axis=1, keepdims=True)
    groups = (counts.astype(jnp.int32) + GROUP - 1) >> bits_of(GROUP)
    bin_at = lax.broadcasted_iota(jnp.int32, (bin_rows, width), 0)
    lane_at = lax.broadcasted_iota(jnp.int32, (bin_rows, width), 1)
    firsts = jnp.sum(jnp.where(bin_at < lane_at, groups, 0).astype(F32), axis=0, keepdims=True)
    here = lax.broadcasted_iota(jnp.int32, (bin_rows, bin_rows), 0)
    other = lax.broadcasted_iota(jnp.int32, (bin_rows, bin_rows), 1)
    firsts_of = exact_dot((other < here).astype(jnp.int32), groups, ((1,), (0,))).astype(jnp.int32)
    group_bin = jnp.sum((firsts_of + groups <= lane_at).astype(F32), axis=0, keepdims=True)
    place = jnp.sum(
        mine.astype(F32) * (before + (firsts_of * GROUP).astype(F32)), axis=0, keepdims=True
    ).astype(jnp.int32)
    place = jnp.where(live, place, -1)
    hit = (lax.broadcasted_iota(jnp.int32, (width, lanes), 0) == place).astype(jnp.int32)
    row = lax.broadcasted_iota(jnp.int32, (8, lanes), 0)
    facts = jnp.where(row == 0, slots, jnp.where(row == 1, sources, 1))
    found = exact_dot(facts, hit, ((1,), (1,))).astype(jnp.int32)
    members = jnp.where(found[2:3] > 0, found[0:1] * PACK + found[1:2], empty)
    rows = lax.broadcasted_iota(jnp.int32, (8, width), 0)
    out_ref[...] = jnp.where(
        rows == 0,
        members,
        jnp.where(rows == 1, group_bin.astype(jnp.int32), firsts.astype(jnp.int32)),
    )


def load_kernel(sizes, here_ref, facts_ref, tiles_ref, out_ref, ahead_ref, back_ref, gate_ref, sems):
    chips, cols, piece = sizes
    slot_total = tiles_ref.shape[0]
    share = slot_total // LOADS
    copies = [
        pltpu.make_async_copy(
            tiles_ref.at[pl.ds(k * share, share)], out_ref.at[pl.ds(k * share, share)], sems.at[k]
        )
        for k in range(LOADS)
    ]
    for copy in copies:
        copy.start()
    gate_ref[...] = jnp.zeros_like(gate_ref)
    coord = facts_ref[0:1, :]
    slots = lax.broadcasted_iota(jnp.int32, coord.shape, 1)
    tile_total = facts_ref[1:2, 0:1]
    row_place, col_piece, ahead, row_piece = block_places(coord, here_ref, chips, cols, piece)
    block_rows, block_cols = cols * piece, chips * CORES * piece

    order = [k for group in scatter_order(cols) for k in group]
    bins = jnp.zeros_like(coord)
    for place, k in enumerate(order):
        bins = jnp.where(ahead == k, place, bins)
    bins = bins * piece + row_piece
    write_table(
        ahead_ref, bins, block_rows, row_place * piece + col_piece, slots, tile_total, block_cols
    )

    arrivals = arrival_order(cols)
    part_of, block_at = jnp.zeros_like(coord), jnp.zeros_like(coord)
    for part, group in enumerate(arrivals):
        for at, k in enumerate(group):
            part_of = jnp.where(ahead == k, part, part_of)
            block_at = jnp.where(ahead == k, at, block_at)
    bins = part_of * block_cols + row_place * piece + col_piece
    write_table(
        back_ref,
        bins,
        len(arrivals) * block_cols,
        block_at * piece + row_piece,
        slots,
        tile_total,
        max(len(group) for group in arrivals) * piece,
    )
    for copy in copies:
        copy.wait()


def load_tiles(tiles, coord, count, here, sizes, gate_shape):
    chips, cols, piece = sizes
    slot_total = tiles.shape[0]
    bins_back = len(arrival_order(cols)) * chips * CORES * piece
    lanes = -(-slot_total // LANES) * LANES
    facts = jnp.concatenate([jnp.pad(row, ((0, 0), (0, lanes - row.shape[1]))) for row in (coord, count)])
    vmem = pl.BlockSpec(memory_space=pltpu.VMEM)
    return pl.pallas_call(
        functools.partial(load_kernel, sizes),
        out_shape=[
            jax.ShapeDtypeStruct(tiles.shape, tiles.dtype),
            jax.ShapeDtypeStruct((8, table_width(slot_total, cols * piece)), jnp.int32),
            jax.ShapeDtypeStruct((8, table_width(slot_total, bins_back)), jnp.int32),
            jax.ShapeDtypeStruct(gate_shape, BF16),
        ],
        in_specs=[pl.BlockSpec(memory_space=pltpu.SMEM), vmem, pl.BlockSpec(memory_space=pl.ANY)],
        out_specs=[vmem] * 4,
        scratch_shapes=[pltpu.SemaphoreType.DMA((LOADS,))],
        compiler_params=pltpu.CompilerParams(vmem_limit_bytes=LOAD_BYTES),
        cost_estimate=pl.CostEstimate(flops=0, bytes_accessed=2 * tiles.size, transcendentals=0),
    )(here, facts, tiles)


def part_kernel(spec, table_ref, tiles_ref, *refs):
    transposed, first_bin, bin_count, bin_total, source_count, carried, finish = spec
    source_refs = refs[:source_count]
    out_refs = refs[source_count + carried : -2]
    source, total = refs[-2:]
    slot_total, tile_size, _ = tiles_ref.shape
    group_total = slot_total // GROUP + bin_total + 1
    at = 0
    for ref in source_refs:
        source[at : at + ref.shape[0], :] = ref[...]
        at += ref.shape[0]
    source[at:, :] = jnp.zeros((source.shape[0] - at, source.shape[1]), source.dtype)
    total[...] = refs[source_count][...] if carried else jnp.zeros_like(total)
    begin = table_ref[2, first_bin]
    end = table_ref[2, first_bin + bin_count]
    contract = 0 if transposed else 1

    def step(number, carry):
        products = []
        for member in range(UNROLL):
            group = begin + number * UNROLL + member
            group = jnp.where(group < end, group, group_total - 1)
            left, right = [], []
            for k in range(GROUP):
                packed = table_ref[0, group * GROUP + k]
                left.append(tiles_ref[packed >> PACK_BITS])
                row = pl.multiple_of((packed & (PACK - 1)) * tile_size, tile_size)
                right.append(source[pl.ds(row, tile_size), :])
            product = lax.dot_general(
                jnp.concatenate(left, axis=contract),
                jnp.concatenate(right, axis=0),
                (((contract,), (0,)), ((), ())),
                preferred_element_type=F32,
            )
            products.append((jnp.minimum(table_ref[1, group] - first_bin, bin_count - 1), product))
        for place, product in products:
            rows = pl.ds(pl.multiple_of(place * tile_size, tile_size), tile_size)
            total[rows, :] += product
        return carry

    lax.fori_loop(0, (end - begin + UNROLL - 1) // UNROLL, step, 0)
    if finish:
        at = 0
        for ref in out_refs:
            ref[...] = total[at : at + ref.shape[0], :].astype(ref.dtype)
            at += ref.shape[0]
    else:
        out_refs[0][...] = total[...]


def tile_part(transposed, table, bins, bin_total, tiles, sources, empty, acc=None, pieces=None):
    first_bin, bin_count = bins
    slot_total, tile_size, _ = tiles.shape
    width = sources[0].shape[1]
    rows = bin_count * tile_size
    vmem = pl.BlockSpec(memory_space=pltpu.VMEM)
    if pieces is None:
        out_shape = [jax.ShapeDtypeStruct((rows, width), F32)]
    else:
        out_shape = [jax.ShapeDtypeStruct((pieces, width), BF16)] * (rows // pieces)
    carried = acc is not None
    share = slot_total * bin_count // bin_total
    given = [table, tiles, *sources] + ([] if acc is None else [acc])
    spec = (transposed, first_bin, bin_count, bin_total, len(sources), carried, pieces is not None)
    return pl.pallas_call(
        functools.partial(part_kernel, spec),
        out_shape=out_shape,
        in_specs=[pl.BlockSpec(memory_space=pltpu.SMEM)] + [vmem] * (len(given) - 1),
        out_specs=[vmem] * len(out_shape),
        scratch_shapes=[
            pltpu.VMEM(((empty + 1) * tile_size, width), BF16),
            pltpu.VMEM((rows, width), F32),
        ],
        compiler_params=pltpu.CompilerParams(vmem_limit_bytes=VMEM_BYTES),
        cost_estimate=pl.CostEstimate(
            flops=2 * share * tile_size * tile_size * width,
            bytes_accessed=2 * share * tile_size * tile_size,
            transcendentals=0,
        ),
    )(*given)


def grid_cycle(size):
    ny = 1
    while (2 * ny) ** 2 <= size:
        ny *= 2
    nz = size // ny
    walk = [0]
    for z in range(nz):
        ys = range(1, ny) if z % 2 == 0 else range(ny - 1, 0, -1)
        walk += [z * ny + y for y in ys]
    walk += [z * ny for z in range(nz - 1, 0, -1)]
    return walk


class Grid:
    def __init__(self, rows, cols):
        self.rows, self.cols, self.chips = rows, cols, rows // CORES
        self.walk = grid_cycle(cols)
        self.place_of = [self.walk.index(c) for c in range(cols)]
        self.row, self.col = lax.axis_index("row"), lax.axis_index("col")
        self.x, self.core = self.row // CORES, self.row % CORES
        place = sum(jnp.where(self.col == c, self.place_of[c], 0) for c in range(cols))
        self.ahead_of = [
            jnp.where(self.core == 0, self.place_of[c] - place, place - self.place_of[c]) % cols
            for c in range(cols)
        ]

    def along_walk(self, step):
        pairs = []
        for r in range(self.rows):
            walk = self.walk if r % CORES == 0 else self.walk[::-1]
            for k in range(self.cols):
                pairs.append((r * self.cols + walk[k], r * self.cols + walk[(k + step) % self.cols]))
        return pairs

    def along_x(self, step):
        return [
            (r * self.cols + c, ((r + step * CORES) % self.rows) * self.cols + c)
            for r in range(self.rows)
            for c in range(self.cols)
        ]

    def across(self, row_bit, col_bit):
        return [
            (r * self.cols + c, (r ^ row_bit) * self.cols + (c ^ col_bit))
            for r in range(self.rows)
            for c in range(self.cols)
        ]


def move(value, pairs):
    return lax.ppermute(value, ("row", "col"), pairs)


def after(value, *others):
    return lax.optimization_barrier((value, *others))[0]


def ring_hops(size):
    return (size - 1) // 2


def arrival_order(size):
    hops = ring_hops(size)
    groups = [[0]] + [[size - step, step] for step in range(1, hops + 1)]
    if size % 2 == 0:
        if hops:
            groups[min(2, hops)].append(size // 2)
        else:
            groups.append([size // 2])
    return groups


def ring_gather(own, size, pairs_of, hold):
    yield {0: own}
    ahead = behind = own
    for step, group in enumerate(arrival_order(size)[1:], 1):
        found = {}
        if step == 1:
            opposite = move(own, pairs_of(size // 2)) if size % 2 == 0 else None
        if step <= ring_hops(size):
            behind = move(after(behind, *hold.get(step, [])), pairs_of(1))
            ahead = move(ahead, pairs_of(-1))
            found = {size - step: behind, step: ahead}
        if size // 2 in group and size % 2 == 0:
            found[size // 2] = opposite
        yield found


def scatter_order(size):
    hops = ring_hops(size)
    groups = [[hop, size - hop] for hop in range(hops, 0, -1)] or [[]]
    if size % 2 == 0:
        groups[0].append(size // 2)
    groups[-1].append(0)
    return groups


def ring_scatter(chunks_of, size, pairs_of):
    ahead = behind = opposite = None

    def onward(running, term):
        return term if running is None else (running.astype(F32) + term.astype(F32)).astype(BF16)

    for step, group in enumerate(scatter_order(size)):
        terms = dict(zip(group, chunks_of(step, ahead)))
        hop = ring_hops(size) - step
        if hop > 0:
            ahead = move(onward(ahead, terms[hop]), pairs_of(1))
            behind = move(onward(behind, terms[size - hop]), pairs_of(-1))
        if size // 2 in group and size % 2 == 0:
            opposite = move(terms[size // 2], pairs_of(size // 2))
    total = terms[0].astype(F32)
    for part in (opposite, ahead, behind):
        if part is not None:
            total = total + part.astype(F32)
    return total


def summed_everywhere(part, grid, gate):
    held = after(part.astype(BF16), *gate)
    got = move(held, grid.across(1, 0))
    yield None
    half = held.shape[0] // CORES
    chip = (held.astype(F32) + after(got, *gate).astype(F32)).astype(BF16)
    held = jnp.where(grid.core == 0, chip[:half], chip[half:])
    bits = [(0, 1 << k) for k in range(bits_of(grid.cols))]
    bits[:2] = bits[1::-1]
    bits += [(1 << k, 0) for k in range(1, bits_of(grid.rows))]
    for row_bit, col_bit in bits:
        got = move(held, grid.across(row_bit, col_bit))
        yield None
        held = (held.astype(F32) + after(got, *gate).astype(F32)).astype(BF16)
    got = move(held, grid.across(1, 0))
    yield None
    own_first, own_last = jnp.concatenate([held, got]), jnp.concatenate([got, held])
    yield jnp.where(grid.core == 0, own_first, own_last).astype(F32)


def per_device(features, node_order, tile_vals, tile_coord, tile_count, weight, cotangent):
    nodes_here, feat_width = features.shape
    tile_size = tile_vals.shape[3]
    row_devices = lax.axis_size("row")
    col_devices = lax.axis_size("col")
    piece = nodes_here // tile_size
    block_cols = row_devices * piece
    block_rows = col_devices * piece
    grad_scale = float(nodes_here * row_devices * col_devices) ** (-0.5)
    grid = Grid(row_devices, col_devices)
    chips = grid.chips

    first_node = (grid.row * col_devices + grid.col) * nodes_here
    moves = row_moves(node_order, first_node, nodes_here)
    placed = reorder(moves, features)
    here = jnp.stack([*grid.ahead_of, grid.x, grid.core]).astype(jnp.int32)
    tiles, table_out, table_back, loaded = load_tiles(
        tile_vals[0, 0], tile_coord[0], tile_count, here, (chips, col_devices, piece), placed.shape
    )

    along_x = {}
    for found in ring_gather(placed, chips, grid.along_x, {}):
        along_x.update(found)
    along_x = [along_x[k] for k in range(chips)]
    other_core = [move(along_x[0], grid.across(1, 0))]
    other_core += [
        move(jnp.where(loaded == 0, block, 0), grid.across(1, 0)) for block in along_x[1:]
    ]
    sources_out = along_x + other_core
    grads_in = reorder(moves, cotangent)
    order = scatter_order(col_devices)
    edges = [sum(len(group) for group in order[:k]) * piece for k in range(len(order) + 1)]

    def chunks_of(step, arrived):
        table = table_out if step < 2 else after(table_out, earlier[step - 1])
        earlier.append(arrived)
        bins = (edges[step], edges[step + 1] - edges[step])
        return tile_part(
            False, table, bins, block_rows, tiles, sources_out, block_cols, pieces=nodes_here
        )

    earlier = []
    own_rows = ring_scatter(chunks_of, col_devices, grid.along_walk).astype(BF16)

    pre_act = jnp.dot(own_rows, weight, preferred_element_type=F32)
    own_act = elu_value(pre_act).astype(BF16)
    own_grad = (grads_in.astype(F32) * elu_slope(pre_act)).astype(BF16)
    own_agg_grad = lax.dot_general(
        own_grad, weight, (((1,), (1,)), ((), ())), preferred_element_type=F32
    ).astype(BF16)
    arrivals = arrival_order(col_devices)
    bins_back = len(arrivals) * block_cols
    empty_back = max(len(group) for group in arrivals) * piece
    weight_part = (
        lax.dot_general(own_rows, own_grad, (((0,), (0,)), ((), ())), preferred_element_type=F32)
        * grad_scale
    )
    acc, gate, hold, weight_grad = None, [], {}, None
    weight_steps = summed_everywhere(weight_part, grid, gate)
    weight_grad = next(weight_steps)
    for number, found in enumerate(ring_gather(own_agg_grad, col_devices, grid.along_walk, hold)):
        blocks = [found[k] for k in arrivals[number]]
        if number == len(arrivals) - 1:
            break
        bins = (number * block_cols, block_cols)
        (acc,) = tile_part(True, table_back, bins, bins_back, tiles, blocks, empty_back, acc=acc)
        hold[number + 2] = [acc]
        gate[:] = [found[number]] if number else [acc]
        weight_grad = next(weight_steps, weight_grad)
    gate[:] = blocks
    weight_grad = next(weight_steps, weight_grad)
    bins = ((len(arrivals) - 1) * block_cols, block_cols)
    mine, theirs = tile_part(
        True, table_back, bins, bins_back, tiles, blocks, empty_back, acc=acc, pieces=chips * nodes_here
    )
    got = move(theirs, grid.across(1, 0))
    both = mine.astype(F32) + got.astype(F32)
    sums = [both[k * nodes_here : (k + 1) * nodes_here] for k in range(chips)]
    sums = [sums[0]] + [term.astype(BF16) for term in sums[1:]]
    gate[:] = sums[1:]
    while weight_grad is None:
        weight_grad = next(weight_steps)
    order = scatter_order(chips)
    placed_grad = ring_scatter(
        lambda step, arrived: [sums[k] for k in order[step]], chips, grid.along_x
    ).astype(BF16)
    activations = restore(moves, own_act)
    feature_grad = restore(moves, placed_grad)
    return (activations, weight_grad, feature_grad)


def solution(mesh):
    in_specs = (
        P(("row", "col"), None),
        P(("row", "col")),
        P("row", "col", None, None, None),
        P("row", "col", None),
        P("row", "col"),
        P(),
        P(("row", "col"), None),
    )
    out_specs = (P(("row", "col"), None), P(), P(("row", "col"), None))
    return jax.shard_map(
        per_device, mesh=mesh, in_specs=in_specs, out_specs=out_specs, check_vma=False
    )
```

```python
import functools

import jax
import jax.numpy as jnp
from jax import lax
from jax.experimental import pallas as pl
from jax.experimental.pallas import tpu as pltpu
from jax.sharding import PartitionSpec as P

CORES = 2
GROUP = 4
UNROLL = 4
LANES = 128
PACK_BITS = 8
PACK = 1 << PACK_BITS
VMEM_BYTES = 16 * 1024 * 1024
LOAD_BYTES = 45 * 1024 * 1024
LOADS = 4
F32 = jnp.float32
BF16 = jnp.bfloat16


def elu_value(pre_act):
    return jnp.where(pre_act > 0, pre_act, jnp.expm1(jnp.minimum(pre_act, 0.0)))


def elu_slope(pre_act):
    return jnp.where(pre_act > 0, 1.0, jnp.exp(jnp.minimum(pre_act, 0.0)))


def row_moves(node_order, first_node, nodes_here):
    own = first_node + jnp.arange(nodes_here, dtype=jnp.int32)
    return (node_order[:, None] == own[None, :]).astype(BF16)


def reorder(moves, values):
    return jnp.dot(moves, values, preferred_element_type=F32).astype(BF16)


def restore(moves, values):
    moved = lax.dot_general(moves, values, (((0,), (0,)), ((), ())), preferred_element_type=F32)
    return moved.astype(BF16)


def bits_of(size):
    return size.bit_length() - 1


def block_places(coord, here_ref, chips, cols, piece):
    block_cols = chips * CORES * piece
    row_of, col_of = coord >> bits_of(block_cols), coord & (block_cols - 1)
    row_dev, col_dev = col_of >> bits_of(piece), row_of >> bits_of(piece)
    far = ((row_dev >> bits_of(CORES)) - here_ref[cols]) & (chips - 1)
    swap = ((row_dev & (CORES - 1)) - here_ref[cols + 1]) & (CORES - 1)
    ahead = jnp.zeros_like(coord)
    for c in range(cols):
        ahead = jnp.where(col_dev == c, here_ref[c], ahead)
    return swap * chips + far, col_of & (piece - 1), ahead, row_of & (piece - 1)


def exact_dot(left, right, contract):
    return lax.dot_general(
        left.astype(F32).astype(BF16),
        right.astype(F32).astype(BF16),
        (contract, ((), ())),
        preferred_element_type=F32,
    )


def table_width(slot_total, bin_total):
    group_total = slot_total // GROUP + bin_total + 1
    return -(-max(group_total * GROUP, bin_total + 1) // LANES) * LANES


def write_table(out_ref, bins, bin_total, sources, slots, tile_total, empty):
    lanes = slots.shape[1]
    width = out_ref.shape[1]
    bin_rows = -(-bin_total // 8) * 8
    live = slots < tile_total
    of_bin = lax.broadcasted_iota(jnp.int32, (bin_rows, lanes), 0)
    mine = ((of_bin == bins) & live).astype(jnp.int32)
    earlier = lax.broadcasted_iota(jnp.int32, (lanes, lanes), 0) < lax.broadcasted_iota(
        jnp.int32, (lanes, lanes), 1
    )
    before = exact_dot(mine, earlier.astype(jnp.int32), ((1,), (0,)))
    counts = jnp.sum(mine.astype(F32), axis=1, keepdims=True)
    groups = (counts.astype(jnp.int32) + GROUP - 1) >> bits_of(GROUP)
    bin_at = lax.broadcasted_iota(jnp.int32, (bin_rows, width), 0)
    lane_at = lax.broadcasted_iota(jnp.int32, (bin_rows, width), 1)
    firsts = jnp.sum(jnp.where(bin_at < lane_at, groups, 0).astype(F32), axis=0, keepdims=True)
    here = lax.broadcasted_iota(jnp.int32, (bin_rows, bin_rows), 0)
    other = lax.broadcasted_iota(jnp.int32, (bin_rows, bin_rows), 1)
    firsts_of = exact_dot((other < here).astype(jnp.int32), groups, ((1,), (0,))).astype(jnp.int32)
    group_bin = jnp.sum((firsts_of + groups <= lane_at).astype(F32), axis=0, keepdims=True)
    place = jnp.sum(
        mine.astype(F32) * (before + (firsts_of * GROUP).astype(F32)), axis=0, keepdims=True
    ).astype(jnp.int32)
    place = jnp.where(live, place, -1)
    hit = (lax.broadcasted_iota(jnp.int32, (width, lanes), 0) == place).astype(jnp.int32)
    row = lax.broadcasted_iota(jnp.int32, (8, lanes), 0)
    facts = jnp.where(row == 0, slots, jnp.where(row == 1, sources, 1))
    found = exact_dot(facts, hit, ((1,), (1,))).astype(jnp.int32)
    members = jnp.where(found[2:3] > 0, found[0:1] * PACK + found[1:2], empty)
    rows = lax.broadcasted_iota(jnp.int32, (8, width), 0)
    out_ref[...] = jnp.where(
        rows == 0,
        members,
        jnp.where(rows == 1, group_bin.astype(jnp.int32), firsts.astype(jnp.int32)),
    )


def load_kernel(sizes, here_ref, facts_ref, tiles_ref, out_ref, ahead_ref, back_ref, gate_ref, sems):
    chips, cols, piece = sizes
    slot_total = tiles_ref.shape[0]
    share = slot_total // LOADS
    copies = [
        pltpu.make_async_copy(
            tiles_ref.at[pl.ds(k * share, share)], out_ref.at[pl.ds(k * share, share)], sems.at[k]
        )
        for k in range(LOADS)
    ]
    for copy in copies:
        copy.start()
    gate_ref[...] = jnp.zeros_like(gate_ref)
    coord = facts_ref[0:1, :]
    slots = lax.broadcasted_iota(jnp.int32, coord.shape, 1)
    tile_total = facts_ref[1:2, 0:1]
    row_place, col_piece, ahead, row_piece = block_places(coord, here_ref, chips, cols, piece)
    block_rows, block_cols = cols * piece, chips * CORES * piece

    order = [k for group in scatter_order(cols) for k in group]
    bins = jnp.zeros_like(coord)
    for place, k in enumerate(order):
        bins = jnp.where(ahead == k, place, bins)
    bins = bins * piece + row_piece
    write_table(
        ahead_ref, bins, block_rows, row_place * piece + col_piece, slots, tile_total, block_cols
    )

    arrivals = arrival_order(cols)
    part_of, block_at = jnp.zeros_like(coord), jnp.zeros_like(coord)
    for part, group in enumerate(arrivals):
        for at, k in enumerate(group):
            part_of = jnp.where(ahead == k, part, part_of)
            block_at = jnp.where(ahead == k, at, block_at)
    bins = part_of * block_cols + row_place * piece + col_piece
    write_table(
        back_ref,
        bins,
        len(arrivals) * block_cols,
        block_at * piece + row_piece,
        slots,
        tile_total,
        max(len(group) for group in arrivals) * piece,
    )
    for copy in copies:
        copy.wait()


def load_tiles(tiles, coord, count, here, sizes, gate_shape):
    chips, cols, piece = sizes
    slot_total = tiles.shape[0]
    bins_back = len(arrival_order(cols)) * chips * CORES * piece
    lanes = -(-slot_total // LANES) * LANES
    facts = jnp.concatenate([jnp.pad(row, ((0, 0), (0, lanes - row.shape[1]))) for row in (coord, count)])
    vmem = pl.BlockSpec(memory_space=pltpu.VMEM)
    return pl.pallas_call(
        functools.partial(load_kernel, sizes),
        out_shape=[
            jax.ShapeDtypeStruct(tiles.shape, tiles.dtype),
            jax.ShapeDtypeStruct((8, table_width(slot_total, cols * piece)), jnp.int32),
            jax.ShapeDtypeStruct((8, table_width(slot_total, bins_back)), jnp.int32),
            jax.ShapeDtypeStruct(gate_shape, BF16),
        ],
        in_specs=[pl.BlockSpec(memory_space=pltpu.SMEM), vmem, pl.BlockSpec(memory_space=pl.ANY)],
        out_specs=[vmem] * 4,
        scratch_shapes=[pltpu.SemaphoreType.DMA((LOADS,))],
        compiler_params=pltpu.CompilerParams(vmem_limit_bytes=LOAD_BYTES),
        cost_estimate=pl.CostEstimate(flops=0, bytes_accessed=2 * tiles.size, transcendentals=0),
    )(here, facts, tiles)


def part_kernel(spec, table_ref, tiles_ref, *refs):
    transposed, first_bin, bin_count, bin_total, source_count, carried, finish = spec
    source_refs = refs[:source_count]
    out_refs = refs[source_count + carried : -2]
    source, total = refs[-2:]
    slot_total, tile_size, _ = tiles_ref.shape
    group_total = slot_total // GROUP + bin_total + 1
    at = 0
    for ref in source_refs:
        source[at : at + ref.shape[0], :] = ref[...]
        at += ref.shape[0]
    source[at:, :] = jnp.zeros((source.shape[0] - at, source.shape[1]), source.dtype)
    total[...] = refs[source_count][...] if carried else jnp.zeros_like(total)
    begin = table_ref[2, first_bin]
    end = table_ref[2, first_bin + bin_count]
    contract = 0 if transposed else 1

    def step(number, carry):
        products = []
        for member in range(UNROLL):
            group = begin + number * UNROLL + member
            group = jnp.where(group < end, group, group_total - 1)
            left, right = [], []
            for k in range(GROUP):
                packed = table_ref[0, group * GROUP + k]
                left.append(tiles_ref[packed >> PACK_BITS])
                row = pl.multiple_of((packed & (PACK - 1)) * tile_size, tile_size)
                right.append(source[pl.ds(row, tile_size), :])
            product = lax.dot_general(
                jnp.concatenate(left, axis=contract),
                jnp.concatenate(right, axis=0),
                (((contract,), (0,)), ((), ())),
                preferred_element_type=F32,
            )
            products.append((jnp.minimum(table_ref[1, group] - first_bin, bin_count - 1), product))
        for place, product in products:
            rows = pl.ds(pl.multiple_of(place * tile_size, tile_size), tile_size)
            total[rows, :] += product
        return carry

    lax.fori_loop(0, (end - begin + UNROLL - 1) // UNROLL, step, 0)
    if finish:
        at = 0
        for ref in out_refs:
            ref[...] = total[at : at + ref.shape[0], :].astype(ref.dtype)
            at += ref.shape[0]
    else:
        out_refs[0][...] = total[...]


def tile_part(transposed, table, bins, bin_total, tiles, sources, empty, acc=None, pieces=None):
    first_bin, bin_count = bins
    slot_total, tile_size, _ = tiles.shape
    width = sources[0].shape[1]
    rows = bin_count * tile_size
    vmem = pl.BlockSpec(memory_space=pltpu.VMEM)
    if pieces is None:
        out_shape = [jax.ShapeDtypeStruct((rows, width), F32)]
    else:
        out_shape = [jax.ShapeDtypeStruct((pieces, width), BF16)] * (rows // pieces)
    carried = acc is not None
    share = slot_total * bin_count // bin_total
    given = [table, tiles, *sources] + ([] if acc is None else [acc])
    spec = (transposed, first_bin, bin_count, bin_total, len(sources), carried, pieces is not None)
    return pl.pallas_call(
        functools.partial(part_kernel, spec),
        out_shape=out_shape,
        in_specs=[pl.BlockSpec(memory_space=pltpu.SMEM)] + [vmem] * (len(given) - 1),
        out_specs=[vmem] * len(out_shape),
        scratch_shapes=[
            pltpu.VMEM(((empty + 1) * tile_size, width), BF16),
            pltpu.VMEM((rows, width), F32),
        ],
        compiler_params=pltpu.CompilerParams(vmem_limit_bytes=VMEM_BYTES),
        cost_estimate=pl.CostEstimate(
            flops=2 * share * tile_size * tile_size * width,
            bytes_accessed=2 * share * tile_size * tile_size,
            transcendentals=0,
        ),
    )(*given)


def grid_cycle(size):
    ny = 1
    while (2 * ny) ** 2 <= size:
        ny *= 2
    nz = size // ny
    walk = [0]
    for z in range(nz):
        ys = range(1, ny) if z % 2 == 0 else range(ny - 1, 0, -1)
        walk += [z * ny + y for y in ys]
    walk += [z * ny for z in range(nz - 1, 0, -1)]
    return walk


class Grid:
    def __init__(self, rows, cols):
        self.rows, self.cols, self.chips = rows, cols, rows // CORES
        self.walk = grid_cycle(cols)
        self.place_of = [self.walk.index(c) for c in range(cols)]
        self.row, self.col = lax.axis_index("row"), lax.axis_index("col")
        self.x, self.core = self.row // CORES, self.row % CORES
        place = sum(jnp.where(self.col == c, self.place_of[c], 0) for c in range(cols))
        self.ahead_of = [
            jnp.where(self.core == 0, self.place_of[c] - place, place - self.place_of[c]) % cols
            for c in range(cols)
        ]

    def along_walk(self, step):
        pairs = []
        for r in range(self.rows):
            walk = self.walk if r % CORES == 0 else self.walk[::-1]
            for k in range(self.cols):
                pairs.append((r * self.cols + walk[k], r * self.cols + walk[(k + step) % self.cols]))
        return pairs

    def along_x(self, step):
        return [
            (r * self.cols + c, ((r + step * CORES) % self.rows) * self.cols + c)
            for r in range(self.rows)
            for c in range(self.cols)
        ]

    def across(self, row_bit, col_bit):
        return [
            (r * self.cols + c, (r ^ row_bit) * self.cols + (c ^ col_bit))
            for r in range(self.rows)
            for c in range(self.cols)
        ]


def move(value, pairs):
    return lax.ppermute(value, ("row", "col"), pairs)


def after(value, *others):
    return lax.optimization_barrier((value, *others))[0]


def ring_hops(size):
    return (size - 1) // 2


def arrival_order(size):
    hops = ring_hops(size)
    groups = [[0]] + [[size - step, step] for step in range(1, hops + 1)]
    if size % 2 == 0:
        if hops:
            groups[min(2, hops)].append(size // 2)
        else:
            groups.append([size // 2])
    return groups


def ring_gather(own, size, pairs_of, hold):
    yield {0: own}
    ahead = behind = own
    for step, group in enumerate(arrival_order(size)[1:], 1):
        found = {}
        if step == 1:
            opposite = move(own, pairs_of(size // 2)) if size % 2 == 0 else None
        if step <= ring_hops(size):
            behind = move(after(behind, *hold.get(step, [])), pairs_of(1))
            ahead = move(ahead, pairs_of(-1))
            found = {size - step: behind, step: ahead}
        if size // 2 in group and size % 2 == 0:
            found[size // 2] = opposite
        yield found


def scatter_order(size):
    hops = ring_hops(size)
    groups = [[hop, size - hop] for hop in range(hops, 0, -1)] or [[]]
    if size % 2 == 0:
        groups[0].append(size // 2)
    groups[-1].append(0)
    return groups


def ring_scatter(chunks_of, size, pairs_of):
    ahead = behind = opposite = None

    def onward(running, term):
        return term if running is None else (running.astype(F32) + term.astype(F32)).astype(BF16)

    for step, group in enumerate(scatter_order(size)):
        terms = dict(zip(group, chunks_of(step, ahead)))
        hop = ring_hops(size) - step
        if hop > 0:
            ahead = move(onward(ahead, terms[hop]), pairs_of(1))
            behind = move(onward(behind, terms[size - hop]), pairs_of(-1))
        if size // 2 in group and size % 2 == 0:
            opposite = move(terms[size // 2], pairs_of(size // 2))
    total = terms[0].astype(F32)
    for part in (opposite, ahead, behind):
        if part is not None:
            total = total + part.astype(F32)
    return total


def summed_everywhere(part, grid, gate):
    held = after(part.astype(BF16), *gate)
    got = move(held, grid.across(1, 0))
    yield None
    half = held.shape[0] // CORES
    chip = (held.astype(F32) + after(got, *gate).astype(F32)).astype(BF16)
    held = jnp.where(grid.core == 0, chip[:half], chip[half:])
    bits = [(0, 1 << k) for k in range(bits_of(grid.cols))]
    bits[:2] = bits[1::-1]
    bits += [(1 << k, 0) for k in range(1, bits_of(grid.rows))]
    for row_bit, col_bit in bits:
        got = move(held, grid.across(row_bit, col_bit))
        yield None
        held = (held.astype(F32) + after(got, *gate).astype(F32)).astype(BF16)
    got = move(held, grid.across(1, 0))
    yield None
    own_first, own_last = jnp.concatenate([held, got]), jnp.concatenate([got, held])
    yield jnp.where(grid.core == 0, own_first, own_last).astype(F32)


def per_device(features, node_order, tile_vals, tile_coord, tile_count, weight, cotangent):
    nodes_here, feat_width = features.shape
    tile_size = tile_vals.shape[3]
    row_devices = lax.axis_size("row")
    col_devices = lax.axis_size("col")
    piece = nodes_here // tile_size
    block_cols = row_devices * piece
    block_rows = col_devices * piece
    grad_scale = float(nodes_here * row_devices * col_devices) ** (-0.5)
    grid = Grid(row_devices, col_devices)
    chips = grid.chips

    first_node = (grid.row * col_devices + grid.col) * nodes_here
    moves = row_moves(node_order, first_node, nodes_here)
    placed = reorder(moves, features)
    here = jnp.stack([*grid.ahead_of, grid.x, grid.core]).astype(jnp.int32)
    tiles, table_out, table_back, loaded = load_tiles(
        tile_vals[0, 0], tile_coord[0], tile_count, here, (chips, col_devices, piece), placed.shape
    )

    along_x = {}
    for found in ring_gather(placed, chips, grid.along_x, {}):
        along_x.update(found)
    along_x = [along_x[k] for k in range(chips)]
    other_core = [move(along_x[0], grid.across(1, 0))]
    other_core += [
        move(jnp.where(loaded == 0, block, 0), grid.across(1, 0)) for block in along_x[1:]
    ]
    sources_out = along_x + other_core
    grads_in = reorder(moves, cotangent)
    order = scatter_order(col_devices)
    edges = [sum(len(group) for group in order[:k]) * piece for k in range(len(order) + 1)]

    def chunks_of(step, arrived):
        table = table_out if step < 2 else after(table_out, earlier[step - 1])
        earlier.append(arrived)
        bins = (edges[step], edges[step + 1] - edges[step])
        return tile_part(
            False, table, bins, block_rows, tiles, sources_out, block_cols, pieces=nodes_here
        )

    earlier = []
    own_rows = ring_scatter(chunks_of, col_devices, grid.along_walk).astype(BF16)

    pre_act = jnp.dot(own_rows, weight, preferred_element_type=F32)
    own_act = elu_value(pre_act).astype(BF16)
    own_grad = (grads_in.astype(F32) * elu_slope(pre_act)).astype(BF16)
    own_agg_grad = lax.dot_general(
        own_grad, weight, (((1,), (1,)), ((), ())), preferred_element_type=F32
    ).astype(BF16)
    arrivals = arrival_order(col_devices)
    bins_back = len(arrivals) * block_cols
    empty_back = max(len(group) for group in arrivals) * piece
    weight_part = (
        lax.dot_general(own_rows, own_grad, (((0,), (0,)), ((), ())), preferred_element_type=F32)
        * grad_scale
    )
    acc, gate, hold, weight_grad = None, [], {}, None
    weight_steps = summed_everywhere(weight_part, grid, gate)
    weight_grad = next(weight_steps)
    for number, found in enumerate(ring_gather(own_agg_grad, col_devices, grid.along_walk, hold)):
        blocks = [found[k] for k in arrivals[number]]
        if number == len(arrivals) - 1:
            break
        bins = (number * block_cols, block_cols)
        (acc,) = tile_part(True, table_back, bins, bins_back, tiles, blocks, empty_back, acc=acc)
        hold[number + 2] = [acc]
        gate[:] = [found[number]] if number else [acc]
        weight_grad = next(weight_steps, weight_grad)
    gate[:] = blocks
    weight_grad = next(weight_steps, weight_grad)
    bins = ((len(arrivals) - 1) * block_cols, block_cols)
    mine, theirs = tile_part(
        True, table_back, bins, bins_back, tiles, blocks, empty_back, acc=acc, pieces=chips * nodes_here
    )
    got = move(theirs, grid.across(1, 0))
    both = mine.astype(F32) + got.astype(F32)
    sums = [both[k * nodes_here : (k + 1) * nodes_here] for k in range(chips)]
    sums = [sums[0]] + [term.astype(BF16) for term in sums[1:]]
    gate[:] = sums[1:]
    while weight_grad is None:
        weight_grad = next(weight_steps)
    order = scatter_order(chips)
    placed_grad = ring_scatter(
        lambda step, arrived: [sums[k] for k in order[step]], chips, grid.along_x
    ).astype(BF16)
    activations = restore(moves, own_act)
    feature_grad = restore(moves, placed_grad)
    return (activations, weight_grad, feature_grad)


def solution(mesh):
    in_specs = (
        P(("row", "col"), None),
        P(("row", "col")),
        P("row", "col", None, None, None),
        P("row", "col", None),
        P("row", "col"),
        P(),
        P(("row", "col"), None),
    )
    out_specs = (P(("row", "col"), None), P(), P(("row", "col"), None))
    return jax.shard_map(
        per_device, mesh=mesh, in_specs=in_specs, out_specs=out_specs, check_vma=False
    )
```

```python
import functools

import jax
import jax.numpy as jnp
from jax import lax
from jax.experimental import pallas as pl
from jax.experimental.pallas import tpu as pltpu
from jax.sharding import PartitionSpec as P

CORES = 2
GROUP = 4
UNROLL = 8
LANES = 128
PACK_BITS = 8
PACK = 1 << PACK_BITS
VMEM_BYTES = 16 * 1024 * 1024
LOAD_BYTES = 45 * 1024 * 1024
LOADS = 2
F32 = jnp.float32
BF16 = jnp.bfloat16


def elu_value(pre_act):
    return jnp.where(pre_act > 0, pre_act, jnp.expm1(jnp.minimum(pre_act, 0.0)))


def elu_slope(pre_act):
    return jnp.where(pre_act > 0, 1.0, jnp.exp(jnp.minimum(pre_act, 0.0)))


def row_moves(node_order, first_node, nodes_here):
    own = first_node + jnp.arange(nodes_here, dtype=jnp.int32)
    return (node_order[:, None] == own[None, :]).astype(BF16)


def reorder(moves, values):
    return jnp.dot(moves, values, preferred_element_type=F32).astype(BF16)


def restore(moves, values):
    moved = lax.dot_general(moves, values, (((0,), (0,)), ((), ())), preferred_element_type=F32)
    return moved.astype(BF16)


def bits_of(size):
    return size.bit_length() - 1


def block_places(coord, here_ref, chips, cols, piece):
    block_cols = chips * CORES * piece
    row_of, col_of = coord >> bits_of(block_cols), coord & (block_cols - 1)
    row_dev, col_dev = col_of >> bits_of(piece), row_of >> bits_of(piece)
    far = ((row_dev >> bits_of(CORES)) - here_ref[cols]) & (chips - 1)
    swap = ((row_dev & (CORES - 1)) - here_ref[cols + 1]) & (CORES - 1)
    ahead = jnp.zeros_like(coord)
    for c in range(cols):
        ahead = jnp.where(col_dev == c, here_ref[c], ahead)
    return swap * chips + far, col_of & (piece - 1), ahead, row_of & (piece - 1)


def exact_dot(left, right, contract):
    return lax.dot_general(
        left.astype(F32).astype(BF16),
        right.astype(F32).astype(BF16),
        (contract, ((), ())),
        preferred_element_type=F32,
    )


def table_width(slot_total, bin_total):
    group_total = slot_total // GROUP + bin_total + 1
    return -(-max(group_total * GROUP, bin_total + 1) // LANES) * LANES


def write_table(out_ref, bins, bin_total, sources, slots, tile_total, empty):
    lanes = slots.shape[1]
    width = out_ref.shape[1]
    bin_rows = -(-bin_total // 8) * 8
    live = slots < tile_total
    of_bin = lax.broadcasted_iota(jnp.int32, (bin_rows, lanes), 0)
    mine = ((of_bin == bins) & live).astype(jnp.int32)
    earlier = lax.broadcasted_iota(jnp.int32, (lanes, lanes), 0) < lax.broadcasted_iota(
        jnp.int32, (lanes, lanes), 1
    )
    before = exact_dot(mine, earlier.astype(jnp.int32), ((1,), (0,)))
    counts = jnp.sum(mine.astype(F32), axis=1, keepdims=True)
    groups = (counts.astype(jnp.int32) + GROUP - 1) >> bits_of(GROUP)
    bin_at = lax.broadcasted_iota(jnp.int32, (bin_rows, width), 0)
    lane_at = lax.broadcasted_iota(jnp.int32, (bin_rows, width), 1)
    firsts = jnp.sum(jnp.where(bin_at < lane_at, groups, 0).astype(F32), axis=0, keepdims=True)
    here = lax.broadcasted_iota(jnp.int32, (bin_rows, bin_rows), 0)
    other = lax.broadcasted_iota(jnp.int32, (bin_rows, bin_rows), 1)
    firsts_of = exact_dot((other < here).astype(jnp.int32), groups, ((1,), (0,))).astype(jnp.int32)
    group_bin = jnp.sum((firsts_of + groups <= lane_at).astype(F32), axis=0, keepdims=True)
    place = jnp.sum(
        mine.astype(F32) * (before + (firsts_of * GROUP).astype(F32)), axis=0, keepdims=True
    ).astype(jnp.int32)
    place = jnp.where(live, place, -1)
    hit = (lax.broadcasted_iota(jnp.int32, (width, lanes), 0) == place).astype(jnp.int32)
    row = lax.broadcasted_iota(jnp.int32, (8, lanes), 0)
    facts = jnp.where(row == 0, slots, jnp.where(row == 1, sources, 1))
    found = exact_dot(facts, hit, ((1,), (1,))).astype(jnp.int32)
    members = jnp.where(found[2:3] > 0, found[0:1] * PACK + found[1:2], empty)
    rows = lax.broadcasted_iota(jnp.int32, (8, width), 0)
    out_ref[...] = jnp.where(
        rows == 0,
        members,
        jnp.where(rows == 1, group_bin.astype(jnp.int32), firsts.astype(jnp.int32)),
    )


def load_kernel(sizes, here_ref, facts_ref, tiles_ref, out_ref, ahead_ref, back_ref, gate_ref, sems):
    chips, cols, piece = sizes
    slot_total = tiles_ref.shape[0]
    share = slot_total // LOADS
    copies = [
        pltpu.make_async_copy(
            tiles_ref.at[pl.ds(k * share, share)], out_ref.at[pl.ds(k * share, share)], sems.at[k]
        )
        for k in range(LOADS)
    ]
    for copy in copies:
        copy.start()
    gate_ref[...] = jnp.zeros_like(gate_ref)
    coord = facts_ref[0:1, :]
    slots = lax.broadcasted_iota(jnp.int32, coord.shape, 1)
    tile_total = facts_ref[1:2, 0:1]
    row_place, col_piece, ahead, row_piece = block_places(coord, here_ref, chips, cols, piece)
    block_rows, block_cols = cols * piece, chips * CORES * piece

    order = [k for group in scatter_order(cols) for k in group]
    bins = jnp.zeros_like(coord)
    for place, k in enumerate(order):
        bins = jnp.where(ahead == k, place, bins)
    bins = bins * piece + row_piece
    write_table(
        ahead_ref, bins, block_rows, row_place * piece + col_piece, slots, tile_total, block_cols
    )

    arrivals = arrival_order(cols)
    part_of, block_at = jnp.zeros_like(coord), jnp.zeros_like(coord)
    for part, group in enumerate(arrivals):
        for at, k in enumerate(group):
            part_of = jnp.where(ahead == k, part, part_of)
            block_at = jnp.where(ahead == k, at, block_at)
    bins = part_of * block_cols + row_place * piece + col_piece
    write_table(
        back_ref,
        bins,
        len(arrivals) * block_cols,
        block_at * piece + row_piece,
        slots,
        tile_total,
        max(len(group) for group in arrivals) * piece,
    )
    for copy in copies:
        copy.wait()


def load_tiles(tiles, coord, count, here, sizes, gate_shape):
    chips, cols, piece = sizes
    slot_total = tiles.shape[0]
    bins_back = len(arrival_order(cols)) * chips * CORES * piece
    lanes = -(-slot_total // LANES) * LANES
    facts = jnp.concatenate([jnp.pad(row, ((0, 0), (0, lanes - row.shape[1]))) for row in (coord, count)])
    vmem = pl.BlockSpec(memory_space=pltpu.VMEM)
    return pl.pallas_call(
        functools.partial(load_kernel, sizes),
        out_shape=[
            jax.ShapeDtypeStruct(tiles.shape, tiles.dtype),
            jax.ShapeDtypeStruct((8, table_width(slot_total, cols * piece)), jnp.int32),
            jax.ShapeDtypeStruct((8, table_width(slot_total, bins_back)), jnp.int32),
            jax.ShapeDtypeStruct(gate_shape, BF16),
        ],
        in_specs=[pl.BlockSpec(memory_space=pltpu.SMEM), vmem, pl.BlockSpec(memory_space=pl.ANY)],
        out_specs=[vmem] * 4,
        scratch_shapes=[pltpu.SemaphoreType.DMA((LOADS,))],
        compiler_params=pltpu.CompilerParams(vmem_limit_bytes=LOAD_BYTES),
        cost_estimate=pl.CostEstimate(flops=0, bytes_accessed=2 * tiles.size, transcendentals=0),
    )(here, facts, tiles)


def part_kernel(spec, table_ref, tiles_ref, *refs):
    transposed, first_bin, bin_count, bin_total, source_count, carried, finish = spec
    source_refs = refs[:source_count]
    out_refs = refs[source_count + carried : -2]
    source, total = refs[-2:]
    slot_total, tile_size, _ = tiles_ref.shape
    group_total = slot_total // GROUP + bin_total + 1
    at = 0
    for ref in source_refs:
        source[at : at + ref.shape[0], :] = ref[...]
        at += ref.shape[0]
    source[at:, :] = jnp.zeros((source.shape[0] - at, source.shape[1]), source.dtype)
    total[...] = refs[source_count][...] if carried else jnp.zeros_like(total)
    begin = table_ref[2, first_bin]
    end = table_ref[2, first_bin + bin_count]
    contract = 0 if transposed else 1

    def step(number, carry):
        products = []
        for member in range(UNROLL):
            group = begin + number * UNROLL + member
            group = jnp.where(group < end, group, group_total - 1)
            left, right = [], []
            for k in range(GROUP):
                packed = table_ref[0, group * GROUP + k]
                left.append(tiles_ref[packed >> PACK_BITS])
                row = pl.multiple_of((packed & (PACK - 1)) * tile_size, tile_size)
                right.append(source[pl.ds(row, tile_size), :])
            product = lax.dot_general(
                jnp.concatenate(left, axis=contract),
                jnp.concatenate(right, axis=0),
                (((contract,), (0,)), ((), ())),
                preferred_element_type=F32,
            )
            products.append((jnp.minimum(table_ref[1, group] - first_bin, bin_count - 1), product))
        for place, product in products:
            rows = pl.ds(pl.multiple_of(place * tile_size, tile_size), tile_size)
            total[rows, :] += product
        return carry

    lax.fori_loop(0, (end - begin + UNROLL - 1) // UNROLL, step, 0)
    if finish:
        at = 0
        for ref in out_refs:
            ref[...] = total[at : at + ref.shape[0], :].astype(ref.dtype)
            at += ref.shape[0]
    else:
        out_refs[0][...] = total[...]


def tile_part(transposed, table, bins, bin_total, tiles, sources, empty, acc=None, pieces=None):
    first_bin, bin_count = bins
    slot_total, tile_size, _ = tiles.shape
    width = sources[0].shape[1]
    rows = bin_count * tile_size
    vmem = pl.BlockSpec(memory_space=pltpu.VMEM)
    if pieces is None:
        out_shape = [jax.ShapeDtypeStruct((rows, width), F32)]
    else:
        out_shape = [jax.ShapeDtypeStruct((pieces, width), BF16)] * (rows // pieces)
    carried = acc is not None
    share = slot_total * bin_count // bin_total
    given = [table, tiles, *sources] + ([] if acc is None else [acc])
    spec = (transposed, first_bin, bin_count, bin_total, len(sources), carried, pieces is not None)
    return pl.pallas_call(
        functools.partial(part_kernel, spec),
        out_shape=out_shape,
        in_specs=[pl.BlockSpec(memory_space=pltpu.SMEM)] + [vmem] * (len(given) - 1),
        out_specs=[vmem] * len(out_shape),
        scratch_shapes=[
            pltpu.VMEM(((empty + 1) * tile_size, width), BF16),
            pltpu.VMEM((rows, width), F32),
        ],
        compiler_params=pltpu.CompilerParams(vmem_limit_bytes=VMEM_BYTES),
        cost_estimate=pl.CostEstimate(
            flops=2 * share * tile_size * tile_size * width,
            bytes_accessed=2 * share * tile_size * tile_size,
            transcendentals=0,
        ),
    )(*given)


def grid_cycle(size):
    ny = 1
    while (2 * ny) ** 2 <= size:
        ny *= 2
    nz = size // ny
    walk = [0]
    for z in range(nz):
        ys = range(1, ny) if z % 2 == 0 else range(ny - 1, 0, -1)
        walk += [z * ny + y for y in ys]
    walk += [z * ny for z in range(nz - 1, 0, -1)]
    return walk


class Grid:
    def __init__(self, rows, cols):
        self.rows, self.cols, self.chips = rows, cols, rows // CORES
        self.walk = grid_cycle(cols)
        self.place_of = [self.walk.index(c) for c in range(cols)]
        self.row, self.col = lax.axis_index("row"), lax.axis_index("col")
        self.x, self.core = self.row // CORES, self.row % CORES
        place = sum(jnp.where(self.col == c, self.place_of[c], 0) for c in range(cols))
        self.ahead_of = [
            jnp.where(self.core == 0, self.place_of[c] - place, place - self.place_of[c]) % cols
            for c in range(cols)
        ]

    def along_walk(self, step):
        pairs = []
        for r in range(self.rows):
            walk = self.walk if r % CORES == 0 else self.walk[::-1]
            for k in range(self.cols):
                pairs.append((r * self.cols + walk[k], r * self.cols + walk[(k + step) % self.cols]))
        return pairs

    def along_x(self, step):
        return [
            (r * self.cols + c, ((r + step * CORES) % self.rows) * self.cols + c)
            for r in range(self.rows)
            for c in range(self.cols)
        ]

    def across(self, row_bit, col_bit):
        return [
            (r * self.cols + c, (r ^ row_bit) * self.cols + (c ^ col_bit))
            for r in range(self.rows)
            for c in range(self.cols)
        ]


def move(value, pairs):
    return lax.ppermute(value, ("row", "col"), pairs)


def after(value, *others):
    return lax.optimization_barrier((value, *others))[0]


def ring_hops(size):
    return (size - 1) // 2


def arrival_order(size):
    hops = ring_hops(size)
    groups = [[0]] + [[size - step, step] for step in range(1, hops + 1)]
    if size % 2 == 0:
        if hops:
            groups[min(2, hops)].append(size // 2)
        else:
            groups.append([size // 2])
    return groups


def ring_gather(own, size, pairs_of, hold):
    yield {0: own}
    ahead = behind = own
    for step, group in enumerate(arrival_order(size)[1:], 1):
        found = {}
        if step == 1:
            opposite = move(own, pairs_of(size // 2)) if size % 2 == 0 else None
        if step <= ring_hops(size):
            behind = move(after(behind, *hold.get(step, [])), pairs_of(1))
            ahead = move(ahead, pairs_of(-1))
            found = {size - step: behind, step: ahead}
        if size // 2 in group and size % 2 == 0:
            found[size // 2] = opposite
        yield found


def scatter_order(size):
    hops = ring_hops(size)
    groups = [[hop, size - hop] for hop in range(hops, 0, -1)] or [[]]
    if size % 2 == 0:
        groups[0].append(size // 2)
    groups[-1].append(0)
    return groups


def ring_scatter(chunks_of, size, pairs_of):
    ahead = behind = opposite = None

    def onward(running, term):
        return term if running is None else (running.astype(F32) + term.astype(F32)).astype(BF16)

    for step, group in enumerate(scatter_order(size)):
        terms = dict(zip(group, chunks_of(step, ahead)))
        hop = ring_hops(size) - step
        if hop > 0:
            ahead = move(onward(ahead, terms[hop]), pairs_of(1))
            behind = move(onward(behind, terms[size - hop]), pairs_of(-1))
        if size // 2 in group and size % 2 == 0:
            opposite = move(terms[size // 2], pairs_of(size // 2))
    total = terms[0].astype(F32)
    for part in (opposite, ahead, behind):
        if part is not None:
            total = total + part.astype(F32)
    return total


def summed_everywhere(part, grid, gate):
    held = after(part.astype(BF16), *gate)
    got = move(held, grid.across(1, 0))
    yield None
    half = held.shape[0] // CORES
    chip = (held.astype(F32) + after(got, *gate).astype(F32)).astype(BF16)
    held = jnp.where(grid.core == 0, chip[:half], chip[half:])
    bits = [(0, 1 << k) for k in range(bits_of(grid.cols))]
    bits[:2] = bits[1::-1]
    bits += [(1 << k, 0) for k in range(1, bits_of(grid.rows))]
    for row_bit, col_bit in bits:
        got = move(held, grid.across(row_bit, col_bit))
        yield None
        held = (held.astype(F32) + after(got, *gate).astype(F32)).astype(BF16)
    got = move(held, grid.across(1, 0))
    yield None
    own_first, own_last = jnp.concatenate([held, got]), jnp.concatenate([got, held])
    yield jnp.where(grid.core == 0, own_first, own_last).astype(F32)


def per_device(features, node_order, tile_vals, tile_coord, tile_count, weight, cotangent):
    nodes_here, feat_width = features.shape
    tile_size = tile_vals.shape[3]
    row_devices = lax.axis_size("row")
    col_devices = lax.axis_size("col")
    piece = nodes_here // tile_size
    block_cols = row_devices * piece
    block_rows = col_devices * piece
    grad_scale = float(nodes_here * row_devices * col_devices) ** (-0.5)
    grid = Grid(row_devices, col_devices)
    chips = grid.chips

    first_node = (grid.row * col_devices + grid.col) * nodes_here
    moves = row_moves(node_order, first_node, nodes_here)
    placed = reorder(moves, features)
    here = jnp.stack([*grid.ahead_of, grid.x, grid.core]).astype(jnp.int32)
    tiles, table_out, table_back, loaded = load_tiles(
        tile_vals[0, 0], tile_coord[0], tile_count, here, (chips, col_devices, piece), placed.shape
    )

    along_x = {}
    for found in ring_gather(placed, chips, grid.along_x, {}):
        along_x.update(found)
    along_x = [along_x[k] for k in range(chips)]
    other_core = [move(along_x[0], grid.across(1, 0))]
    other_core += [
        move(jnp.where(loaded == 0, block, 0), grid.across(1, 0)) for block in along_x[1:]
    ]
    sources_out = along_x + other_core
    grads_in = reorder(moves, cotangent)
    order = scatter_order(col_devices)
    edges = [sum(len(group) for group in order[:k]) * piece for k in range(len(order) + 1)]

    def chunks_of(step, arrived):
        table = table_out if step < 2 else after(table_out, earlier[step - 1])
        earlier.append(arrived)
        bins = (edges[step], edges[step + 1] - edges[step])
        return tile_part(
            False, table, bins, block_rows, tiles, sources_out, block_cols, pieces=nodes_here
        )

    earlier = []
    own_rows = ring_scatter(chunks_of, col_devices, grid.along_walk).astype(BF16)

    pre_act = jnp.dot(own_rows, weight, preferred_element_type=F32)
    own_act = elu_value(pre_act).astype(BF16)
    own_grad = (grads_in.astype(F32) * elu_slope(pre_act)).astype(BF16)
    own_agg_grad = lax.dot_general(
        own_grad, weight, (((1,), (1,)), ((), ())), preferred_element_type=F32
    ).astype(BF16)
    arrivals = arrival_order(col_devices)
    bins_back = len(arrivals) * block_cols
    empty_back = max(len(group) for group in arrivals) * piece
    weight_part = (
        lax.dot_general(own_rows, own_grad, (((0,), (0,)), ((), ())), preferred_element_type=F32)
        * grad_scale
    )
    acc, gate, hold, weight_grad = None, [], {}, None
    weight_steps = summed_everywhere(weight_part, grid, gate)
    weight_grad = next(weight_steps)
    for number, found in enumerate(ring_gather(own_agg_grad, col_devices, grid.along_walk, hold)):
        blocks = [found[k] for k in arrivals[number]]
        if number == len(arrivals) - 1:
            break
        bins = (number * block_cols, block_cols)
        (acc,) = tile_part(True, table_back, bins, bins_back, tiles, blocks, empty_back, acc=acc)
        hold[number + 2] = [acc]
        gate[:] = [found[number]] if number else [acc]
        weight_grad = next(weight_steps, weight_grad)
    gate[:] = blocks
    weight_grad = next(weight_steps, weight_grad)
    bins = ((len(arrivals) - 1) * block_cols, block_cols)
    mine, theirs = tile_part(
        True, table_back, bins, bins_back, tiles, blocks, empty_back, acc=acc, pieces=chips * nodes_here
    )
    got = move(theirs, grid.across(1, 0))
    both = mine.astype(F32) + got.astype(F32)
    sums = [both[k * nodes_here : (k + 1) * nodes_here] for k in range(chips)]
    sums = [sums[0]] + [term.astype(BF16) for term in sums[1:]]
    gate[:] = sums[1:]
    while weight_grad is None:
        weight_grad = next(weight_steps)
    order = scatter_order(chips)
    placed_grad = ring_scatter(
        lambda step, arrived: [sums[k] for k in order[step]], chips, grid.along_x
    ).astype(BF16)
    activations = restore(moves, own_act)
    feature_grad = restore(moves, placed_grad)
    return (activations, weight_grad, feature_grad)


def solution(mesh):
    in_specs = (
        P(("row", "col"), None),
        P(("row", "col")),
        P("row", "col", None, None, None),
        P("row", "col", None),
        P("row", "col"),
        P(),
        P(("row", "col"), None),
    )
    out_specs = (P(("row", "col"), None), P(), P(("row", "col"), None))
    return jax.shard_map(
        per_device, mesh=mesh, in_specs=in_specs, out_specs=out_specs, check_vma=False
    )
```
